128 devices in a mesh: lon: 8 (over x, y_hi), dp: 16 (over z, y_lo, core).
Axes of the slice: x: 4, y: 4 (y_hi: 2, y_lo: 2; y = y_hi * 2 + y_lo), z: 4, core: 2. Of those that a mesh axis runs over, the one named last changes fastest.
Arguments:
- latents: bfloat16 [16, 16, 512, 640], P('dp', None, 'lon'), may hold values from -24 to 24
- target: bfloat16 [16, 16, 512, 640], P('dp', None, 'lon'), may hold values from -14 to 14
- norm_gain: float32 [640], replicated, may hold values from 0.25 to 1.75
- norm_shift: float32 [640], replicated, may hold values from -3 to 3
- conv_weight: bfloat16 [640, 3, 3, 640], P('dp'), may hold values from -0.078125 to 0.078125
- conv_bias: float32 [640], replicated, may hold values from -2 to 2
- timesteps: int32 [16], P('dp'), may hold values from 0 to 999
- buckets: int32 [16], P('dp'), may hold values from 0 to 3
- clip_milli: int32 [4], replicated, may hold values from 1000 to 11999
Outputs:
- bucket_losses: float32 [4], replicated
- input_grad: bfloat16 [16, 16, 512, 640], P('dp', None, 'lon')
- weight_grad: float32 [640, 3, 3, 640], P('dp')
- gain_grad: float32 [640], replicated
- shift_grad: float32 [640], replicated
- bias_grad: float32 [640], replicated
The draws below stay inside these ranges and needn't reach their ends.
All inputs are finite; a program needn't handle non-finite values.
Results may differ from the reference program's by a relative error of at most 0.015.
Values may be sent and summed in bfloat16 or wider, within the bound.
A program may use at most 448 MiB of HBM per device.

```python
import jax
import jax.numpy as jnp
from jax import lax

C = 640
GROUPS = 32
ROWS = 16
COLS = 64
NB = 4
PANS = 16
W = 512


def draw_latents(key, part):
    key = jax.random.fold_in(key, 11)
    first = jax.random.fold_in(key, 0)
    third = jax.random.fold_in(key, 2)
    fourth = jax.random.fold_in(key, 3)
    column = jnp.arange(W, dtype=jnp.float32)
    ramp = (1.0 + 2.0 * column / max(W - 1, 1))[None, None, :, None]
    shape = (PANS, ROWS, W, C)
    blocks = W // COLS
    block_scale = jnp.exp(jax.random.uniform(third, (PANS, 1, blocks, 1), jnp.float32, -0.5, 0.5))
    block_scale = jnp.repeat(block_scale, COLS, axis=2)
    block_offset = jax.random.uniform(fourth, (PANS, 1, blocks, 1), jnp.float32, -1.0, 1.0)
    block_offset = jnp.repeat(block_offset, COLS, axis=2)
    base = jnp.clip(jax.random.normal(first, shape, jnp.float32), -4.0, 4.0)
    values = (base * block_scale + block_offset) * ramp
    return jnp.clip(values, -24.0, 24.0).astype(jnp.bfloat16)


def draw_target(key, part):
    key = jax.random.fold_in(key, 23)
    shape = (PANS, ROWS, W, C)
    index = jnp.arange(PANS, dtype=jnp.float32)
    ramp = (1.0 + 2.0 * index / max(PANS - 1, 1))[:, None, None, None]
    base = jnp.clip(jax.random.normal(key, shape, jnp.float32), -4.0, 4.0)
    return (base * ramp).astype(jnp.bfloat16)


def plant(drawn, rng, least, high):
    longest = drawn.shape.index(max(drawn.shape))
    spots = []
    for shift in (0, 1):
        where = [jax.random.randint(jax.random.fold_in(rng, axis), (), 0, length) for axis, length in enumerate(drawn.shape)]
        where[longest] = (where[longest] + shift) % drawn.shape[longest]
        spots.append(tuple(where))
    return drawn.at[spots[0]].set(least).at[spots[1]].set(high)


def levels(stream_key, shape, pieces, low, largest):
    loudness = 1.0
    for position, parts in pieces:
        draws = jax.random.uniform(jax.random.fold_in(jax.random.fold_in(stream_key, 6), position), (parts,), jnp.float32, low / len(pieces), largest / len(pieces))
        loudness = loudness * jnp.repeat(jnp.exp(draws), shape[position] // parts).reshape((-1,) + (1,) * (len(shape) - 1 - position))
    return loudness


def bell_draw(key, shape, deviation, most, pieces=(), kind=jnp.bfloat16):
    entries = jax.random.normal(key, shape, jnp.float32) * deviation
    if len(pieces) > 0:
        entries = levels(key, shape, pieces, -0.22, 0.18) * entries
    return jnp.clip(entries, min=-most, max=most).astype(kind)


def setup_inputs(seed: int = 0) -> dict:
    key_list = jax.random.split(jax.random.key(seed), 10)
    latents = draw_latents(jax.random.fold_in(key_list[9], 71), 0)
    target = draw_target(jax.random.fold_in(key_list[9], 71), 0)
    norm_gain = jnp.clip(1.0 + 0.15 * jax.random.normal(key_list[2], (C,), jnp.float32), 0.25, 1.75)
    norm_shift = bell_draw(key_list[3], (C,), 0.5, 3.0, (), jnp.float32)
    conv_weight = bell_draw(key_list[4], (C, 3, 3, C), (9 * C) ** -0.5, 0.078125, ((0, 16),))
    conv_bias = bell_draw(key_list[5], (C,), 0.4, 2.0, (), jnp.float32)
    timesteps = plant(jax.random.randint(key_list[6], (PANS,), 0, 1000), jax.random.fold_in(key_list[6], 1), 0, 999).astype(jnp.int32)
    buckets = plant(jax.random.randint(key_list[7], (PANS,), 0, NB), jax.random.fold_in(key_list[7], 1), 0, NB - 1).astype(jnp.int32)
    clip_milli = plant(jax.random.randint(key_list[8], (NB,), 1000, 12000), jax.random.fold_in(key_list[8], 1), 1000, 11999).astype(jnp.int32)
    return dict(latents=latents, target=target, norm_gain=norm_gain, norm_shift=norm_shift, conv_weight=conv_weight, conv_bias=conv_bias, timesteps=timesteps, buckets=buckets, clip_milli=clip_milli)


def circular(field):
    wide = jnp.concatenate([field[:, :, -1:], field, field[:, :, :1]], axis=2)
    return jnp.pad(wide, ((0, 0), (1, 1), (0, 0), (0, 0)))

def group_mean(values, count):
    pans = values.shape[0]
    chans = values.shape[-1]
    per_chan = lax.optimization_barrier(jnp.sum(values, axis=(1, 2)))
    return lax.optimization_barrier(jnp.sum(per_chan.reshape(pans, GROUPS, chans // GROUPS), axis=2)) / count

def spread(stat, chans):
    return jnp.repeat(stat, chans // GROUPS, axis=1)[:, None, None, :]

def reference(latents, target, norm_gain, norm_shift, conv_weight, conv_bias, timesteps, buckets, clip_milli):
    pans, rows, width, chans = latents.shape
    pixels = pans * rows * width
    count = rows * width * (chans // GROUPS)
    field = latents.astype(jnp.float32)
    mean = group_mean(field, count)
    centered = field - spread(mean, chans)
    var = group_mean(centered * centered, count)
    rstd = lax.rsqrt(var + 1e-05)
    normed = centered * spread(rstd, chans)
    pre = normed * norm_gain + norm_shift
    act = jax.nn.silu(pre).astype(jnp.bfloat16)
    act_pad = circular(act)
    total = jnp.zeros((pixels, chans), jnp.float32)
    for kh in range(3):
        for kw in range(3):
            tap = act_pad[:, kh:kh + rows, kw:kw + width, :].reshape(pixels, chans)
            total = total + jnp.dot(tap, conv_weight[:, kh, kw, :], preferred_element_type=jnp.float32)
    branch = total.reshape(pans, rows, width, chans) + conv_bias
    err = field + branch - target.astype(jnp.float32)
    tweight = 1.0 / (1.0 + timesteps.astype(jnp.float32) / 250.0)
    loss = tweight * lax.optimization_barrier(jnp.mean(err * err, axis=(1, 2, 3)))
    member = (buckets[:, None] == jnp.arange(NB, dtype=jnp.int32)[None, :]).astype(jnp.float32)
    counts = lax.optimization_barrier(jnp.sum(member, axis=0))
    denom = jnp.maximum(counts, 1.0)
    bucket_mean = lax.optimization_barrier(jnp.sum(member * loss[:, None], axis=0)) / denom
    limit = clip_milli.astype(jnp.float32) / 1000.0
    bucket_losses = jnp.minimum(bucket_mean, limit)
    passing = (bucket_mean < limit).astype(jnp.float32)
    coef = tweight * lax.optimization_barrier(jnp.sum(member * (passing / denom)[None, :], axis=1))
    grad_out = (coef[:, None, None, None] * err).astype(jnp.bfloat16)
    grad_pad = circular(grad_out)
    flat_grad = grad_out.reshape(pixels, chans)
    dact = jnp.zeros((pixels, chans), jnp.float32)
    wgrad = []
    for kh in range(3):
        for kw in range(3):
            tap = grad_pad[:, kh:kh + rows, kw:kw + width, :].reshape(pixels, chans)
            dact = dact + lax.dot_general(tap, conv_weight[:, 2 - kh, 2 - kw, :], (((1,), (1,)), ((), ())), preferred_element_type=jnp.float32)
            atap = act_pad[:, kh:kh + rows, kw:kw + width, :].reshape(pixels, chans)
            wgrad.append(lax.dot_general(atap, flat_grad, (((0,), (0,)), ((), ())), preferred_element_type=jnp.float32))
    dact = dact.reshape(pans, rows, width, chans)
    sig = jax.nn.sigmoid(pre)
    dpre = dact * sig * (1.0 + pre * (1.0 - sig))
    dnorm = dpre * norm_gain
    first = group_mean(dnorm, count)
    second = group_mean(dnorm * normed, count)
    dfield = spread(rstd, chans) * (dnorm - spread(first, chans) - normed * spread(second, chans))
    input_grad = (grad_out.astype(jnp.float32) + dfield).astype(jnp.bfloat16)
    scale = 1.0 / (ROWS * COLS)
    weight_grad = jnp.stack(wgrad, axis=1).reshape(chans, 3, 3, chans) * scale
    gain_grad = lax.optimization_barrier(jnp.sum(dpre * normed, axis=(0, 1, 2))) * scale
    shift_grad = lax.optimization_barrier(jnp.sum(dpre, axis=(0, 1, 2))) * scale
    bias_grad = lax.optimization_barrier(jnp.sum(grad_out.astype(jnp.float32), axis=(0, 1, 2))) * scale
    return (bucket_losses, input_grad, weight_grad, gain_grad, shift_grad, bias_grad)
```

```python
import functools

import jax
import jax.numpy as jnp
from jax import lax
from jax.experimental import pallas as pl
from jax.experimental.pallas import tpu as pltpu
from jax.sharding import PartitionSpec as P

F32 = jnp.float32
BF16 = jnp.bfloat16
ROWS, COLS, C = 16, 64, 640
PIX = ROWS * COLS
PADPIX = PIX + 2 * COLS
NLON, NDP = 8, 16
COUNT = ROWS * COLS * NLON * (C // 32)
SCALE = 1.0 / (ROWS * COLS)
ORDERS = ("xyz", "yzx", "zxy")
LANES = ((0, 256), (256, 512), (512, 640))
NT = (((1,), (1,)), ((), ()))


class Sems:
    def __init__(self):
        self.used = 0

    def take(self, n=1):
        first = self.used
        self.used += n
        return first


NUM_SEMS = 200


def kernel(
    ts, bk, clip, lat_in, tgt_in, win_in, gain_r, shift_r, bias_r,
    igrad, wout, sg_out,
    lat, tgt, win, dsilu, sibw, wg_all, x3, x3t, acc, dacc, e3, agb,
    mask, stat, hs, hr, es, er, l1, l2, g1, g2, sem, *red,
):
    lon, dp = lax.axis_index("lon"), lax.axis_index("dp")
    x, yhi = lon // 2, lon % 2
    z, ylo, c = dp // 4, (dp // 2) % 2, dp % 2
    y = yhi * 2 + ylo
    here = {"x": x, "y": y, "z": z}
    alloc = Sems()

    def dev(xx, yy, zz, cc):
        return {"lon": xx * 2 + yy // 2, "dp": (zz * 2 + yy % 2) * 2 + cc}

    def along(axis, step):
        at = dict(here)
        at[axis] = (at[axis] + step) % 4
        return dev(at["x"], at["y"], at["z"], c)

    sibling = dev(x, y, z, 1 - c)

    def rcopy(src, dst, send, recv, to):
        return pltpu.make_async_remote_copy(
            src_ref=src, dst_ref=dst, send_sem=sem.at[send], recv_sem=sem.at[recv],
            device_id=to, device_id_type=pl.DeviceIdType.MESH,
        )

    def got(ref, number):
        rcopy(ref, ref, number, number, sibling).wait_recv()

    def sent(ref, number):
        rcopy(ref, ref, number, number, sibling).wait_send()

    def to_lon(i):
        return {"lon": i, "dp": dp}

    def to_dp(i):
        return {"lon": lon, "dp": i}

    loads = [
        pltpu.make_async_copy(src, dst, sem.at[alloc.take()])
        for src, dst in ((win_in, win), (lat_in, lat), (tgt_in, tgt))
    ]
    for one in loads:
        one.start()

    bar = pltpu.get_barrier_semaphore()

    def greet(to):
        pl.semaphore_signal(bar, inc=1, device_id=to, device_id_type=pl.DeviceIdType.MESH)

    @pl.loop(1, NLON)
    def _(k):
        greet(to_lon((lon + k) % NLON))

    @pl.loop(1, NDP)
    def _(k):
        greet(to_dp((dp + k) % NDP))

    far = (y + 3 + 2 * ylo) % 4
    greet(dev(x, far, z, c))

    class Exchange:
        def __init__(self, rx, me, size, to):
            self.rx, self.me, self.size, self.to = rx, me, size, to
            self.base = alloc.take(2)

        def send(self):
            @pl.loop(1, self.size)
            def _(k):
                slot = self.rx.at[self.me]
                rcopy(slot, slot, self.base, self.base + 1, self.to((self.me + k) % self.size)).start()

        def wait(self):
            others = self.rx.at[0 : self.size - 1]
            sent(others, self.base)
            got(others, self.base + 1)

        def total(self):
            return functools.reduce(lambda a, b: a + b, [self.rx[i] for i in range(self.size)])

    def at_row(r):
        return pl.ds(pl.multiple_of(r * COLS, COLS), COLS)

    def sums(r, tot):
        v = lat[r].astype(F32)
        hs[0, pl.ds(r, 1), :] = v[COLS - 1 : COLS]
        hs[1, pl.ds(r, 1), :] = v[0:1]
        return tot + jnp.sum(v, axis=0, keepdims=True)

    loads[1].wait()
    chan = lax.fori_loop(0, ROWS, sums, jnp.zeros((1, C), F32))
    gi = jnp.floor((lax.broadcasted_iota(jnp.int32, (C, C), 0).astype(F32) + 0.5) * 0.05)
    gj = jnp.floor((lax.broadcasted_iota(jnp.int32, (C, C), 1).astype(F32) + 0.5) * 0.05)
    mask[...] = jnp.where(gi == gj, 1.0, 0.0).astype(BF16)

    def group_sum(v):
        top = v.astype(BF16)
        rest = v - top.astype(F32)
        mid = rest.astype(BF16)
        low = (rest - mid.astype(F32)).astype(BF16)
        zeros = jnp.zeros((8, C), F32)
        terms = jnp.concatenate(
            [top.astype(F32), mid.astype(F32), low.astype(F32), zeros], axis=0
        ).astype(BF16)
        out = jnp.dot(terms, mask[...], preferred_element_type=F32)
        return out[0:8] + out[8:16] + out[16:24]

    sub = lax.broadcasted_iota(jnp.int32, (8, C), 0)
    pl.semaphore_wait(bar, NLON - 1 + NDP - 1 + 1)
    loads[0].wait()

    swaps = alloc.take(6)

    def swap_tap(j):
        return rcopy(win.at[2 * j + 1 - c], sibw.at[j], swaps, swaps + 1 + j, sibling)

    for j in range(4):
        swap_tap(j).start()
    pl.when(c == 1)(lambda: swap_tap(4).start())

    right, left = to_lon((lon + 1) % NLON), to_lon((lon + NLON - 1) % NLON)
    hsem = alloc.take(2)
    rcopy(hs.at[0], hr.at[0], hsem, hsem + 1, right).start()
    rcopy(hs.at[1], hr.at[1], hsem, hsem + 1, left).start()

    local_mean = group_sum(jnp.where(sub == 0, chan, 0.0))[0:1] / (PIX * 20)

    odd = x % 2
    own_d = z * 2 + ylo

    def jyz(slot, core):
        return (odd, 2 + (1 - core) * odd, 4 - core)[slot]

    def jx(slot):
        return (1 - odd, 3 - odd)[slot]

    def assemble(j):
        got(sibw.at[j], swaps + 1 + j)
        a = win[2 * j + c].astype(F32)
        b = sibw[j].astype(F32)
        first = jnp.where(c == 0, a, b)
        second = jnp.where(c == 0, b, a)
        rows = pl.ds(pl.multiple_of(own_d * 80, 16), 80)
        wg_all[2 * j + c, rows, :] = jnp.concatenate([first, second], axis=0).astype(BF16)

    LO, HI = (0, 48), (48, 32)

    def blk(j, zz, parity, part=(0, 80)):
        row = pl.multiple_of((zz * 2 + parity) * 80 + part[0], 16)
        return wg_all.at[2 * j + c, pl.ds(row, part[1]), :]

    zl, zr, zo = (z + 3) % 4, (z + 1) % 4, (z + 2) % 4
    gz = [alloc.take(3) for _ in range(3)]
    gy = [alloc.take(5) for _ in range(3)]
    gx = [alloc.take(8) for _ in range(2)]
    gd = [alloc.take(2) for _ in range(5)]

    def rows_of(n):
        return wg_all.at[0, 0:n]

    def two_ways(axis, j, zz, parity, send, recv, slot):
        plus, minus = (LO, HI) if slot % 2 == 0 else (HI, LO)
        one, two = blk(j, zz, parity, plus), blk(j, zz, parity, minus)
        return (
            rcopy(one, one, send, recv, along(axis, 1)),
            rcopy(two, two, send, recv, along(axis, 3)),
        )

    def y_copies(s, k, zz):
        return two_ways("y", jyz(s, c), zz, ylo, gy[s], gy[s] + 1 + k, s)

    def x_copies(s, k, zz, parity):
        return two_ways("x", jyz(s, c), zz, parity, gx[s], gx[s] + k, s)

    def z1(s):
        block = blk(jyz(s, c), z, ylo)
        return [rcopy(block, block, gz[s], gz[s] + 1, along("z", k)) for k in (1, 3)]

    def z2(s):
        j = jyz(s, c)
        plus, minus = (LO, HI) if s % 2 == 0 else (HI, LO)
        one, two = blk(j, zl, ylo, plus), blk(j, zr, ylo, minus)
        return (
            rcopy(one, one, gz[s], gz[s] + 2, along("z", 1)),
            rcopy(two, two, gz[s], gz[s] + 2, along("z", 3)),
        )

    def start(copies):
        for one in copies:
            one.start()

    AROUND = (z, zl, zr, zo)

    def over_x(s, body):
        if s == 0:
            body()
        elif s == 1:
            pl.when(c == 0)(body)

    BLOCKS = ((z, ylo), (zl, ylo), (zr, ylo), (zo, ylo), *((q, 1 - ylo) for q in AROUND))

    def across(n, j, core, k):
        zz, parity = BLOCKS[k]
        row = pl.multiple_of((zz * 2 + parity) * 80, 16)
        block = wg_all.at[2 * j + core, pl.ds(row, 80), :]
        return rcopy(block, block, gd[n], gd[n] + 1, sibling)

    def give(n, j, ks):
        start([across(n, j, c, k) for k in ks])

    def wave1(s):
        assemble(jyz(s, c))
        start(z1(s))
        start(y_copies(s, 0, z))
        give(s, jyz(s, c), (0,))

    def x_send(s, ks):
        def body():
            for k in ks:
                start(x_copies(s, k, *BLOCKS[k]))

        over_x(s, body)

    def wave2(s):
        got(rows_of(160), gz[s] + 1)
        start(z2(s))
        start(y_copies(s, 1, zl))
        start(y_copies(s, 2, zr))
        x_send(s, (1, 2))
        give(s, jyz(s, c), (1, 2))

    def wave3(s):
        got(rows_of(80), gz[s] + 2)
        start(y_copies(s, 3, zo))
        x_send(s, (3,))
        give(s, jyz(s, c), (3,))

    def wave4(s):
        for k in range(4):
            got(rows_of(80), gy[s] + 1 + k)
            x_send(s, (4 + k,))
            give(s, jyz(s, c), (4 + k,))

    def own_x(s):
        def body():
            assemble(jx(s))
            give(3 + s, jx(s), (0,))

        over_x(s, body)

    def wave_x(s, ks):
        def body():
            for k in ks:
                got(rows_of(80), gx[s] + k)
                give(3 + s, jx(s), (k,))

        over_x(s, body)

    def from_sibling(s):
        got(rows_of(C), gd[s] + 1)

    def from_sibling_x(s):
        def body():
            got(rows_of(C), gd[3 + s] + 1)

        if s == 0:
            body()
        else:
            pl.when(c == 1)(body)

    def sends_done():
        pl.when(c == 0)(lambda: sent(sibw.at[0:4], swaps))
        pl.when(c == 1)(lambda: sent(sibw, swaps))
        for s in range(3):
            sent(rows_of(240), gz[s])
            sent(rows_of(320), gy[s])
            sent(rows_of(C), gd[s])
        for s in range(2):

            def body(s=s):
                sent(rows_of(560), gx[s])
                sent(rows_of(C), gd[3 + s])

            over_x(s, body)

    wave1(0)
    wave1(1)
    dacc[...] = jnp.zeros((PIX + 4 * COLS, C), F32)
    own_x(0)
    own_x(1)

    def squares(r, tot):
        d = lat[r].astype(F32) - local_mean
        return tot + jnp.sum(d * d, axis=0, keepdims=True)

    chan2 = lax.fori_loop(0, ROWS, squares, jnp.zeros((1, C), F32))
    m2loc = group_sum(jnp.where(sub == 0, chan2, 0.0))[0:1]
    stat[lon] = jnp.where(sub == 0, local_mean, jnp.where(sub == 1, m2loc, 0.0))
    ex_stat = Exchange(stat, lon, NLON, to_lon)
    ex_stat.send()

    wave2(0)
    wave1(2)
    ex_stat.wait()
    sent(hs, hsem)
    got(hr, hsem + 1)
    stats = [stat[i] for i in range(NLON)]
    mean = functools.reduce(lambda a, b: a + b, [s[0:1] for s in stats]) / NLON
    spread = functools.reduce(lambda a, b: a + b, [(s[0:1] - mean) * (s[0:1] - mean) for s in stats])
    within = functools.reduce(lambda a, b: a + b, [s[1:2] for s in stats])
    var = (within + (PIX * 20) * spread) / COUNT
    rstd = lax.rsqrt(var + 1e-05)
    gain, shift = gain_r[...].reshape(1, C), shift_r[...].reshape(1, C)

    def pre_of(v):
        normed = (v - mean) * rstd
        return normed, normed * gain + shift

    def silu(v):
        _, pre = pre_of(v)
        return pre * jax.nn.sigmoid(pre)

    hr[0] = silu(hr[0])
    hr[1] = silu(hr[1])
    edge = lax.broadcasted_iota(jnp.int32, (COLS, C), 0)

    def put_sides(dst, to, a, halo, r):
        before = jnp.where(edge == 0, halo[0, pl.ds(r, 1), :], pltpu.roll(a, 1, 0))
        after = jnp.where(edge == COLS - 1, halo[1, pl.ds(r, 1), :], pltpu.roll(a, COLS - 1, 0))
        dst[at_row(to), 0:C] = before.astype(BF16)
        dst[at_row(to), 2 * C : 3 * C] = after.astype(BF16)

    zero_row = jnp.zeros((COLS, 3 * C), BF16)
    for buf, ends in ((x3, (0, PADPIX - COLS)), (e3, (0, COLS, PADPIX, PADPIX + COLS))):
        for low in ends:
            buf[low : low + COLS, :] = zero_row

    def activate(first, end):
        @pl.loop(first, end)
        def _(r):
            _normed, pre = pre_of(lat[r].astype(F32))
            sig = jax.nn.sigmoid(pre)
            a = pre * sig
            dsilu[r] = sig * (1.0 + pre * (1.0 - sig))
            x3[at_row(r + 1), C : 2 * C] = a.astype(BF16)
            put_sides(x3, r + 1, a, hr, r)

    unit = jnp.where(
        lax.broadcasted_iota(jnp.int32, (256, 256), 0) == lax.broadcasted_iota(jnp.int32, (256, 256), 1),
        1.0, 0.0,
    ).astype(BF16)

    def turn(first, end):
        for j in range(first, end):
            low, high = j * 256, min(j * 256 + 256, 3 * C)
            n = high - low
            x3t[low:high, :] = lax.dot_general(
                unit[:n, :n], x3[:, low:high], NT, preferred_element_type=F32
            ).astype(BF16)

    def forward(tap, count, fresh=False):
        @pl.loop(0, 2)
        def _(m):
            fields = []
            for n in range(count):
                kh, kw = (tap + n) // 3, (tap + n) % 3
                rows = pl.ds(pl.multiple_of(kh * COLS + m * 512, COLS), 512)
                fields.append(x3[rows, pl.ds(pl.multiple_of(kw * C, 128), C)])
            w = wg_all[pl.ds(tap, count)].reshape(count * C, C)
            part = jnp.dot(jnp.concatenate(fields, axis=1), w, preferred_element_type=F32)
            out = pl.ds(pl.multiple_of(m * 512, 512), 512)
            acc[out, :] = part if fresh else acc[out, :] + part

    activate(0, 8)
    wave2(1)
    wave3(0)
    activate(8, ROWS)
    wave3(1)
    wave4(0)
    wave_x(0, (1, 2))
    turn(0, 3)
    wave2(2)
    wave_x(0, (3,))
    from_sibling(0)
    forward(2 * odd, 2, True)
    wave4(1)
    wave_x(1, (1, 2, 3))
    wave3(2)
    wave_x(0, (4, 5, 6, 7))
    turn(3, 8)
    from_sibling_x(0)
    forward(2 - 2 * odd, 2)
    wave_x(1, (4, 5, 6, 7))
    wave4(2)
    from_sibling(1)
    from_sibling_x(1)
    forward(4, 3)
    from_sibling(2)
    forward(7, 2)
    sends_done()

    loads[2].wait()
    bias = bias_r[...].reshape(1, C)

    def error(r, carry):
        sq, tot = carry
        v = acc[at_row(r), :] + bias + lat[r].astype(F32) - tgt[r].astype(F32)
        e3[at_row(r + 2), C : 2 * C] = v.astype(BF16)
        es[0, pl.ds(r, 1), :] = v[COLS - 1 : COLS]
        es[1, pl.ds(r, 1), :] = v[0:1]
        return sq + jnp.sum(v * v, axis=0, keepdims=True), tot + jnp.sum(v, axis=0, keepdims=True)

    zero = jnp.zeros((1, C), F32)
    sq, err_sum = lax.fori_loop(0, ROWS, error, (zero, zero))
    l1[lon] = jnp.broadcast_to(jnp.sum(sq, axis=1, keepdims=True), (8, 128))
    ex_l1 = Exchange(l1, lon, NLON, to_lon)
    ex_l1.send()
    esem = alloc.take(2)
    rcopy(es.at[0], er.at[0], esem, esem + 1, right).start()
    rcopy(es.at[1], er.at[1], esem, esem + 1, left).start()

    def back(m):
        low = m * (PADPIX // 3)
        w = jnp.concatenate(
            [
                jnp.concatenate([wg_all[3 * kh + kw] for kw in (2, 1, 0)], axis=1)
                for kh in range(3)
            ],
            axis=0,
        )
        part = lax.dot_general(
            e3[COLS + low : COLS + low + PADPIX // 3, :], w, NT, preferred_element_type=F32
        )
        for kh in range(3):
            out = slice(low + kh * COLS, low + kh * COLS + PADPIX // 3)
            dacc[out, :] = dacc[out, :] + part[:, kh * C : (kh + 1) * C]

    NRED = 9
    groups = [red[NRED * g : NRED * g + NRED] for g in range(3)]

    def order(kw, g):
        return ORDERS[(kw + g) % 3]

    def place(kw, g, core, lon_to, d):
        at = {"x": lon_to // 2, "y": (lon_to % 2) * 2 + d % 2, "z": d // 2}
        a1, a2, a3 = order(kw, g)
        return kw, core, at[a1], at[a2], at[a3]

    def weight_part(kw):
        for g in range(3):
            first, end = LANES[g]
            for d in range(8):
                groups[g][0][place(kw, g, 1, 7, d)] = jnp.zeros((16, end - first), BF16)
        err = jnp.concatenate(
            [e3[(2 - kh) * COLS : (2 - kh) * COLS + PADPIX, C : 2 * C] for kh in range(3)], axis=1
        )
        for half in range(2):
            top = kw * C + half * (C // 2)
            res = jnp.dot(x3t[top : top + C // 2, :], err, preferred_element_type=F32)
            res = res.astype(BF16)
            for d in range(4):
                for t in range(5):
                    low = d * 80 + t * 16
                    for kh in range(3):
                        s = kh * 5 + t
                        for g in range(3):
                            first, end = LANES[g]
                            groups[g][0][place(kw, g, s % 2, s // 2, half * 4 + d)] = res[
                                low : low + 16, kh * C + first : kh * C + end
                            ]

    def add(out, terms):
        val = functools.reduce(lambda a, b: a + b, [t[...].astype(F32) for t in terms])
        out[...] = val.astype(out.dtype)

    send_sems = [alloc.take(4) for _ in range(3)]

    def reduce_sends_done():
        for g in range(3):
            rxs, r2rx, r3 = groups[g][1], groups[g][7], groups[g][8]
            sent(rxs, send_sems[g])
            sent(rxs.at[:, 0:3], send_sems[g] + 1)
            sent(r2rx, send_sems[g] + 2)
            sent(r3.at[:, 4:7], send_sems[g] + 3)

    class Lanes:
        def __init__(self, kw, g):
            wg, rxs, ra, rb, rc, rd, r2, r2rx, r3 = groups[g]
            self.r3rx = r3.at[kw, 4:7]
            self.kw, self.g, self.axes = kw, g, order(kw, g)
            self.rxs, self.r2, self.r2rx, self.r3 = rxs.at[kw], r2.at[kw], r2rx.at[kw], r3.at[kw]
            self.ra, self.rb, self.rc, self.rd = ra.at[kw], rb.at[kw], rc.at[kw], rd.at[kw]
            self.buf = wg.at[kw, c]
            send, self.recv = send_sems[g], alloc.take(5)
            self.two = wg.at[kw, 0, 0:2]
            self.swap = rcopy(wg.at[kw, 1 - c], self.rxs, send, self.recv, sibling)
            axis = self.axes[0]
            self.me = [here[a] for a in self.axes]
            far_, up, down = ((self.me[0] + k) % 4 for k in (2, 1, 3))
            self.up, self.down = up, down
            self.first = [
                rcopy(src, dst, send + 1, self.recv + n, along(axis, to))
                for src, dst, n, to in (
                    (self.buf.at[far_, 0:2], self.ra, 1, 1),
                    (self.buf.at[far_, 2:4], self.rb, 1, 3),
                    (self.buf.at[up], self.rc, 2, 1),
                    (self.buf.at[down], self.rd, 2, 3),
                )
            ]
            self.second = self.direct(1, self.r2, self.r2rx, send + 2, self.recv + 3)
            self.third = self.direct(2, self.r3, self.r3rx, send + 3, self.recv + 4)

        def direct(self, stage, buf, rx, send, recv):
            return [
                rcopy(
                    buf.at[(self.me[stage] + k) % 4], rx.at[k - 1],
                    send, recv, along(self.axes[stage], k),
                )
                for k in (1, 3, 2)
            ]

        def join(self, mine_by, theirs_by):
            got(self.rxs, self.recv)

            @pl.loop(0, 4)
            def _(i):
                own = self.buf[i].astype(F32) * mine_by
                self.buf[i] = (own + self.rxs[i].astype(F32) * theirs_by).astype(BF16)

            start(self.first[:2])

        def middle(self):
            got(self.rc, self.recv + 1)
            add(self.buf.at[self.up, 0:2], [self.buf.at[self.up, 0:2], self.ra])
            add(self.buf.at[self.down, 2:4], [self.buf.at[self.down, 2:4], self.rb])
            start(self.first[2:])

        def end_first(self):
            got(self.two, self.recv + 2)
            add(self.r2, [self.buf.at[self.me[0]], self.rc, self.rd])
            start(self.second)

        def end_second(self):
            got(self.r2rx, self.recv + 3)
            add(self.r3.at[0:4], [self.r2.at[self.me[1]]] + [self.r2rx.at[k] for k in range(3)])
            start(self.third)

        def end_third(self):
            got(self.r3rx, self.recv + 4)
            val = self.r3[self.me[2]].astype(F32)
            for k in range(3):
                val = val + self.r3[4 + k].astype(F32)
            first, end = LANES[self.g]
            agb[self.kw, c, lon, :, first:end] = val.astype(BF16)

    class Reduce:
        def __init__(self, kw):
            self.kw = kw
            self.lanes = [Lanes(kw, g) for g in range(3)]
            slot = agb.at[kw, c, lon]
            self.sems = alloc.take(5)
            send, recv = self.sems, self.sems + 1
            self.over_y = rcopy(slot, slot, send, recv, dev(x, (y + 2) % 4, z, c))
            pair = agb.at[kw, c, pl.ds(2 * x, 2)]
            self.over_x = [rcopy(pair, pair, send, recv + 1, along("x", k)) for k in (1, 3, 2)]
            self.give = rcopy(agb.at[kw, c], agb.at[kw, c], send + 3, recv + 3, sibling)

        def join(self, mine_by, theirs_by):
            for one in self.lanes:
                one.join(mine_by, theirs_by)

        def step(self, n):
            kw = self.kw
            if n == 0:
                for one in self.lanes:
                    one.swap.start()
            elif n == 2:
                for one in self.lanes:
                    one.middle()
            elif n == 3:
                for one in self.lanes:
                    one.end_first()
            elif n == 4:
                for one in self.lanes:
                    one.end_second()
            elif n == 5:
                for one in self.lanes:
                    one.end_third()
                self.over_y.start()
            elif n == 6:
                got(agb.at[kw, c, 0], self.sems + 1)
                start(self.over_x)
            elif n == 7:
                got(agb.at[kw, c, 0:6], self.sems + 2)
                self.give.start()
            elif n == 8:
                got(agb.at[kw, 1 - c], self.sems + 4)
                sent(agb.at[kw, c, 0:7], self.sems)
                sent(agb.at[kw, c], self.sems + 3)
                for row in range(3):
                    tiles = []
                    for t in range(5):
                        s = row * 5 + t
                        tiles.append(agb[kw, s % 2, s // 2].astype(F32))
                    rows = jnp.concatenate(tiles, axis=0)
                    wout[3 * row + kw] = jnp.where(c == 0, rows[0:40], rows[40:80]) * SCALE

    parts = [Reduce(kw) for kw in range(3)]
    weight_part(0)
    parts[0].step(0)

    ex_l1.wait()
    tweight = 1.0 / (1.0 + jnp.full((8, 128), ts[0], jnp.int32).astype(F32) / 250.0)
    pano = tweight * ex_l1.total() / (ROWS * COLS * NLON * C)
    lane = lax.broadcasted_iota(jnp.int32, (8, 128), 1)
    row8 = lax.broadcasted_iota(jnp.int32, (8, 128), 0)
    member = jnp.where(lane == jnp.full((8, 128), bk[0], jnp.int32), 1.0, 0.0).astype(F32)
    l2[dp] = jnp.where(
        row8 == 0, member * pano, jnp.where(row8 == 1, member, jnp.where(row8 == 2, tweight, 0.0))
    )
    ex_l2 = Exchange(l2, dp, NDP, to_dp)
    ex_l2.send()
    weight_part(1)
    parts[1].step(0)
    ex_l2.wait()
    sums2 = ex_l2.total()
    denom = jnp.maximum(sums2[1:2], 1.0)
    bucket_mean = sums2[0:1] / denom
    lane1 = lane[0:1]
    limit = jnp.zeros((1, 128), jnp.int32)
    for b in range(4):
        limit = jnp.where(lane1 == b, jnp.full((1, 128), clip[b], jnp.int32), limit)
    limit = limit.astype(F32) / 1000.0
    losses = jnp.minimum(bucket_mean, limit)
    passing = jnp.where((bucket_mean < limit) & (lane1 < 4), 1.0, 0.0)

    def coef_of(tile):
        picked = jnp.sum(tile[1:2] * passing / denom, axis=1, keepdims=True)
        return tile[2:3, 0:1] * picked

    coef, sib_coef = coef_of(l2[dp]), coef_of(l2[dp + 1 - 2 * c])

    parts[0].join(coef, sib_coef)
    weight_part(2)
    parts[2].step(0)
    parts[1].join(coef, sib_coef)
    parts[0].step(2)

    sent(es, esem)
    got(er, esem + 1)

    @pl.loop(0, ROWS)
    def _(r):
        put_sides(e3, r + 2, e3[at_row(r + 2), C : 2 * C].astype(F32), er, r)

    parts[1].step(2)
    parts[2].join(coef, sib_coef)
    parts[0].step(3)
    back(0)
    parts[2].step(2)
    parts[1].step(3)
    parts[0].step(4)
    back(1)
    parts[2].step(3)
    parts[1].step(4)
    parts[0].step(5)
    back(2)
    parts[2].step(4)
    parts[1].step(5)
    parts[0].step(6)

    def through(r, carry):
        a, b = carry
        normed = (lat[r].astype(F32) - mean) * rstd
        dpre = dacc[at_row(r + 2), :] * coef * dsilu[r]
        dacc[at_row(r + 2), :] = dpre
        return (
            a + jnp.sum(dpre, axis=0, keepdims=True),
            b + jnp.sum(dpre * normed, axis=0, keepdims=True),
        )

    s1, s2 = lax.fori_loop(0, ROWS, through, (zero, zero))
    g1[lon] = jnp.where(
        sub == 0, s1, jnp.where(sub == 1, s2, jnp.where(sub == 2, err_sum * coef, 0.0))
    )
    ex_g1 = Exchange(g1, lon, NLON, to_lon)
    ex_g1.send()
    parts[2].step(5)
    parts[1].step(6)
    parts[0].step(7)
    ex_g1.wait()
    pan = ex_g1.total()
    g2[dp] = pan
    ex_g2 = Exchange(g2, dp, NDP, to_dp)
    ex_g2.send()
    means = group_sum(pan * gain) / COUNT
    m1, m2 = means[0:1], means[1:2]

    @pl.loop(0, ROWS)
    def _(r):
        normed = (lat[r].astype(F32) - mean) * rstd
        dn = dacc[at_row(r + 2), :] * gain
        g = e3[at_row(r + 2), C : 2 * C].astype(F32) * coef
        igrad[r] = (g + rstd * (dn - m1 - normed * m2)).astype(BF16)

    parts[2].step(6)
    parts[1].step(7)
    parts[0].step(8)
    ex_g2.wait()
    totals = ex_g2.total() * SCALE
    wide = jnp.concatenate([losses] + [jnp.zeros_like(losses)] * 4, axis=1)
    sg_out[...] = jnp.where(sub == 3, wide, totals)
    parts[2].step(7)
    parts[1].step(8)
    parts[2].step(8)
    reduce_sends_done()
    assert alloc.used <= NUM_SEMS, alloc.used


def reduce_shapes(lanes):
    tile = (16, lanes)
    return [
        (3, 2, 4, 4, 4, *tile),
        (3, 4, 4, 4, *tile),
        (3, 2, 4, *tile),
        (3, 2, 4, *tile),
        (3, 4, 4, *tile),
        (3, 4, 4, *tile),
        (3, 4, 4, *tile),
        (3, 3, 4, *tile),
        (3, 7, *tile),
    ]


def shards(
    latents, target, norm_gain, norm_shift, conv_weight, conv_bias, timesteps, buckets, clip_milli
):
    win = jnp.transpose(conv_weight, (1, 2, 0, 3)).reshape(9, 40, C)
    vmem = pl.BlockSpec(memory_space=pltpu.VMEM)
    smem = pl.BlockSpec(memory_space=pltpu.SMEM)
    outs = pl.pallas_call(
        kernel,
        out_shape=(
            pltpu.VMEM((ROWS, COLS, C), BF16),
            pltpu.VMEM((9, 40, C), F32),
            pltpu.VMEM((8, C), F32),
        ),
        in_specs=[smem] * 3 + [pl.BlockSpec(memory_space=pl.ANY)] * 3 + [vmem] * 3,
        out_specs=(vmem,) * 3,
        scratch_shapes=[
            pltpu.VMEM((ROWS, COLS, C), BF16),
            pltpu.VMEM((ROWS, COLS, C), BF16),
            pltpu.VMEM((9, 40, C), BF16),
            pltpu.VMEM((ROWS, COLS, C), F32),
            pltpu.VMEM((5, 40, C), BF16),
            pltpu.VMEM((9, C, C), BF16),
            pltpu.VMEM((PADPIX, 3 * C), BF16),
            pltpu.VMEM((3 * C, PADPIX), BF16),
            pltpu.VMEM((PIX, C), F32),
            pltpu.VMEM((PIX + 4 * COLS, C), F32),
            pltpu.VMEM((PADPIX + 2 * COLS, 3 * C), BF16),
            pltpu.VMEM((3, 2, NLON, 16, C), BF16),
            pltpu.VMEM((C, C), BF16),
            pltpu.VMEM((NLON, 8, C), F32),
            pltpu.VMEM((2, ROWS, C), F32),
            pltpu.VMEM((2, ROWS, C), F32),
            pltpu.VMEM((2, ROWS, C), F32),
            pltpu.VMEM((2, ROWS, C), F32),
            pltpu.VMEM((NLON, 8, 128), F32),
            pltpu.VMEM((NDP, 8, 128), F32),
            pltpu.VMEM((NLON, 8, C), F32),
            pltpu.VMEM((NDP, 8, C), F32),
            pltpu.SemaphoreType.DMA((NUM_SEMS,)),
        ]
        + [pltpu.VMEM(shape, BF16) for first, end in LANES for shape in reduce_shapes(end - first)],
        compiler_params=pltpu.CompilerParams(
            collective_id=0, has_side_effects=True, vmem_limit_bytes=60 * 1024 * 1024
        ),
        cost_estimate=pl.CostEstimate(
            flops=3 * 2 * PIX * 9 * C * C, bytes_accessed=8 * 1024 * 1024, transcendentals=2 * PIX * C
        ),
    )(
        timesteps, buckets, clip_milli, latents[0], target[0], win,
        norm_gain, norm_shift, conv_bias,
    )
    igrad, wout, sg = outs
    weight_grad = jnp.transpose(wout.reshape(3, 3, 40, C), (2, 0, 1, 3))
    return sg[3, :4], igrad[None], weight_grad, sg[1], sg[0], sg[2]


def solution(mesh):
    placed = (
        P("dp", None, "lon", None),
        P("dp", None, "lon", None),
        P(),
        P(),
        P("dp", None, None, None),
        P(),
        P("dp"),
        P("dp"),
        P(),
    )
    return jax.shard_map(
        shards,
        mesh=mesh,
        in_specs=placed,
        out_specs=(P(), P("dp", None, "lon", None), P("dp", None, None, None), P(), P(), P()),
        check_vma=False,
    )
```

```python
import functools

import jax
import jax.numpy as jnp
from jax import lax
from jax.experimental import pallas as pl
from jax.experimental.pallas import tpu as pltpu
from jax.sharding import PartitionSpec as P

F32 = jnp.float32
BF16 = jnp.bfloat16
ROWS, COLS, C = 16, 64, 640
PIX = ROWS * COLS
PADPIX = PIX + 2 * COLS
NLON, NDP = 8, 16
COUNT = ROWS * COLS * NLON * (C // 32)
SCALE = 1.0 / (ROWS * COLS)
ORDERS = ("xyz", "yzx", "zxy")
LANES = ((0, 256), (256, 512), (512, 640))
NT = (((1,), (1,)), ((), ()))


class Sems:
    def __init__(self):
        self.used = 0

    def take(self, n=1):
        first = self.used
        self.used += n
        return first


NUM_SEMS = 200


def kernel(
    ts, bk, clip, lat_in, tgt_in, win_in, gain_r, shift_r, bias_r,
    igrad, wout, sg_out,
    lat, tgt, win, dsilu, sibw, wg_all, x3, x3t, acc, dacc, e3, agb,
    mask, stat, hs, hr, es, er, l1, l2, g1, g2, sem, *red,
):
    lon, dp = lax.axis_index("lon"), lax.axis_index("dp")
    x, yhi = lon // 2, lon % 2
    z, ylo, c = dp // 4, (dp // 2) % 2, dp % 2
    y = yhi * 2 + ylo
    here = {"x": x, "y": y, "z": z}
    alloc = Sems()

    def dev(xx, yy, zz, cc):
        return {"lon": xx * 2 + yy // 2, "dp": (zz * 2 + yy % 2) * 2 + cc}

    def along(axis, step):
        at = dict(here)
        at[axis] = (at[axis] + step) % 4
        return dev(at["x"], at["y"], at["z"], c)

    sibling = dev(x, y, z, 1 - c)

    def rcopy(src, dst, send, recv, to):
        return pltpu.make_async_remote_copy(
            src_ref=src, dst_ref=dst, send_sem=sem.at[send], recv_sem=sem.at[recv],
            device_id=to, device_id_type=pl.DeviceIdType.MESH,
        )

    def got(ref, number):
        rcopy(ref, ref, number, number, sibling).wait_recv()

    def sent(ref, number):
        rcopy(ref, ref, number, number, sibling).wait_send()

    def to_lon(i):
        return {"lon": i, "dp": dp}

    def to_dp(i):
        return {"lon": lon, "dp": i}

    loads = [
        pltpu.make_async_copy(src, dst, sem.at[alloc.take()])
        for src, dst in ((win_in, win), (lat_in, lat), (tgt_in, tgt))
    ]
    for one in loads:
        one.start()

    bar = pltpu.get_barrier_semaphore()

    def greet(to):
        pl.semaphore_signal(bar, inc=1, device_id=to, device_id_type=pl.DeviceIdType.MESH)

    @pl.loop(1, NLON)
    def _(k):
        greet(to_lon((lon + k) % NLON))

    @pl.loop(1, NDP)
    def _(k):
        greet(to_dp((dp + k) % NDP))

    far = (y + 3 + 2 * ylo) % 4
    greet(dev(x, far, z, c))

    class Exchange:
        def __init__(self, rx, me, size, to):
            self.rx, self.me, self.size, self.to = rx, me, size, to
            self.base = alloc.take(2)

        def send(self):
            @pl.loop(1, self.size)
            def _(k):
                slot = self.rx.at[self.me]
                rcopy(slot, slot, self.base, self.base + 1, self.to((self.me + k) % self.size)).start()

        def wait(self):
            others = self.rx.at[0 : self.size - 1]
            sent(others, self.base)
            got(others, self.base + 1)

        def total(self):
            return functools.reduce(lambda a, b: a + b, [self.rx[i] for i in range(self.size)])

    def at_row(r):
        return pl.ds(pl.multiple_of(r * COLS, COLS), COLS)

    def sums(r, tot):
        v = lat[r].astype(F32)
        hs[0, pl.ds(r, 1), :] = v[COLS - 1 : COLS]
        hs[1, pl.ds(r, 1), :] = v[0:1]
        return tot + jnp.sum(v, axis=0, keepdims=True)

    loads[1].wait()
    chan = lax.fori_loop(0, ROWS, sums, jnp.zeros((1, C), F32))
    gi = jnp.floor((lax.broadcasted_iota(jnp.int32, (C, C), 0).astype(F32) + 0.5) * 0.05)
    gj = jnp.floor((lax.broadcasted_iota(jnp.int32, (C, C), 1).astype(F32) + 0.5) * 0.05)
    mask[...] = jnp.where(gi == gj, 1.0, 0.0).astype(BF16)

    def group_sum(v):
        top = v.astype(BF16)
        rest = v - top.astype(F32)
        mid = rest.astype(BF16)
        low = (rest - mid.astype(F32)).astype(BF16)
        zeros = jnp.zeros((8, C), F32)
        terms = jnp.concatenate(
            [top.astype(F32), mid.astype(F32), low.astype(F32), zeros], axis=0
        ).astype(BF16)
        out = jnp.dot(terms, mask[...], preferred_element_type=F32)
        return out[0:8] + out[8:16] + out[16:24]

    sub = lax.broadcasted_iota(jnp.int32, (8, C), 0)
    pl.semaphore_wait(bar, NLON - 1 + NDP - 1 + 1)
    loads[0].wait()

    swaps = alloc.take(6)

    def swap_tap(j):
        return rcopy(win.at[2 * j + 1 - c], sibw.at[j], swaps, swaps + 1 + j, sibling)

    for j in range(4):
        swap_tap(j).start()
    pl.when(c == 1)(lambda: swap_tap(4).start())

    right, left = to_lon((lon + 1) % NLON), to_lon((lon + NLON - 1) % NLON)
    hsem = alloc.take(2)
    rcopy(hs.at[0], hr.at[0], hsem, hsem + 1, right).start()
    rcopy(hs.at[1], hr.at[1], hsem, hsem + 1, left).start()

    local_mean = group_sum(jnp.where(sub == 0, chan, 0.0))[0:1] / (PIX * 20)

    odd = x % 2
    own_d = z * 2 + ylo

    def jyz(slot, core):
        return (odd, 2 + (1 - core) * odd, 4 - core)[slot]

    def jx(slot):
        return (1 - odd, 3 - odd)[slot]

    def assemble(j):
        got(sibw.at[j], swaps + 1 + j)
        a = win[2 * j + c].astype(F32)
        b = sibw[j].astype(F32)
        first = jnp.where(c == 0, a, b)
        second = jnp.where(c == 0, b, a)
        rows = pl.ds(pl.multiple_of(own_d * 80, 16), 80)
        wg_all[2 * j + c, rows, :] = jnp.concatenate([first, second], axis=0).astype(BF16)

    def blk(j, zz, parity):
        row = pl.multiple_of((zz * 2 + parity) * 80, 16)
        return wg_all.at[2 * j + c, pl.ds(row, 80), :]

    zl, zr, zo = (z + 3) % 4, (z + 1) % 4, (z + 2) % 4
    gz = [alloc.take(3) for _ in range(3)]
    gy = [alloc.take(5) for _ in range(3)]
    gx = [alloc.take(8) for _ in range(2)]
    gd = [alloc.take(2) for _ in range(5)]

    def rows_of(n):
        return wg_all.at[0, 0:n]

    def one_way(axis, block, send, recv, up):
        return rcopy(block, block, send, recv, along(axis, 1 if up else 3))

    def y_copy(s, k, zz):
        block = blk(jyz(s, c), zz, ylo)
        return one_way("y", block, gy[s], gy[s] + 1 + k, (k in (0, 3)) == (s != 1))

    def x_copy(s, k, zz, parity):
        block = blk(jyz(s, c), zz, parity)
        return one_way("x", block, gx[s], gx[s] + k, (k % 2 == 0) == (s == 0))

    def z1(s):
        block = blk(jyz(s, c), z, ylo)
        return [one_way("z", block, gz[s], gz[s] + 1, up) for up in (True, False)]

    def z2(s):
        return one_way("z", blk(jyz(s, c), zr if s == 1 else zl, ylo), gz[s], gz[s] + 2, s != 1)

    def start(copies):
        for one in copies:
            one.start()

    AROUND = (z, zl, zr, zo)

    def over_x(s, body):
        if s == 0:
            body()
        elif s == 1:
            pl.when(c == 0)(body)

    BLOCKS = ((z, ylo), (zl, ylo), (zr, ylo), (zo, ylo), *((q, 1 - ylo) for q in AROUND))

    def across(n, j, core, k):
        zz, parity = BLOCKS[k]
        row = pl.multiple_of((zz * 2 + parity) * 80, 16)
        block = wg_all.at[2 * j + core, pl.ds(row, 80), :]
        return rcopy(block, block, gd[n], gd[n] + 1, sibling)

    def give(n, j, ks):
        if n in (0, 1, 3):
            if ks[-1] == 7:
                tap = wg_all.at[2 * j + c]
                rcopy(tap, tap, gd[n], gd[n] + 1, sibling).start()
        else:
            start([across(n, j, c, k) for k in ks])

    def wave1(s):
        assemble(jyz(s, c))
        start(z1(s))
        y_copy(s, 0, z).start()
        give(s, jyz(s, c), (0,))

    def x_send(s, ks):
        def body():
            for k in ks:
                x_copy(s, k, *BLOCKS[k]).start()

        over_x(s, body)

    def wave2(s):
        got(rows_of(160), gz[s] + 1)
        z2(s).start()
        y_copy(s, 1, zl).start()
        y_copy(s, 2, zr).start()
        x_send(s, (1, 2))
        give(s, jyz(s, c), (1, 2))

    def wave3(s):
        got(rows_of(80), gz[s] + 2)
        y_copy(s, 3, zo).start()
        x_send(s, (3,))
        give(s, jyz(s, c), (3,))

    def wave4(s):
        for k in range(4):
            got(rows_of(80), gy[s] + 1 + k)
            x_send(s, (4 + k,))
            give(s, jyz(s, c), (4 + k,))

    def own_x(s):
        def body():
            assemble(jx(s))
            give(3 + s, jx(s), (0,))

        over_x(s, body)

    def wave_x(s, ks):
        def body():
            for k in ks:
                got(rows_of(80), gx[s] + k)
                give(3 + s, jx(s), (k,))

        over_x(s, body)

    def from_sibling(s):
        got(rows_of(C), gd[s] + 1)

    def from_sibling_x(s):
        def body():
            got(rows_of(C), gd[3 + s] + 1)

        if s == 0:
            body()
        else:
            pl.when(c == 1)(body)

    def sends_done():
        pl.when(c == 0)(lambda: sent(sibw.at[0:4], swaps))
        pl.when(c == 1)(lambda: sent(sibw, swaps))
        for s in range(3):
            sent(rows_of(240), gz[s])
            sent(rows_of(320), gy[s])
            sent(rows_of(C), gd[s])
        for s in range(2):

            def body(s=s):
                sent(rows_of(560), gx[s])
                sent(rows_of(C), gd[3 + s])

            over_x(s, body)

    wave1(0)
    wave1(1)
    dacc[...] = jnp.zeros((PIX + 4 * COLS, C), F32)
    own_x(0)
    own_x(1)

    def squares(r, tot):
        d = lat[r].astype(F32) - local_mean
        return tot + jnp.sum(d * d, axis=0, keepdims=True)

    chan2 = lax.fori_loop(0, ROWS, squares, jnp.zeros((1, C), F32))
    m2loc = group_sum(jnp.where(sub == 0, chan2, 0.0))[0:1]
    stat[lon] = jnp.where(sub == 0, local_mean, jnp.where(sub == 1, m2loc, 0.0))
    ex_stat = Exchange(stat, lon, NLON, to_lon)
    ex_stat.send()

    wave2(0)
    wave1(2)
    ex_stat.wait()
    sent(hs, hsem)
    got(hr, hsem + 1)
    stats = [stat[i] for i in range(NLON)]
    mean = functools.reduce(lambda a, b: a + b, [s[0:1] for s in stats]) / NLON
    spread = functools.reduce(lambda a, b: a + b, [(s[0:1] - mean) * (s[0:1] - mean) for s in stats])
    within = functools.reduce(lambda a, b: a + b, [s[1:2] for s in stats])
    var = (within + (PIX * 20) * spread) / COUNT
    rstd = lax.rsqrt(var + 1e-05)
    gain, shift = gain_r[...].reshape(1, C), shift_r[...].reshape(1, C)

    def pre_of(v):
        normed = (v - mean) * rstd
        return normed, normed * gain + shift

    def silu(v):
        _, pre = pre_of(v)
        return pre * jax.nn.sigmoid(pre)

    hr[0] = silu(hr[0])
    hr[1] = silu(hr[1])
    edge = lax.broadcasted_iota(jnp.int32, (COLS, C), 0)

    def put_sides(dst, to, a, halo, r):
        before = jnp.where(edge == 0, halo[0, pl.ds(r, 1), :], pltpu.roll(a, 1, 0))
        after = jnp.where(edge == COLS - 1, halo[1, pl.ds(r, 1), :], pltpu.roll(a, COLS - 1, 0))
        dst[at_row(to), 0:C] = before.astype(BF16)
        dst[at_row(to), 2 * C : 3 * C] = after.astype(BF16)

    zero_row = jnp.zeros((COLS, 3 * C), BF16)
    for buf, ends in ((x3, (0, PADPIX - COLS)), (e3, (0, COLS, PADPIX, PADPIX + COLS))):
        for low in ends:
            buf[low : low + COLS, :] = zero_row

    def activate(first, end):
        @pl.loop(first, end)
        def _(r):
            _normed, pre = pre_of(lat[r].astype(F32))
            sig = jax.nn.sigmoid(pre)
            a = pre * sig
            dsilu[r] = sig * (1.0 + pre * (1.0 - sig))
            x3[at_row(r + 1), C : 2 * C] = a.astype(BF16)
            put_sides(x3, r + 1, a, hr, r)

    unit = jnp.where(
        lax.broadcasted_iota(jnp.int32, (256, 256), 0) == lax.broadcasted_iota(jnp.int32, (256, 256), 1),
        1.0, 0.0,
    ).astype(BF16)

    def turn(first, end):
        for j in range(first, end):
            low, high = j * 256, min(j * 256 + 256, 3 * C)
            n = high - low
            x3t[low:high, :] = lax.dot_general(
                unit[:n, :n], x3[:, low:high], NT, preferred_element_type=F32
            ).astype(BF16)

    def forward(tap, count, fresh=False):
        @pl.loop(0, 2)
        def _(m):
            fields = []
            for n in range(count):
                kh, kw = (tap + n) // 3, (tap + n) % 3
                rows = pl.ds(pl.multiple_of(kh * COLS + m * 512, COLS), 512)
                fields.append(x3[rows, pl.ds(pl.multiple_of(kw * C, 128), C)])
            w = wg_all[pl.ds(tap, count)].reshape(count * C, C)
            part = jnp.dot(jnp.concatenate(fields, axis=1), w, preferred_element_type=F32)
            out = pl.ds(pl.multiple_of(m * 512, 512), 512)
            acc[out, :] = part if fresh else acc[out, :] + part

    activate(0, 8)
    wave2(1)
    wave3(0)
    activate(8, ROWS)
    wave3(1)
    wave4(0)
    wave_x(0, (1, 2))
    turn(0, 3)
    wave2(2)
    wave_x(0, (3,))
    from_sibling(0)
    forward(2 * odd, 2, True)
    wave4(1)
    wave_x(1, (1, 2, 3))
    wave3(2)
    wave_x(0, (4, 5, 6, 7))
    turn(3, 8)
    from_sibling_x(0)
    forward(2 - 2 * odd, 2)
    wave_x(1, (4, 5, 6, 7))
    wave4(2)
    from_sibling(1)
    from_sibling_x(1)
    forward(4, 3)
    from_sibling(2)
    forward(7, 2)
    sends_done()

    loads[2].wait()
    bias = bias_r[...].reshape(1, C)

    def error(r, carry):
        sq, tot = carry
        v = acc[at_row(r), :] + bias + lat[r].astype(F32) - tgt[r].astype(F32)
        e3[at_row(r + 2), C : 2 * C] = v.astype(BF16)
        es[0, pl.ds(r, 1), :] = v[COLS - 1 : COLS]
        es[1, pl.ds(r, 1), :] = v[0:1]
        return sq + jnp.sum(v * v, axis=0, keepdims=True), tot + jnp.sum(v, axis=0, keepdims=True)

    zero = jnp.zeros((1, C), F32)
    sq, err_sum = lax.fori_loop(0, ROWS, error, (zero, zero))
    l1[lon] = jnp.broadcast_to(jnp.sum(sq, axis=1, keepdims=True), (8, 128))
    ex_l1 = Exchange(l1, lon, NLON, to_lon)
    ex_l1.send()
    esem = alloc.take(2)
    rcopy(es.at[0], er.at[0], esem, esem + 1, right).start()
    rcopy(es.at[1], er.at[1], esem, esem + 1, left).start()

    def back(m):
        low = m * (PADPIX // 3)
        w = jnp.concatenate(
            [
                jnp.concatenate([wg_all[3 * kh + kw] for kw in (2, 1, 0)], axis=1)
                for kh in range(3)
            ],
            axis=0,
        )
        part = lax.dot_general(
            e3[COLS + low : COLS + low + PADPIX // 3, :], w, NT, preferred_element_type=F32
        )
        for kh in range(3):
            out = slice(low + kh * COLS, low + kh * COLS + PADPIX // 3)
            dacc[out, :] = dacc[out, :] + part[:, kh * C : (kh + 1) * C]

    NRED = 9
    groups = [red[NRED * g : NRED * g + NRED] for g in range(3)]

    def order(kw, g):
        return ORDERS[(kw + g) % 3]

    def place(kw, g, core, lon_to, d, z_from=0):
        at = {"x": lon_to // 2, "y": (lon_to % 2) * 2 + d % 2, "z": z_from + d // 2}
        a1, a2, a3 = order(kw, g)
        return kw, core, at[a1], at[a2], at[a3]

    def weight_part(kw):
        for g in range(3):
            first, end = LANES[g]
            for d in range(8):
                groups[g][0][place(kw, g, 1, 7, d)] = jnp.zeros((16, end - first), BF16)
        @pl.loop(0, 2)
        def _(half):
            err = jnp.concatenate(
                [e3[(2 - kh) * COLS : (2 - kh) * COLS + PADPIX, C : 2 * C] for kh in range(3)], axis=1
            )
            top = pl.ds(pl.multiple_of(kw * C + half * (C // 2), C // 2), C // 2)
            res = jnp.dot(x3t[top, :], err, preferred_element_type=F32)
            res = res.astype(BF16)
            for d in range(4):
                for t in range(5):
                    low = d * 80 + t * 16
                    for kh in range(3):
                        s = kh * 5 + t
                        for g in range(3):
                            first, end = LANES[g]
                            groups[g][0][place(kw, g, s % 2, s // 2, d, 2 * half)] = res[
                                low : low + 16, kh * C + first : kh * C + end
                            ]

    def add(out, terms):
        val = functools.reduce(lambda a, b: a + b, [t[...].astype(F32) for t in terms])
        out[...] = val.astype(out.dtype)

    send_sems = [alloc.take(4) for _ in range(3)]

    def reduce_sends_done():
        for g in range(3):
            rxs, r2rx, r3 = groups[g][1], groups[g][7], groups[g][8]
            sent(rxs, send_sems[g])
            sent(rxs.at[:, 0:3], send_sems[g] + 1)
            sent(r2rx, send_sems[g] + 2)
            sent(r3.at[:, 4:7], send_sems[g] + 3)

    class Lanes:
        def __init__(self, kw, g):
            wg, rxs, ra, rb, rc, rd, r2, r2rx, r3 = groups[g]
            self.r3rx = r3.at[kw, 4:7]
            self.kw, self.g, self.axes = kw, g, order(kw, g)
            self.rxs, self.r2, self.r2rx, self.r3 = rxs.at[kw], r2.at[kw], r2rx.at[kw], r3.at[kw]
            self.ra, self.rb, self.rc, self.rd = ra.at[kw], rb.at[kw], rc.at[kw], rd.at[kw]
            self.buf = wg.at[kw, c]
            send, self.recv = send_sems[g], alloc.take(5)
            self.two = wg.at[kw, 0, 0:2]
            self.swap = rcopy(wg.at[kw, 1 - c], self.rxs, send, self.recv, sibling)
            axis = self.axes[0]
            self.me = [here[a] for a in self.axes]
            far_, up, down = ((self.me[0] + k) % 4 for k in (2, 1, 3))
            self.up, self.down = up, down
            self.first = [
                rcopy(src, dst, send + 1, self.recv + n, along(axis, to))
                for src, dst, n, to in (
                    (self.buf.at[far_, 0:2], self.ra, 1, 1),
                    (self.buf.at[far_, 2:4], self.rb, 1, 3),
                    (self.buf.at[up], self.rc, 2, 1),
                    (self.buf.at[down], self.rd, 2, 3),
                )
            ]
            self.second = self.direct(1, self.r2, self.r2rx, send + 2, self.recv + 3)
            self.third = self.direct(2, self.r3, self.r3rx, send + 3, self.recv + 4)

        def direct(self, stage, buf, rx, send, recv):
            return [
                rcopy(
                    buf.at[(self.me[stage] + k) % 4], rx.at[k - 1],
                    send, recv, along(self.axes[stage], k),
                )
                for k in (1, 3, 2)
            ]

        def join(self, mine_by, theirs_by):
            got(self.rxs, self.recv)

            @pl.loop(0, 4)
            def _(i):
                own = self.buf[i].astype(F32) * mine_by
                self.buf[i] = (own + self.rxs[i].astype(F32) * theirs_by).astype(BF16)

            start(self.first[:2])

        def middle(self):
            got(self.rc, self.recv + 1)
            add(self.buf.at[self.up, 0:2], [self.buf.at[self.up, 0:2], self.ra])
            add(self.buf.at[self.down, 2:4], [self.buf.at[self.down, 2:4], self.rb])
            start(self.first[2:])

        def end_first(self):
            got(self.two, self.recv + 2)
            add(self.r2, [self.buf.at[self.me[0]], self.rc, self.rd])
            start(self.second)

        def end_second(self):
            got(self.r2rx, self.recv + 3)
            add(self.r3.at[0:4], [self.r2.at[self.me[1]]] + [self.r2rx.at[k] for k in range(3)])
            start(self.third)

        def end_third(self):
            got(self.r3rx, self.recv + 4)
            val = self.r3[self.me[2]].astype(F32)
            for k in range(3):
                val = val + self.r3[4 + k].astype(F32)
            first, end = LANES[self.g]
            agb[self.kw, c, lon, :, first:end] = val.astype(BF16)

    class Reduce:
        def __init__(self, kw):
            self.kw = kw
            self.lanes = [Lanes(kw, g) for g in range(3)]
            slot = agb.at[kw, c, lon]
            self.sems = alloc.take(5)
            send, recv = self.sems, self.sems + 1
            self.over_y = rcopy(slot, slot, send, recv, dev(x, (y + 2) % 4, z, c))
            pair = agb.at[kw, c, pl.ds(2 * x, 2)]
            self.over_x = [rcopy(pair, pair, send, recv + 1, along("x", k)) for k in (1, 3, 2)]
            self.give = rcopy(agb.at[kw, c], agb.at[kw, c], send + 3, recv + 3, sibling)

        def join(self, mine_by, theirs_by):
            for one in self.lanes:
                one.join(mine_by, theirs_by)

        def step(self, n):
            kw = self.kw
            if n == 0:
                for one in self.lanes:
                    one.swap.start()
            elif n == 2:
                for one in self.lanes:
                    one.middle()
            elif n == 3:
                for one in self.lanes:
                    one.end_first()
            elif n == 4:
                for one in self.lanes:
                    one.end_second()
            elif n == 5:
                for one in self.lanes:
                    one.end_third()
                self.over_y.start()
            elif n == 6:
                got(agb.at[kw, c, 0], self.sems + 1)
                start(self.over_x)
            elif n == 7:
                got(agb.at[kw, c, 0:6], self.sems + 2)
                self.give.start()
            elif n == 8:
                got(agb.at[kw, 1 - c], self.sems + 4)
                sent(agb.at[kw, c, 0:7], self.sems)
                sent(agb.at[kw, c], self.sems + 3)
                for row in range(3):
                    tiles = []
                    for t in range(5):
                        s = row * 5 + t
                        tiles.append(agb[kw, s % 2, s // 2].astype(F32))
                    rows = jnp.concatenate(tiles, axis=0)
                    wout[3 * row + kw] = jnp.where(c == 0, rows[0:40], rows[40:80]) * SCALE

    parts = [Reduce(kw) for kw in range(3)]
    weight_part(0)
    parts[0].step(0)

    ex_l1.wait()
    tweight = 1.0 / (1.0 + jnp.full((8, 128), ts[0], jnp.int32).astype(F32) / 250.0)
    pano = tweight * ex_l1.total() / (ROWS * COLS * NLON * C)
    lane = lax.broadcasted_iota(jnp.int32, (8, 128), 1)
    row8 = lax.broadcasted_iota(jnp.int32, (8, 128), 0)
    member = jnp.where(lane == jnp.full((8, 128), bk[0], jnp.int32), 1.0, 0.0).astype(F32)
    l2[dp] = jnp.where(
        row8 == 0, member * pano, jnp.where(row8 == 1, member, jnp.where(row8 == 2, tweight, 0.0))
    )
    ex_l2 = Exchange(l2, dp, NDP, to_dp)
    ex_l2.send()
    weight_part(1)
    parts[1].step(0)
    ex_l2.wait()
    sums2 = ex_l2.total()
    denom = jnp.maximum(sums2[1:2], 1.0)
    bucket_mean = sums2[0:1] / denom
    lane1 = lane[0:1]
    limit = jnp.zeros((1, 128), jnp.int32)
    for b in range(4):
        limit = jnp.where(lane1 == b, jnp.full((1, 128), clip[b], jnp.int32), limit)
    limit = limit.astype(F32) / 1000.0
    losses = jnp.minimum(bucket_mean, limit)
    passing = jnp.where((bucket_mean < limit) & (lane1 < 4), 1.0, 0.0)

    def coef_of(tile):
        picked = jnp.sum(tile[1:2] * passing / denom, axis=1, keepdims=True)
        return tile[2:3, 0:1] * picked

    coef, sib_coef = coef_of(l2[dp]), coef_of(l2[dp + 1 - 2 * c])

    parts[0].join(coef, sib_coef)
    weight_part(2)
    parts[2].step(0)
    parts[1].join(coef, sib_coef)
    parts[0].step(2)

    sent(es, esem)
    got(er, esem + 1)

    @pl.loop(0, ROWS)
    def _(r):
        put_sides(e3, r + 2, e3[at_row(r + 2), C : 2 * C].astype(F32), er, r)

    parts[1].step(2)
    parts[2].join(coef, sib_coef)
    parts[0].step(3)
    back(0)
    parts[2].step(2)
    parts[1].step(3)
    parts[0].step(4)
    back(1)
    parts[2].step(3)
    parts[1].step(4)
    parts[0].step(5)
    back(2)
    parts[2].step(4)
    parts[1].step(5)
    parts[0].step(6)

    def through(r, carry):
        a, b = carry
        normed = (lat[r].astype(F32) - mean) * rstd
        dpre = dacc[at_row(r + 2), :] * coef * dsilu[r]
        dacc[at_row(r + 2), :] = dpre
        return (
            a + jnp.sum(dpre, axis=0, keepdims=True),
            b + jnp.sum(dpre * normed, axis=0, keepdims=True),
        )

    s1, s2 = lax.fori_loop(0, ROWS, through, (zero, zero))
    g1[lon] = jnp.where(
        sub == 0, s1, jnp.where(sub == 1, s2, jnp.where(sub == 2, err_sum * coef, 0.0))
    )
    ex_g1 = Exchange(g1, lon, NLON, to_lon)
    ex_g1.send()
    parts[2].step(5)
    parts[1].step(6)
    parts[0].step(7)
    ex_g1.wait()
    pan = ex_g1.total()
    g2[z] = pan
    ex_z = Exchange(g2.at[0:4], z, 4, lambda i: dev(x, y, i, c))
    ex_z.send()
    means = group_sum(pan * gain) / COUNT
    m1, m2 = means[0:1], means[1:2]

    @pl.loop(0, ROWS)
    def _(r):
        normed = (lat[r].astype(F32) - mean) * rstd
        dn = dacc[at_row(r + 2), :] * gain
        g = e3[at_row(r + 2), C : 2 * C].astype(F32) * coef
        igrad[r] = (g + rstd * (dn - m1 - normed * m2)).astype(BF16)

    parts[2].step(6)
    ex_z.wait()
    g2[4 + dp % 4] = ex_z.total()
    ex_g2 = Exchange(g2.at[4:8], dp % 4, 4, lambda i: to_dp(z * 4 + i))
    ex_g2.send()
    parts[1].step(7)
    parts[0].step(8)
    ex_g2.wait()
    totals = ex_g2.total() * SCALE
    wide = jnp.concatenate([losses] + [jnp.zeros_like(losses)] * 4, axis=1)
    sg_out[...] = jnp.where(sub == 3, wide, totals)
    parts[2].step(7)
    parts[1].step(8)
    parts[2].step(8)
    reduce_sends_done()
    assert alloc.used <= NUM_SEMS, alloc.used


def reduce_shapes(lanes):
    tile = (16, lanes)
    return [
        (3, 2, 4, 4, 4, *tile),
        (3, 4, 4, 4, *tile),
        (3, 2, 4, *tile),
        (3, 2, 4, *tile),
        (3, 4, 4, *tile),
        (3, 4, 4, *tile),
        (3, 4, 4, *tile),
        (3, 3, 4, *tile),
        (3, 7, *tile),
    ]


def shards(
    latents, target, norm_gain, norm_shift, conv_weight, conv_bias, timesteps, buckets, clip_milli
):
    win = jnp.transpose(conv_weight, (1, 2, 0, 3)).reshape(9, 40, C)
    vmem = pl.BlockSpec(memory_space=pltpu.VMEM)
    smem = pl.BlockSpec(memory_space=pltpu.SMEM)
    outs = pl.pallas_call(
        kernel,
        out_shape=(
            pltpu.VMEM((ROWS, COLS, C), BF16),
            pltpu.VMEM((9, 40, C), F32),
            pltpu.VMEM((8, C), F32),
        ),
        in_specs=[smem] * 3 + [pl.BlockSpec(memory_space=pl.ANY)] * 3 + [vmem] * 3,
        out_specs=(vmem,) * 3,
        scratch_shapes=[
            pltpu.VMEM((ROWS, COLS, C), BF16),
            pltpu.VMEM((ROWS, COLS, C), BF16),
            pltpu.VMEM((9, 40, C), BF16),
            pltpu.VMEM((ROWS, COLS, C), F32),
            pltpu.VMEM((5, 40, C), BF16),
            pltpu.VMEM((9, C, C), BF16),
            pltpu.VMEM((PADPIX, 3 * C), BF16),
            pltpu.VMEM((3 * C, PADPIX), BF16),
            pltpu.VMEM((PIX, C), F32),
            pltpu.VMEM((PIX + 4 * COLS, C), F32),
            pltpu.VMEM((PADPIX + 2 * COLS, 3 * C), BF16),
            pltpu.VMEM((3, 2, NLON, 16, C), BF16),
            pltpu.VMEM((C, C), BF16),
            pltpu.VMEM((NLON, 8, C), F32),
            pltpu.VMEM((2, ROWS, C), F32),
            pltpu.VMEM((2, ROWS, C), F32),
            pltpu.VMEM((2, ROWS, C), F32),
            pltpu.VMEM((2, ROWS, C), F32),
            pltpu.VMEM((NLON, 8, 128), F32),
            pltpu.VMEM((NDP, 8, 128), F32),
            pltpu.VMEM((NLON, 8, C), F32),
            pltpu.VMEM((8, 8, C), F32),
            pltpu.SemaphoreType.DMA((NUM_SEMS,)),
        ]
        + [pltpu.VMEM(shape, BF16) for first, end in LANES for shape in reduce_shapes(end - first)],
        compiler_params=pltpu.CompilerParams(
            collective_id=0, has_side_effects=True, vmem_limit_bytes=60 * 1024 * 1024
        ),
        cost_estimate=pl.CostEstimate(
            flops=3 * 2 * PIX * 9 * C * C, bytes_accessed=8 * 1024 * 1024, transcendentals=2 * PIX * C
        ),
    )(
        timesteps, buckets, clip_milli, latents[0], target[0], win,
        norm_gain, norm_shift, conv_bias,
    )
    igrad, wout, sg = outs
    weight_grad = jnp.transpose(wout.reshape(3, 3, 40, C), (2, 0, 1, 3))
    return sg[3, :4], igrad[None], weight_grad, sg[1], sg[0], sg[2]


def solution(mesh):
    placed = (
        P("dp", None, "lon", None),
        P("dp", None, "lon", None),
        P(),
        P(),
        P("dp", None, None, None),
        P(),
        P("dp"),
        P("dp"),
        P(),
    )
    return jax.shard_map(
        shards,
        mesh=mesh,
        in_specs=placed,
        out_specs=(P(), P("dp", None, "lon", None), P("dp", None, None, None), P(), P(), P()),
        check_vma=False,
    )
```

```python
import functools

import jax
import jax.numpy as jnp
from jax import lax
from jax.experimental import pallas as pl
from jax.experimental.pallas import tpu as pltpu
from jax.sharding import PartitionSpec as P

F32 = jnp.float32
BF16 = jnp.bfloat16
ROWS, COLS, C = 16, 64, 640
PIX = ROWS * COLS
PADPIX = PIX + 2 * COLS
NLON, NDP = 8, 16
COUNT = ROWS * COLS * NLON * (C // 32)
SCALE = 1.0 / (ROWS * COLS)
ORDERS = ("xyz", "yzx", "zxy")
LANES = ((0, 256), (256, 512), (512, 640))
NT = (((1,), (1,)), ((), ()))


class Sems:
    def __init__(self):
        self.used = 0

    def take(self, n=1):
        first = self.used
        self.used += n
        return first


NUM_SEMS = 200


def kernel(
    ts, bk, clip, lat_in, tgt_in, win_in, gain_r, shift_r, bias_r,
    igrad, wout, sg_out,
    lat, tgt, win, dsilu, sibw, wg_all, x3, x3t, acc, dacc, e3, agb,
    mask, stat, hs, hr, es, er, l1, l2, g1, g2, sem, *red,
):
    lon, dp = lax.axis_index("lon"), lax.axis_index("dp")
    x, yhi = lon // 2, lon % 2
    z, ylo, c = dp // 4, (dp // 2) % 2, dp % 2
    y = yhi * 2 + ylo
    here = {"x": x, "y": y, "z": z}
    alloc = Sems()

    def dev(xx, yy, zz, cc):
        return {"lon": xx * 2 + yy // 2, "dp": (zz * 2 + yy % 2) * 2 + cc}

    def along(axis, step):
        at = dict(here)
        at[axis] = (at[axis] + step) % 4
        return dev(at["x"], at["y"], at["z"], c)

    sibling = dev(x, y, z, 1 - c)

    def rcopy(src, dst, send, recv, to):
        return pltpu.make_async_remote_copy(
            src_ref=src, dst_ref=dst, send_sem=sem.at[send], recv_sem=sem.at[recv],
            device_id=to, device_id_type=pl.DeviceIdType.MESH,
        )

    def got(ref, number):
        rcopy(ref, ref, number, number, sibling).wait_recv()

    def sent(ref, number):
        rcopy(ref, ref, number, number, sibling).wait_send()

    def to_lon(i):
        return {"lon": i, "dp": dp}

    def to_dp(i):
        return {"lon": lon, "dp": i}

    loads = [
        pltpu.make_async_copy(src, dst, sem.at[alloc.take()])
        for src, dst in ((win_in, win), (lat_in, lat), (tgt_in, tgt))
    ]
    for one in loads:
        one.start()

    bar = pltpu.get_barrier_semaphore()

    def greet(to):
        pl.semaphore_signal(bar, inc=1, device_id=to, device_id_type=pl.DeviceIdType.MESH)

    @pl.loop(1, NLON)
    def _(k):
        greet(to_lon((lon + k) % NLON))

    @pl.loop(1, NDP)
    def _(k):
        greet(to_dp((dp + k) % NDP))

    far = (y + 3 + 2 * ylo) % 4
    greet(dev(x, far, z, c))

    class Exchange:
        def __init__(self, rx, me, size, to):
            self.rx, self.me, self.size, self.to = rx, me, size, to
            self.base = alloc.take(2)

        def send(self):
            @pl.loop(1, self.size)
            def _(k):
                slot = self.rx.at[self.me]
                rcopy(slot, slot, self.base, self.base + 1, self.to((self.me + k) % self.size)).start()

        def wait(self):
            others = self.rx.at[0 : self.size - 1]
            sent(others, self.base)
            got(others, self.base + 1)

        def total(self):
            return functools.reduce(lambda a, b: a + b, [self.rx[i] for i in range(self.size)])

    def at_row(r):
        return pl.ds(pl.multiple_of(r * COLS, COLS), COLS)

    def sums(r, tot):
        v = lat[r].astype(F32)
        hs[0, pl.ds(r, 1), :] = v[COLS - 1 : COLS]
        hs[1, pl.ds(r, 1), :] = v[0:1]
        return tot + jnp.sum(v, axis=0, keepdims=True)

    loads[1].wait()
    chan = lax.fori_loop(0, ROWS, sums, jnp.zeros((1, C), F32))
    gi = jnp.floor((lax.broadcasted_iota(jnp.int32, (C, C), 0).astype(F32) + 0.5) * 0.05)
    gj = jnp.floor((lax.broadcasted_iota(jnp.int32, (C, C), 1).astype(F32) + 0.5) * 0.05)
    mask[...] = jnp.where(gi == gj, 1.0, 0.0).astype(BF16)

    def group_sum(v):
        top = v.astype(BF16)
        rest = v - top.astype(F32)
        mid = rest.astype(BF16)
        low = (rest - mid.astype(F32)).astype(BF16)
        zeros = jnp.zeros((8, C), F32)
        terms = jnp.concatenate(
            [top.astype(F32), mid.astype(F32), low.astype(F32), zeros], axis=0
        ).astype(BF16)
        out = jnp.dot(terms, mask[...], preferred_element_type=F32)
        return out[0:8] + out[8:16] + out[16:24]

    sub = lax.broadcasted_iota(jnp.int32, (8, C), 0)
    pl.semaphore_wait(bar, NLON - 1 + NDP - 1 + 1)
    loads[0].wait()

    swaps = alloc.take(6)

    def swap_tap(j):
        return rcopy(win.at[2 * j + 1 - c], sibw.at[j], swaps, swaps + 1 + j, sibling)

    for j in range(4):
        swap_tap(j).start()
    pl.when(c == 1)(lambda: swap_tap(4).start())

    right, left = to_lon((lon + 1) % NLON), to_lon((lon + NLON - 1) % NLON)
    hsem = alloc.take(2)
    rcopy(hs.at[0], hr.at[0], hsem, hsem + 1, right).start()
    rcopy(hs.at[1], hr.at[1], hsem, hsem + 1, left).start()

    local_mean = group_sum(jnp.where(sub == 0, chan, 0.0))[0:1] / (PIX * 20)

    odd = x % 2
    own_d = z * 2 + ylo

    def jyz(slot, core):
        return (odd, 2 + (1 - core) * odd, 4 - core)[slot]

    def jx(slot):
        return (1 - odd, 3 - odd)[slot]

    def assemble(j):
        got(sibw.at[j], swaps + 1 + j)
        a = win[2 * j + c].astype(F32)
        b = sibw[j].astype(F32)
        first = jnp.where(c == 0, a, b)
        second = jnp.where(c == 0, b, a)
        rows = pl.ds(pl.multiple_of(own_d * 80, 16), 80)
        wg_all[2 * j + c, rows, :] = jnp.concatenate([first, second], axis=0).astype(BF16)

    LO, HI = (0, 48), (48, 32)

    def blk(j, zz, parity, part=(0, 80)):
        row = pl.multiple_of((zz * 2 + parity) * 80 + part[0], 16)
        return wg_all.at[2 * j + c, pl.ds(row, part[1]), :]

    zl, zr, zo = (z + 3) % 4, (z + 1) % 4, (z + 2) % 4
    gz = [alloc.take(3) for _ in range(3)]
    gy = [alloc.take(5) for _ in range(3)]
    gx = [alloc.take(8) for _ in range(2)]
    gd = [alloc.take(2) for _ in range(5)]

    def rows_of(n):
        return wg_all.at[0, 0:n]

    def two_ways(axis, j, zz, parity, send, recv, slot):
        plus, minus = (LO, HI) if slot % 2 == 0 else (HI, LO)
        one, two = blk(j, zz, parity, plus), blk(j, zz, parity, minus)
        return (
            rcopy(one, one, send, recv, along(axis, 1)),
            rcopy(two, two, send, recv, along(axis, 3)),
        )

    def y_copies(s, k, zz):
        return two_ways("y", jyz(s, c), zz, ylo, gy[s], gy[s] + 1 + k, s)

    def x_copies(s, k, zz, parity):
        return two_ways("x", jyz(s, c), zz, parity, gx[s], gx[s] + k, s)

    def z1(s):
        block = blk(jyz(s, c), z, ylo)
        return [rcopy(block, block, gz[s], gz[s] + 1, along("z", k)) for k in (1, 3)]

    def z2(s):
        j = jyz(s, c)
        plus, minus = (LO, HI) if s % 2 == 0 else (HI, LO)
        one, two = blk(j, zl, ylo, plus), blk(j, zr, ylo, minus)
        return (
            rcopy(one, one, gz[s], gz[s] + 2, along("z", 1)),
            rcopy(two, two, gz[s], gz[s] + 2, along("z", 3)),
        )

    def start(copies):
        for one in copies:
            one.start()

    AROUND = (z, zl, zr, zo)

    def over_x(s, body):
        if s == 0:
            body()
        elif s == 1:
            pl.when(c == 0)(body)

    BLOCKS = ((z, ylo), (zl, ylo), (zr, ylo), (zo, ylo), *((q, 1 - ylo) for q in AROUND))

    def across(n, j, core, k):
        zz, parity = BLOCKS[k]
        row = pl.multiple_of((zz * 2 + parity) * 80, 16)
        block = wg_all.at[2 * j + core, pl.ds(row, 80), :]
        return rcopy(block, block, gd[n], gd[n] + 1, sibling)

    def give(n, j, ks):
        start([across(n, j, c, k) for k in ks])

    def wave1(s):
        assemble(jyz(s, c))
        start(z1(s))
        start(y_copies(s, 0, z))
        give(s, jyz(s, c), (0,))

    def x_send(s, ks):
        def body():
            for k in ks:
                start(x_copies(s, k, *BLOCKS[k]))

        over_x(s, body)

    def wave2(s):
        got(rows_of(160), gz[s] + 1)
        start(z2(s))
        start(y_copies(s, 1, zl))
        start(y_copies(s, 2, zr))
        x_send(s, (1, 2))
        block = blk(jyz(s, c), z, ylo)
        for zz in (zr, zl):
            rcopy(block, block, gz[s], gd[s] + 1, dev(x, y, zz, 1 - c)).start()

    def wave3(s):
        got(rows_of(80), gz[s] + 2)
        start(y_copies(s, 3, zo))
        x_send(s, (3,))
        give(s, jyz(s, c), (3,))

    def wave4(s):
        for k in range(4):
            got(rows_of(80), gy[s] + 1 + k)
            x_send(s, (4 + k,))
            give(s, jyz(s, c), (4 + k,))

    def own_x(s):
        def body():
            assemble(jx(s))
            give(3 + s, jx(s), (0,))

        over_x(s, body)

    def wave_x(s, ks):
        def body():
            for k in ks:
                got(rows_of(80), gx[s] + k)
                give(3 + s, jx(s), (k,))

        over_x(s, body)

    def from_sibling(s):
        got(rows_of(C), gd[s] + 1)

    def from_sibling_x(s):
        def body():
            got(rows_of(C), gd[3 + s] + 1)

        if s == 0:
            body()
        else:
            pl.when(c == 1)(body)

    def sends_done():
        pl.when(c == 0)(lambda: sent(sibw.at[0:4], swaps))
        pl.when(c == 1)(lambda: sent(sibw, swaps))
        for s in range(3):
            sent(rows_of(400), gz[s])
            sent(rows_of(320), gy[s])
            sent(rows_of(480), gd[s])
        for s in range(2):

            def body(s=s):
                sent(rows_of(560), gx[s])
                sent(rows_of(C), gd[3 + s])

            over_x(s, body)

    wave1(0)
    wave1(1)
    dacc[...] = jnp.zeros((PIX + 4 * COLS, C), F32)
    own_x(0)
    own_x(1)

    def squares(r, tot):
        d = lat[r].astype(F32) - local_mean
        return tot + jnp.sum(d * d, axis=0, keepdims=True)

    chan2 = lax.fori_loop(0, ROWS, squares, jnp.zeros((1, C), F32))
    m2loc = group_sum(jnp.where(sub == 0, chan2, 0.0))[0:1]
    stat[lon] = jnp.where(sub == 0, local_mean, jnp.where(sub == 1, m2loc, 0.0))
    ex_stat = Exchange(stat, lon, NLON, to_lon)
    ex_stat.send()

    wave2(0)
    wave1(2)
    ex_stat.wait()
    sent(hs, hsem)
    got(hr, hsem + 1)
    stats = [stat[i] for i in range(NLON)]
    mean = functools.reduce(lambda a, b: a + b, [s[0:1] for s in stats]) / NLON
    spread = functools.reduce(lambda a, b: a + b, [(s[0:1] - mean) * (s[0:1] - mean) for s in stats])
    within = functools.reduce(lambda a, b: a + b, [s[1:2] for s in stats])
    var = (within + (PIX * 20) * spread) / COUNT
    rstd = lax.rsqrt(var + 1e-05)
    gain, shift = gain_r[...].reshape(1, C), shift_r[...].reshape(1, C)

    def pre_of(v):
        normed = (v - mean) * rstd
        return normed, normed * gain + shift

    def silu(v):
        _, pre = pre_of(v)
        return pre * jax.nn.sigmoid(pre)

    hr[0] = silu(hr[0])
    hr[1] = silu(hr[1])
    edge = lax.broadcasted_iota(jnp.int32, (COLS, C), 0)

    def put_sides(dst, to, a, halo, r):
        before = jnp.where(edge == 0, halo[0, pl.ds(r, 1), :], pltpu.roll(a, 1, 0))
        after = jnp.where(edge == COLS - 1, halo[1, pl.ds(r, 1), :], pltpu.roll(a, COLS - 1, 0))
        dst[at_row(to), 0:C] = before.astype(BF16)
        dst[at_row(to), 2 * C : 3 * C] = after.astype(BF16)

    zero_row = jnp.zeros((COLS, 3 * C), BF16)
    for buf, ends in ((x3, (0, PADPIX - COLS)), (e3, (0, COLS, PADPIX, PADPIX + COLS))):
        for low in ends:
            buf[low : low + COLS, :] = zero_row

    def activate(first, end):
        @pl.loop(first, end)
        def _(r):
            _normed, pre = pre_of(lat[r].astype(F32))
            sig = jax.nn.sigmoid(pre)
            a = pre * sig
            dsilu[r] = sig * (1.0 + pre * (1.0 - sig))
            x3[at_row(r + 1), C : 2 * C] = a.astype(BF16)
            put_sides(x3, r + 1, a, hr, r)

    unit = jnp.where(
        lax.broadcasted_iota(jnp.int32, (256, 256), 0) == lax.broadcasted_iota(jnp.int32, (256, 256), 1),
        1.0, 0.0,
    ).astype(BF16)

    def turn(first, end):
        for j in range(first, end):
            low, high = j * 256, min(j * 256 + 256, 3 * C)
            n = high - low
            x3t[low:high, :] = lax.dot_general(
                unit[:n, :n], x3[:, low:high], NT, preferred_element_type=F32
            ).astype(BF16)

    def forward(tap, count, fresh=False):
        @pl.loop(0, 2)
        def _(m):
            fields = []
            for n in range(count):
                kh, kw = (tap + n) // 3, (tap + n) % 3
                rows = pl.ds(pl.multiple_of(kh * COLS + m * 512, COLS), 512)
                fields.append(x3[rows, pl.ds(pl.multiple_of(kw * C, 128), C)])
            w = wg_all[pl.ds(tap, count)].reshape(count * C, C)
            part = jnp.dot(jnp.concatenate(fields, axis=1), w, preferred_element_type=F32)
            out = pl.ds(pl.multiple_of(m * 512, 512), 512)
            acc[out, :] = part if fresh else acc[out, :] + part

    activate(0, 8)
    wave2(1)
    wave3(0)
    activate(8, ROWS)
    wave3(1)
    wave4(0)
    wave_x(0, (1, 2))
    turn(0, 3)
    wave2(2)
    wave_x(0, (3,))
    from_sibling(0)
    forward(2 * odd, 2, True)
    wave4(1)
    wave_x(1, (1, 2, 3))
    wave3(2)
    wave_x(0, (4, 5, 6, 7))
    turn(3, 8)
    from_sibling_x(0)
    forward(2 - 2 * odd, 2)
    wave_x(1, (4, 5, 6, 7))
    wave4(2)
    from_sibling(1)
    from_sibling_x(1)
    forward(4, 3)
    from_sibling(2)
    forward(7, 2)
    sends_done()

    loads[2].wait()
    bias = bias_r[...].reshape(1, C)

    def error(r, carry):
        sq, tot = carry
        v = acc[at_row(r), :] + bias + lat[r].astype(F32) - tgt[r].astype(F32)
        e3[at_row(r + 2), C : 2 * C] = v.astype(BF16)
        es[0, pl.ds(r, 1), :] = v[COLS - 1 : COLS]
        es[1, pl.ds(r, 1), :] = v[0:1]
        return sq + jnp.sum(v * v, axis=0, keepdims=True), tot + jnp.sum(v, axis=0, keepdims=True)

    zero = jnp.zeros((1, C), F32)
    sq, err_sum = lax.fori_loop(0, ROWS, error, (zero, zero))
    l1[lon] = jnp.broadcast_to(jnp.sum(sq, axis=1, keepdims=True), (8, 128))
    ex_l1 = Exchange(l1, lon, NLON, to_lon)
    ex_l1.send()
    esem = alloc.take(2)
    rcopy(es.at[0], er.at[0], esem, esem + 1, right).start()
    rcopy(es.at[1], er.at[1], esem, esem + 1, left).start()

    def back(m):
        low = m * (PADPIX // 3)
        w = jnp.concatenate(
            [
                jnp.concatenate([wg_all[3 * kh + kw] for kw in (2, 1, 0)], axis=1)
                for kh in range(3)
            ],
            axis=0,
        )
        part = lax.dot_general(
            e3[COLS + low : COLS + low + PADPIX // 3, :], w, NT, preferred_element_type=F32
        )
        for kh in range(3):
            out = slice(low + kh * COLS, low + kh * COLS + PADPIX // 3)
            dacc[out, :] = dacc[out, :] + part[:, kh * C : (kh + 1) * C]

    NRED = 9
    groups = [red[NRED * g : NRED * g + NRED] for g in range(3)]

    def order(kw, g):
        return ORDERS[(kw + g) % 3]

    def place(kw, g, core, lon_to, d):
        at = {"x": lon_to // 2, "y": (lon_to % 2) * 2 + d % 2, "z": d // 2}
        a1, a2, a3 = order(kw, g)
        return kw, core, at[a1], at[a2], at[a3]

    def weight_part(kw):
        for g in range(3):
            first, end = LANES[g]
            for d in range(8):
                groups[g][0][place(kw, g, 1, 7, d)] = jnp.zeros((16, end - first), BF16)
        err = jnp.concatenate(
            [e3[(2 - kh) * COLS : (2 - kh) * COLS + PADPIX, C : 2 * C] for kh in range(3)], axis=1
        )
        for half in range(2):
            top = kw * C + half * (C // 2)
            res = jnp.dot(x3t[top : top + C // 2, :], err, preferred_element_type=F32)
            res = res.astype(BF16)
            for d in range(4):
                for t in range(5):
                    low = d * 80 + t * 16
                    for kh in range(3):
                        s = kh * 5 + t
                        for g in range(3):
                            first, end = LANES[g]
                            groups[g][0][place(kw, g, s % 2, s // 2, half * 4 + d)] = res[
                                low : low + 16, kh * C + first : kh * C + end
                            ]
            for one in parts[kw].lanes:
                one.swaps[half].start()

    def add(out, terms):
        val = functools.reduce(lambda a, b: a + b, [t[...].astype(F32) for t in terms])
        out[...] = val.astype(out.dtype)

    send_sems = [alloc.take(4) for _ in range(3)]

    def reduce_sends_done():
        for g in range(3):
            rxs, r2rx, r3 = groups[g][1], groups[g][7], groups[g][8]
            sent(rxs, send_sems[g])
            sent(rxs.at[:, 0:3], send_sems[g] + 1)
            sent(r2rx, send_sems[g] + 2)
            sent(r3.at[:, 4:7], send_sems[g] + 3)

    class Lanes:
        def __init__(self, kw, g):
            wg, rxs, ra, rb, rc, rd, r2, r2rx, r3 = groups[g]
            self.r3rx = r3.at[kw, 4:7]
            self.kw, self.g, self.axes = kw, g, order(kw, g)
            self.rxs, self.r2, self.r2rx, self.r3 = rxs.at[kw], r2.at[kw], r2rx.at[kw], r3.at[kw]
            self.ra, self.rb, self.rc, self.rd = ra.at[kw], rb.at[kw], rc.at[kw], rd.at[kw]
            self.buf = wg.at[kw, c]
            send, self.recv = send_sems[g], alloc.take(5)
            self.two = wg.at[kw, 0, 0:2]
            self.swaps = []
            for half in range(2):
                part = [slice(None)] * 3
                part[self.axes.index("z")] = slice(2 * half, 2 * half + 2)
                self.swaps.append(
                    rcopy(
                        wg.at[(kw, 1 - c, *part)], self.rxs.at[tuple(part)], send, self.recv, sibling
                    )
                )
            axis = self.axes[0]
            self.me = [here[a] for a in self.axes]
            far_, up, down = ((self.me[0] + k) % 4 for k in (2, 1, 3))
            self.up, self.down = up, down
            self.first = [
                rcopy(src, dst, send + 1, self.recv + n, along(axis, to))
                for src, dst, n, to in (
                    (self.buf.at[far_, 0:2], self.ra, 1, 1),
                    (self.buf.at[far_, 2:4], self.rb, 1, 3),
                    (self.buf.at[up], self.rc, 2, 1),
                    (self.buf.at[down], self.rd, 2, 3),
                )
            ]
            self.second = self.direct(1, self.r2, self.r2rx, send + 2, self.recv + 3)
            self.third = self.direct(2, self.r3, self.r3rx, send + 3, self.recv + 4)

        def direct(self, stage, buf, rx, send, recv):
            return [
                rcopy(
                    buf.at[(self.me[stage] + k) % 4], rx.at[k - 1],
                    send, recv, along(self.axes[stage], k),
                )
                for k in (1, 3, 2)
            ]

        def join(self, mine_by, theirs_by):
            got(self.rxs, self.recv)

            @pl.loop(0, 4)
            def _(i):
                own = self.buf[i].astype(F32) * mine_by
                self.buf[i] = (own + self.rxs[i].astype(F32) * theirs_by).astype(BF16)

            start(self.first[:2])

        def middle(self):
            got(self.rc, self.recv + 1)
            add(self.buf.at[self.up, 0:2], [self.buf.at[self.up, 0:2], self.ra])
            add(self.buf.at[self.down, 2:4], [self.buf.at[self.down, 2:4], self.rb])
            start(self.first[2:])

        def end_first(self):
            got(self.two, self.recv + 2)
            add(self.r2, [self.buf.at[self.me[0]], self.rc, self.rd])
            start(self.second)

        def end_second(self):
            got(self.r2rx, self.recv + 3)
            add(self.r3.at[0:4], [self.r2.at[self.me[1]]] + [self.r2rx.at[k] for k in range(3)])
            start(self.third)

        def end_third(self):
            got(self.r3rx, self.recv + 4)
            val = self.r3[self.me[2]].astype(F32)
            for k in range(3):
                val = val + self.r3[4 + k].astype(F32)
            first, end = LANES[self.g]
            agb[self.kw, c, lon, :, first:end] = val.astype(BF16)

    class Reduce:
        def __init__(self, kw):
            self.kw = kw
            self.lanes = [Lanes(kw, g) for g in range(3)]
            slot = agb.at[kw, c, lon]
            self.sems = alloc.take(5)
            send, recv = self.sems, self.sems + 1
            self.over_y = rcopy(slot, slot, send, recv, dev(x, (y + 2) % 4, z, c))
            pair = agb.at[kw, c, pl.ds(2 * x, 2)]
            self.over_x = [rcopy(pair, pair, send, recv + 1, along("x", k)) for k in (1, 3, 2)]
            self.give = rcopy(agb.at[kw, c], agb.at[kw, c], send + 3, recv + 3, sibling)

        def join(self, mine_by, theirs_by):
            for one in self.lanes:
                one.join(mine_by, theirs_by)

        def step(self, n):
            kw = self.kw
            if n == 2:
                for one in self.lanes:
                    one.middle()
            elif n == 3:
                for one in self.lanes:
                    one.end_first()
            elif n == 4:
                for one in self.lanes:
                    one.end_second()
            elif n == 5:
                for one in self.lanes:
                    one.end_third()
                self.over_y.start()
            elif n == 6:
                got(agb.at[kw, c, 0], self.sems + 1)
                start(self.over_x)
            elif n == 7:
                got(agb.at[kw, c, 0:6], self.sems + 2)
                self.give.start()
            elif n == 8:
                got(agb.at[kw, 1 - c], self.sems + 4)
                sent(agb.at[kw, c, 0:7], self.sems)
                sent(agb.at[kw, c], self.sems + 3)
                for row in range(3):
                    tiles = []
                    for t in range(5):
                        s = row * 5 + t
                        tiles.append(agb[kw, s % 2, s // 2].astype(F32))
                    rows = jnp.concatenate(tiles, axis=0)
                    wout[3 * row + kw] = jnp.where(c == 0, rows[0:40], rows[40:80]) * SCALE

    parts = [Reduce(kw) for kw in range(3)]
    weight_part(0)

    ex_l1.wait()
    tweight = 1.0 / (1.0 + jnp.full((8, 128), ts[0], jnp.int32).astype(F32) / 250.0)
    pano = tweight * ex_l1.total() / (ROWS * COLS * NLON * C)
    lane = lax.broadcasted_iota(jnp.int32, (8, 128), 1)
    row8 = lax.broadcasted_iota(jnp.int32, (8, 128), 0)
    member = jnp.where(lane == jnp.full((8, 128), bk[0], jnp.int32), 1.0, 0.0).astype(F32)
    l2[dp] = jnp.where(
        row8 == 0, member * pano, jnp.where(row8 == 1, member, jnp.where(row8 == 2, tweight, 0.0))
    )
    ex_l2 = Exchange(l2, dp, NDP, to_dp)
    ex_l2.send()
    weight_part(1)
    ex_l2.wait()
    sums2 = ex_l2.total()
    denom = jnp.maximum(sums2[1:2], 1.0)
    bucket_mean = sums2[0:1] / denom
    lane1 = lane[0:1]
    limit = jnp.zeros((1, 128), jnp.int32)
    for b in range(4):
        limit = jnp.where(lane1 == b, jnp.full((1, 128), clip[b], jnp.int32), limit)
    limit = limit.astype(F32) / 1000.0
    losses = jnp.minimum(bucket_mean, limit)
    passing = jnp.where((bucket_mean < limit) & (lane1 < 4), 1.0, 0.0)

    def coef_of(tile):
        picked = jnp.sum(tile[1:2] * passing / denom, axis=1, keepdims=True)
        return tile[2:3, 0:1] * picked

    coef, sib_coef = coef_of(l2[dp]), coef_of(l2[dp + 1 - 2 * c])

    parts[0].join(coef, sib_coef)
    weight_part(2)
    parts[1].join(coef, sib_coef)
    parts[0].step(2)

    sent(es, esem)
    got(er, esem + 1)

    @pl.loop(0, ROWS)
    def _(r):
        put_sides(e3, r + 2, e3[at_row(r + 2), C : 2 * C].astype(F32), er, r)

    parts[1].step(2)
    parts[2].join(coef, sib_coef)
    parts[0].step(3)
    back(0)
    parts[2].step(2)
    parts[1].step(3)
    parts[0].step(4)
    back(1)
    parts[2].step(3)
    parts[1].step(4)
    parts[0].step(5)
    back(2)
    parts[2].step(4)
    parts[1].step(5)
    parts[0].step(6)

    def through(r, carry):
        a, b = carry
        normed = (lat[r].astype(F32) - mean) * rstd
        dpre = dacc[at_row(r + 2), :] * coef * dsilu[r]
        dacc[at_row(r + 2), :] = dpre
        return (
            a + jnp.sum(dpre, axis=0, keepdims=True),
            b + jnp.sum(dpre * normed, axis=0, keepdims=True),
        )

    s1, s2 = lax.fori_loop(0, ROWS, through, (zero, zero))
    g1[lon] = jnp.where(
        sub == 0, s1, jnp.where(sub == 1, s2, jnp.where(sub == 2, err_sum * coef, 0.0))
    )
    ex_g1 = Exchange(g1, lon, NLON, to_lon)
    ex_g1.send()
    parts[2].step(5)
    parts[1].step(6)
    parts[0].step(7)
    ex_g1.wait()
    pan = ex_g1.total()
    g2[dp] = pan
    ex_g2 = Exchange(g2, dp, NDP, to_dp)
    ex_g2.send()
    means = group_sum(pan * gain) / COUNT
    m1, m2 = means[0:1], means[1:2]

    @pl.loop(0, ROWS)
    def _(r):
        normed = (lat[r].astype(F32) - mean) * rstd
        dn = dacc[at_row(r + 2), :] * gain
        g = e3[at_row(r + 2), C : 2 * C].astype(F32) * coef
        igrad[r] = (g + rstd * (dn - m1 - normed * m2)).astype(BF16)

    parts[2].step(6)
    parts[1].step(7)
    parts[0].step(8)
    ex_g2.wait()
    totals = ex_g2.total() * SCALE
    wide = jnp.concatenate([losses] + [jnp.zeros_like(losses)] * 4, axis=1)
    sg_out[...] = jnp.where(sub == 3, wide, totals)
    parts[2].step(7)
    parts[1].step(8)
    parts[2].step(8)
    reduce_sends_done()
    assert alloc.used <= NUM_SEMS, alloc.used


def reduce_shapes(lanes):
    tile = (16, lanes)
    return [
        (3, 2, 4, 4, 4, *tile),
        (3, 4, 4, 4, *tile),
        (3, 2, 4, *tile),
        (3, 2, 4, *tile),
        (3, 4, 4, *tile),
        (3, 4, 4, *tile),
        (3, 4, 4, *tile),
        (3, 3, 4, *tile),
        (3, 7, *tile),
    ]


def shards(
    latents, target, norm_gain, norm_shift, conv_weight, conv_bias, timesteps, buckets, clip_milli
):
    win = jnp.transpose(conv_weight, (1, 2, 0, 3)).reshape(9, 40, C)
    vmem = pl.BlockSpec(memory_space=pltpu.VMEM)
    smem = pl.BlockSpec(memory_space=pltpu.SMEM)
    outs = pl.pallas_call(
        kernel,
        out_shape=(
            pltpu.VMEM((ROWS, COLS, C), BF16),
            pltpu.VMEM((9, 40, C), F32),
            pltpu.VMEM((8, C), F32),
        ),
        in_specs=[smem] * 3 + [pl.BlockSpec(memory_space=pl.ANY)] * 3 + [vmem] * 3,
        out_specs=(vmem,) * 3,
        scratch_shapes=[
            pltpu.VMEM((ROWS, COLS, C), BF16),
            pltpu.VMEM((ROWS, COLS, C), BF16),
            pltpu.VMEM((9, 40, C), BF16),
            pltpu.VMEM((ROWS, COLS, C), F32),
            pltpu.VMEM((5, 40, C), BF16),
            pltpu.VMEM((9, C, C), BF16),
            pltpu.VMEM((PADPIX, 3 * C), BF16),
            pltpu.VMEM((3 * C, PADPIX), BF16),
            pltpu.VMEM((PIX, C), F32),
            pltpu.VMEM((PIX + 4 * COLS, C), F32),
            pltpu.VMEM((PADPIX + 2 * COLS, 3 * C), BF16),
            pltpu.VMEM((3, 2, NLON, 16, C), BF16),
            pltpu.VMEM((C, C), BF16),
            pltpu.VMEM((NLON, 8, C), F32),
            pltpu.VMEM((2, ROWS, C), F32),
            pltpu.VMEM((2, ROWS, C), F32),
            pltpu.VMEM((2, ROWS, C), F32),
            pltpu.VMEM((2, ROWS, C), F32),
            pltpu.VMEM((NLON, 8, 128), F32),
            pltpu.VMEM((NDP, 8, 128), F32),
            pltpu.VMEM((NLON, 8, C), F32),
            pltpu.VMEM((NDP, 8, C), F32),
            pltpu.SemaphoreType.DMA((NUM_SEMS,)),
        ]
        + [pltpu.VMEM(shape, BF16) for first, end in LANES for shape in reduce_shapes(end - first)],
        compiler_params=pltpu.CompilerParams(
            collective_id=0, has_side_effects=True, vmem_limit_bytes=60 * 1024 * 1024
        ),
        cost_estimate=pl.CostEstimate(
            flops=3 * 2 * PIX * 9 * C * C, bytes_accessed=8 * 1024 * 1024, transcendentals=2 * PIX * C
        ),
    )(
        timesteps, buckets, clip_milli, latents[0], target[0], win,
        norm_gain, norm_shift, conv_bias,
    )
    igrad, wout, sg = outs
    weight_grad = jnp.transpose(wout.reshape(3, 3, 40, C), (2, 0, 1, 3))
    return sg[3, :4], igrad[None], weight_grad, sg[1], sg[0], sg[2]


def solution(mesh):
    placed = (
        P("dp", None, "lon", None),
        P("dp", None, "lon", None),
        P(),
        P(),
        P("dp", None, None, None),
        P(),
        P("dp"),
        P("dp"),
        P(),
    )
    return jax.shard_map(
        shards,
        mesh=mesh,
        in_specs=placed,
        out_specs=(P(), P("dp", None, "lon", None), P("dp", None, None, None), P(), P(), P()),
        check_vma=False,
    )
```

```python
import functools

import jax
import jax.numpy as jnp
from jax import lax
from jax.experimental import pallas as pl
from jax.experimental.pallas import tpu as pltpu
from jax.sharding import PartitionSpec as P

F32 = jnp.float32
BF16 = jnp.bfloat16
ROWS, COLS, C = 16, 64, 640
PIX = ROWS * COLS
PADPIX = PIX + 2 * COLS
NLON, NDP = 8, 16
COUNT = ROWS * COLS * NLON * (C // 32)
SCALE = 1.0 / (ROWS * COLS)
ORDERS = ("xyz", "yzx", "zxy")
LANES = ((0, 256), (256, 512), (512, 640))
NT = (((1,), (1,)), ((), ()))


class Sems:
    def __init__(self):
        self.used = 0

    def take(self, n=1):
        first = self.used
        self.used += n
        return first


NUM_SEMS = 200


def kernel(
    ts, bk, clip, lat_in, tgt_in, win_in, gain_r, shift_r, bias_r,
    igrad, wout, sg_out,
    lat, tgt, win, dsilu, sibw, wg_all, x3, x3t, acc, dacc, e3, agb,
    mask, stat, hs, hr, es, er, l1, l2, g1, g2, sem, *red,
):
    lon, dp = lax.axis_index("lon"), lax.axis_index("dp")
    x, yhi = lon // 2, lon % 2
    z, ylo, c = dp // 4, (dp // 2) % 2, dp % 2
    y = yhi * 2 + ylo
    here = {"x": x, "y": y, "z": z}
    alloc = Sems()

    def dev(xx, yy, zz, cc):
        return {"lon": xx * 2 + yy // 2, "dp": (zz * 2 + yy % 2) * 2 + cc}

    def along(axis, step):
        at = dict(here)
        at[axis] = (at[axis] + step) % 4
        return dev(at["x"], at["y"], at["z"], c)

    sibling = dev(x, y, z, 1 - c)

    def rcopy(src, dst, send, recv, to):
        return pltpu.make_async_remote_copy(
            src_ref=src, dst_ref=dst, send_sem=sem.at[send], recv_sem=sem.at[recv],
            device_id=to, device_id_type=pl.DeviceIdType.MESH,
        )

    def got(ref, number):
        rcopy(ref, ref, number, number, sibling).wait_recv()

    def sent(ref, number):
        rcopy(ref, ref, number, number, sibling).wait_send()

    def to_lon(i):
        return {"lon": i, "dp": dp}

    def to_dp(i):
        return {"lon": lon, "dp": i}

    loads = [
        pltpu.make_async_copy(src, dst, sem.at[alloc.take()])
        for src, dst in ((win_in, win), (lat_in, lat), (tgt_in, tgt))
    ]
    for one in loads:
        one.start()

    bar = pltpu.get_barrier_semaphore()

    def greet(to):
        pl.semaphore_signal(bar, inc=1, device_id=to, device_id_type=pl.DeviceIdType.MESH)

    @pl.loop(1, NLON)
    def _(k):
        greet(to_lon((lon + k) % NLON))

    @pl.loop(1, NDP)
    def _(k):
        greet(to_dp((dp + k) % NDP))

    far = (y + 3 + 2 * ylo) % 4
    greet(dev(x, far, z, c))

    class Exchange:
        def __init__(self, rx, me, size, to):
            self.rx, self.me, self.size, self.to = rx, me, size, to
            self.base = alloc.take(2)

        def send(self):
            @pl.loop(1, self.size)
            def _(k):
                slot = self.rx.at[self.me]
                rcopy(slot, slot, self.base, self.base + 1, self.to((self.me + k) % self.size)).start()

        def wait(self):
            others = self.rx.at[0 : self.size - 1]
            sent(others, self.base)
            got(others, self.base + 1)

        def total(self):
            return functools.reduce(lambda a, b: a + b, [self.rx[i] for i in range(self.size)])

    def at_row(r):
        return pl.ds(pl.multiple_of(r * COLS, COLS), COLS)

    def sums(r, tot):
        v = lat[r].astype(F32)
        hs[0, pl.ds(r, 1), :] = v[COLS - 1 : COLS]
        hs[1, pl.ds(r, 1), :] = v[0:1]
        return tot + jnp.sum(v, axis=0, keepdims=True)

    loads[1].wait()
    chan = lax.fori_loop(0, ROWS, sums, jnp.zeros((1, C), F32))
    gi = jnp.floor((lax.broadcasted_iota(jnp.int32, (C, C), 0).astype(F32) + 0.5) * 0.05)
    gj = jnp.floor((lax.broadcasted_iota(jnp.int32, (C, C), 1).astype(F32) + 0.5) * 0.05)
    mask[...] = jnp.where(gi == gj, 1.0, 0.0).astype(BF16)

    def group_sum(v):
        top = v.astype(BF16)
        rest = v - top.astype(F32)
        mid = rest.astype(BF16)
        low = (rest - mid.astype(F32)).astype(BF16)
        zeros = jnp.zeros((8, C), F32)
        terms = jnp.concatenate(
            [top.astype(F32), mid.astype(F32), low.astype(F32), zeros], axis=0
        ).astype(BF16)
        out = jnp.dot(terms, mask[...], preferred_element_type=F32)
        return out[0:8] + out[8:16] + out[16:24]

    sub = lax.broadcasted_iota(jnp.int32, (8, C), 0)
    pl.semaphore_wait(bar, NLON - 1 + NDP - 1 + 1)
    loads[0].wait()

    swaps = alloc.take(6)

    def swap_tap(j):
        return rcopy(win.at[2 * j + 1 - c], sibw.at[j], swaps, swaps + 1 + j, sibling)

    for j in range(4):
        swap_tap(j).start()
    pl.when(c == 1)(lambda: swap_tap(4).start())

    right, left = to_lon((lon + 1) % NLON), to_lon((lon + NLON - 1) % NLON)
    hsem = alloc.take(2)
    rcopy(hs.at[0], hr.at[0], hsem, hsem + 1, right).start()
    rcopy(hs.at[1], hr.at[1], hsem, hsem + 1, left).start()

    local_mean = group_sum(jnp.where(sub == 0, chan, 0.0))[0:1] / (PIX * 20)

    odd = x % 2
    own_d = z * 2 + ylo

    def jyz(slot, core):
        return (odd, 2 + (1 - core) * odd, 4 - core)[slot]

    def jx(slot):
        return (1 - odd, 3 - odd)[slot]

    def assemble(j):
        got(sibw.at[j], swaps + 1 + j)
        a = win[2 * j + c].astype(F32)
        b = sibw[j].astype(F32)
        first = jnp.where(c == 0, a, b)
        second = jnp.where(c == 0, b, a)
        rows = pl.ds(pl.multiple_of(own_d * 80, 16), 80)
        wg_all[2 * j + c, rows, :] = jnp.concatenate([first, second], axis=0).astype(BF16)

    LO, HI = (0, 48), (48, 32)

    def blk(j, zz, parity, part=(0, 80)):
        row = pl.multiple_of((zz * 2 + parity) * 80 + part[0], 16)
        return wg_all.at[2 * j + c, pl.ds(row, part[1]), :]

    zl, zr, zo = (z + 3) % 4, (z + 1) % 4, (z + 2) % 4
    gz = [alloc.take(3) for _ in range(3)]
    gy = [alloc.take(5) for _ in range(3)]
    gx = [alloc.take(8) for _ in range(2)]
    gd = [alloc.take(2) for _ in range(5)]

    def rows_of(n):
        return wg_all.at[0, 0:n]

    def two_ways(axis, j, zz, parity, send, recv, slot):
        plus, minus = (LO, HI) if slot % 2 == 0 else (HI, LO)
        one, two = blk(j, zz, parity, plus), blk(j, zz, parity, minus)
        return (
            rcopy(one, one, send, recv, along(axis, 1)),
            rcopy(two, two, send, recv, along(axis, 3)),
        )

    def y_copies(s, k, zz):
        return two_ways("y", jyz(s, c), zz, ylo, gy[s], gy[s] + 1 + k, s)

    def x_copies(s, k, zz, parity):
        return two_ways("x", jyz(s, c), zz, parity, gx[s], gx[s] + k, s)

    def z1(s):
        block = blk(jyz(s, c), z, ylo)
        return [rcopy(block, block, gz[s], gz[s] + 1, along("z", k)) for k in (1, 3)]

    def z2(s):
        j = jyz(s, c)
        plus, minus = (LO, HI) if s % 2 == 0 else (HI, LO)
        one, two = blk(j, zl, ylo, plus), blk(j, zr, ylo, minus)
        return (
            rcopy(one, one, gz[s], gz[s] + 2, along("z", 1)),
            rcopy(two, two, gz[s], gz[s] + 2, along("z", 3)),
        )

    def start(copies):
        for one in copies:
            one.start()

    AROUND = (z, zl, zr, zo)

    def over_x(s, body):
        if s == 0:
            body()
        elif s == 1:
            pl.when(c == 0)(body)

    BLOCKS = ((z, ylo), (zl, ylo), (zr, ylo), (zo, ylo), *((q, 1 - ylo) for q in AROUND))

    def across(n, j, core, k):
        zz, parity = BLOCKS[k]
        row = pl.multiple_of((zz * 2 + parity) * 80, 16)
        block = wg_all.at[2 * j + core, pl.ds(row, 80), :]
        return rcopy(block, block, gd[n], gd[n] + 1, sibling)

    def give(n, j, ks):
        start([across(n, j, c, k) for k in ks])

    def wave1(s):
        assemble(jyz(s, c))
        start(z1(s))
        start(y_copies(s, 0, z))
        give(s, jyz(s, c), (0,))

    def x_send(s, ks):
        def body():
            for k in ks:
                start(x_copies(s, k, *BLOCKS[k]))

        over_x(s, body)

    def wave2(s):
        got(rows_of(160), gz[s] + 1)
        start(z2(s))
        start(y_copies(s, 1, zl))
        start(y_copies(s, 2, zr))
        x_send(s, (1, 2))
        give(s, jyz(s, c), (1, 2))

    def wave3(s):
        got(rows_of(80), gz[s] + 2)
        start(y_copies(s, 3, zo))
        x_send(s, (3,))
        give(s, jyz(s, c), (3,))

    def wave4(s):
        for k in range(4):
            got(rows_of(80), gy[s] + 1 + k)
            x_send(s, (4 + k,))
            give(s, jyz(s, c), (4 + k,))

    def own_x(s):
        def body():
            assemble(jx(s))
            give(3 + s, jx(s), (0,))

        over_x(s, body)

    def wave_x(s, ks):
        def body():
            for k in ks:
                got(rows_of(80), gx[s] + k)
                give(3 + s, jx(s), (k,))

        over_x(s, body)

    def from_sibling(s):
        got(rows_of(C), gd[s] + 1)

    def from_sibling_x(s):
        def body():
            got(rows_of(C), gd[3 + s] + 1)

        if s == 0:
            body()
        else:
            pl.when(c == 1)(body)

    def sends_done():
        pl.when(c == 0)(lambda: sent(sibw.at[0:4], swaps))
        pl.when(c == 1)(lambda: sent(sibw, swaps))
        for s in range(3):
            sent(rows_of(240), gz[s])
            sent(rows_of(320), gy[s])
            sent(rows_of(C), gd[s])
        for s in range(2):

            def body(s=s):
                sent(rows_of(560), gx[s])
                sent(rows_of(C), gd[3 + s])

            over_x(s, body)

    wave1(0)
    wave1(1)
    dacc[...] = jnp.zeros((PIX + 4 * COLS, C), F32)
    own_x(0)
    own_x(1)

    def squares(r, tot):
        d = lat[r].astype(F32) - local_mean
        return tot + jnp.sum(d * d, axis=0, keepdims=True)

    chan2 = lax.fori_loop(0, ROWS, squares, jnp.zeros((1, C), F32))
    m2loc = group_sum(jnp.where(sub == 0, chan2, 0.0))[0:1]
    stat[lon] = jnp.where(sub == 0, local_mean, jnp.where(sub == 1, m2loc, 0.0))
    ex_stat = Exchange(stat, lon, NLON, to_lon)
    ex_stat.send()

    wave2(0)
    wave1(2)
    ex_stat.wait()
    sent(hs, hsem)
    got(hr, hsem + 1)
    stats = [stat[i] for i in range(NLON)]
    mean = functools.reduce(lambda a, b: a + b, [s[0:1] for s in stats]) / NLON
    spread = functools.reduce(lambda a, b: a + b, [(s[0:1] - mean) * (s[0:1] - mean) for s in stats])
    within = functools.reduce(lambda a, b: a + b, [s[1:2] for s in stats])
    var = (within + (PIX * 20) * spread) / COUNT
    rstd = lax.rsqrt(var + 1e-05)
    gain, shift = gain_r[...].reshape(1, C), shift_r[...].reshape(1, C)

    def pre_of(v):
        normed = (v - mean) * rstd
        return normed, normed * gain + shift

    def silu(v):
        _, pre = pre_of(v)
        return pre * jax.nn.sigmoid(pre)

    hr[0] = silu(hr[0])
    hr[1] = silu(hr[1])
    edge = lax.broadcasted_iota(jnp.int32, (COLS, C), 0)

    def put_sides(dst, to, a, halo, r):
        before = jnp.where(edge == 0, halo[0, pl.ds(r, 1), :], pltpu.roll(a, 1, 0))
        after = jnp.where(edge == COLS - 1, halo[1, pl.ds(r, 1), :], pltpu.roll(a, COLS - 1, 0))
        dst[at_row(to), 0:C] = before.astype(BF16)
        dst[at_row(to), 2 * C : 3 * C] = after.astype(BF16)

    zero_row = jnp.zeros((COLS, 3 * C), BF16)
    for buf, ends in ((x3, (0, PADPIX - COLS)), (e3, (0, COLS, PADPIX, PADPIX + COLS))):
        for low in ends:
            buf[low : low + COLS, :] = zero_row

    def activate(first, end):
        @pl.loop(first, end)
        def _(r):
            _normed, pre = pre_of(lat[r].astype(F32))
            sig = jax.nn.sigmoid(pre)
            a = pre * sig
            dsilu[r] = sig * (1.0 + pre * (1.0 - sig))
            x3[at_row(r + 1), C : 2 * C] = a.astype(BF16)
            put_sides(x3, r + 1, a, hr, r)

    unit = jnp.where(
        lax.broadcasted_iota(jnp.int32, (256, 256), 0) == lax.broadcasted_iota(jnp.int32, (256, 256), 1),
        1.0, 0.0,
    ).astype(BF16)

    def turn(first, end):
        for j in range(first, end):
            low, high = j * 256, min(j * 256 + 256, 3 * C)
            n = high - low
            x3t[low:high, :] = lax.dot_general(
                unit[:n, :n], x3[:, low:high], NT, preferred_element_type=F32
            ).astype(BF16)

    def forward(tap, count, fresh=False):
        @pl.loop(0, 2)
        def _(m):
            fields = []
            for n in range(count):
                kh, kw = (tap + n) // 3, (tap + n) % 3
                rows = pl.ds(pl.multiple_of(kh * COLS + m * 512, COLS), 512)
                fields.append(x3[rows, pl.ds(pl.multiple_of(kw * C, 128), C)])
            w = wg_all[pl.ds(tap, count)].reshape(count * C, C)
            part = jnp.dot(jnp.concatenate(fields, axis=1), w, preferred_element_type=F32)
            out = pl.ds(pl.multiple_of(m * 512, 512), 512)
            acc[out, :] = part if fresh else acc[out, :] + part

    activate(0, 4)
    wave2(1)
    activate(4, 8)
    wave3(0)
    activate(8, 12)
    wave3(1)
    activate(12, ROWS)
    wave4(0)
    wave_x(0, (1, 2))
    turn(0, 3)
    wave2(2)
    wave_x(0, (3,))
    turn(3, 6)
    wave4(1)
    wave_x(1, (1, 2, 3))
    from_sibling(0)
    forward(2 * odd, 2, True)
    wave3(2)
    wave_x(0, (4, 5, 6, 7))
    turn(6, 8)
    from_sibling_x(0)
    forward(2 - 2 * odd, 2)
    wave_x(1, (4, 5, 6, 7))
    wave4(2)
    from_sibling(1)
    from_sibling_x(1)
    forward(4, 3)
    from_sibling(2)
    forward(7, 2)
    sends_done()

    loads[2].wait()
    bias = bias_r[...].reshape(1, C)

    def error(r, carry):
        sq, tot = carry
        v = acc[at_row(r), :] + bias + lat[r].astype(F32) - tgt[r].astype(F32)
        e3[at_row(r + 2), C : 2 * C] = v.astype(BF16)
        es[0, pl.ds(r, 1), :] = v[COLS - 1 : COLS]
        es[1, pl.ds(r, 1), :] = v[0:1]
        return sq + jnp.sum(v * v, axis=0, keepdims=True), tot + jnp.sum(v, axis=0, keepdims=True)

    zero = jnp.zeros((1, C), F32)
    sq, err_sum = lax.fori_loop(0, ROWS, error, (zero, zero))
    l1[lon] = jnp.broadcast_to(jnp.sum(sq, axis=1, keepdims=True), (8, 128))
    ex_l1 = Exchange(l1, lon, NLON, to_lon)
    ex_l1.send()
    esem = alloc.take(2)
    rcopy(es.at[0], er.at[0], esem, esem + 1, right).start()
    rcopy(es.at[1], er.at[1], esem, esem + 1, left).start()

    def back(m):
        rows = PADPIX // 4
        low = m * rows
        w = jnp.concatenate(
            [
                jnp.concatenate([wg_all[3 * kh + kw] for kw in (2, 1, 0)], axis=1)
                for kh in range(3)
            ],
            axis=0,
        )
        part = lax.dot_general(
            e3[COLS + low : COLS + low + rows, :], w, NT, preferred_element_type=F32
        )
        for kh in range(3):
            out = slice(low + kh * COLS, low + kh * COLS + rows)
            dacc[out, :] = dacc[out, :] + part[:, kh * C : (kh + 1) * C]

    NRED = 9
    groups = [red[NRED * g : NRED * g + NRED] for g in range(3)]

    def order(kw, g):
        return ORDERS[(kw + g) % 3]

    def place(kw, g, core, lon_to, d):
        at = {"x": lon_to // 2, "y": (lon_to % 2) * 2 + d % 2, "z": d // 2}
        a1, a2, a3 = order(kw, g)
        return kw, core, at[a1], at[a2], at[a3]

    def weight_part(kw):
        for g in range(3):
            first, end = LANES[g]
            for d in range(8):
                groups[g][0][place(kw, g, 1, 7, d)] = jnp.zeros((16, end - first), BF16)
        err = jnp.concatenate(
            [e3[(2 - kh) * COLS : (2 - kh) * COLS + PADPIX, C : 2 * C] for kh in range(3)], axis=1
        )
        for half in range(2):
            top = kw * C + half * (C // 2)
            res = jnp.dot(x3t[top : top + C // 2, :], err, preferred_element_type=F32)
            res = res.astype(BF16)
            for d in range(4):
                for t in range(5):
                    low = d * 80 + t * 16
                    for kh in range(3):
                        s = kh * 5 + t
                        for g in range(3):
                            first, end = LANES[g]
                            groups[g][0][place(kw, g, s % 2, s // 2, half * 4 + d)] = res[
                                low : low + 16, kh * C + first : kh * C + end
                            ]

    def add(out, terms):
        val = functools.reduce(lambda a, b: a + b, [t[...].astype(F32) for t in terms])
        out[...] = val.astype(out.dtype)

    send_sems = [alloc.take(4) for _ in range(3)]

    def reduce_sends_done():
        for g in range(3):
            rxs, r2rx, r3 = groups[g][1], groups[g][7], groups[g][8]
            sent(rxs, send_sems[g])
            sent(rxs.at[:, 0:3], send_sems[g] + 1)
            sent(r2rx, send_sems[g] + 2)
            sent(r3.at[:, 4:7], send_sems[g] + 3)

    class Lanes:
        def __init__(self, kw, g):
            wg, rxs, ra, rb, rc, rd, r2, r2rx, r3 = groups[g]
            self.r3rx = r3.at[kw, 4:7]
            self.kw, self.g, self.axes = kw, g, order(kw, g)
            self.rxs, self.r2, self.r2rx, self.r3 = rxs.at[kw], r2.at[kw], r2rx.at[kw], r3.at[kw]
            self.ra, self.rb, self.rc, self.rd = ra.at[kw], rb.at[kw], rc.at[kw], rd.at[kw]
            self.buf = wg.at[kw, c]
            send, self.recv = send_sems[g], alloc.take(5)
            self.two = wg.at[kw, 0, 0:2]
            self.swap = rcopy(wg.at[kw, 1 - c], self.rxs, send, self.recv, sibling)
            axis = self.axes[0]
            self.me = [here[a] for a in self.axes]
            far_, up, down = ((self.me[0] + k) % 4 for k in (2, 1, 3))
            self.up, self.down = up, down
            self.first = [
                rcopy(src, dst, send + 1, self.recv + n, along(axis, to))
                for src, dst, n, to in (
                    (self.buf.at[far_, 0:2], self.ra, 1, 1),
                    (self.buf.at[far_, 2:4], self.rb, 1, 3),
                    (self.buf.at[up], self.rc, 2, 1),
                    (self.buf.at[down], self.rd, 2, 3),
                )
            ]
            self.second = self.direct(1, self.r2, self.r2rx, send + 2, self.recv + 3)
            self.third = self.direct(2, self.r3, self.r3rx, send + 3, self.recv + 4)

        def direct(self, stage, buf, rx, send, recv):
            return [
                rcopy(
                    buf.at[(self.me[stage] + k) % 4], rx.at[k - 1],
                    send, recv, along(self.axes[stage], k),
                )
                for k in (1, 3, 2)
            ]

        def join(self, mine_by, theirs_by):
            got(self.rxs, self.recv)

            @pl.loop(0, 4)
            def _(i):
                own = self.buf[i].astype(F32) * mine_by
                self.buf[i] = (own + self.rxs[i].astype(F32) * theirs_by).astype(BF16)

            start(self.first[:2])

        def middle(self):
            got(self.rc, self.recv + 1)
            add(self.buf.at[self.up, 0:2], [self.buf.at[self.up, 0:2], self.ra])
            add(self.buf.at[self.down, 2:4], [self.buf.at[self.down, 2:4], self.rb])
            start(self.first[2:])

        def end_first(self):
            got(self.two, self.recv + 2)
            add(self.r2, [self.buf.at[self.me[0]], self.rc, self.rd])
            start(self.second)

        def end_second(self):
            got(self.r2rx, self.recv + 3)
            add(self.r3.at[0:4], [self.r2.at[self.me[1]]] + [self.r2rx.at[k] for k in range(3)])
            start(self.third)

        def end_third(self):
            got(self.r3rx, self.recv + 4)
            val = self.r3[self.me[2]].astype(F32)
            for k in range(3):
                val = val + self.r3[4 + k].astype(F32)
            first, end = LANES[self.g]
            agb[self.kw, c, lon, :, first:end] = val.astype(BF16)

    class Reduce:
        def __init__(self, kw):
            self.kw = kw
            self.lanes = [Lanes(kw, g) for g in range(3)]
            slot = agb.at[kw, c, lon]
            self.sems = alloc.take(5)
            send, recv = self.sems, self.sems + 1
            self.over_y = rcopy(slot, slot, send, recv, dev(x, (y + 2) % 4, z, c))
            pair = agb.at[kw, c, pl.ds(2 * x, 2)]
            self.over_x = [rcopy(pair, pair, send, recv + 1, along("x", k)) for k in (1, 3, 2)]
            self.give = rcopy(agb.at[kw, c], agb.at[kw, c], send + 3, recv + 3, sibling)

        def join(self, mine_by, theirs_by):
            for one in self.lanes:
                one.join(mine_by, theirs_by)

        def step(self, n):
            kw = self.kw
            if n == 0:
                for one in self.lanes:
                    one.swap.start()
            elif n == 2:
                for one in self.lanes:
                    one.middle()
            elif n == 3:
                for one in self.lanes:
                    one.end_first()
            elif n == 4:
                for one in self.lanes:
                    one.end_second()
            elif n == 5:
                for one in self.lanes:
                    one.end_third()
                self.over_y.start()
            elif n == 6:
                got(agb.at[kw, c, 0], self.sems + 1)
                start(self.over_x)
            elif n == 7:
                got(agb.at[kw, c, 0:6], self.sems + 2)
                self.give.start()
            elif n == 8:
                got(agb.at[kw, 1 - c], self.sems + 4)
                sent(agb.at[kw, c, 0:7], self.sems)
                sent(agb.at[kw, c], self.sems + 3)
                for row in range(3):
                    tiles = []
                    for t in range(5):
                        s = row * 5 + t
                        tiles.append(agb[kw, s % 2, s // 2].astype(F32))
                    rows = jnp.concatenate(tiles, axis=0)
                    wout[3 * row + kw] = jnp.where(c == 0, rows[0:40], rows[40:80]) * SCALE

    parts = [Reduce(kw) for kw in range(3)]
    weight_part(0)
    parts[0].step(0)

    ex_l1.wait()
    tweight = 1.0 / (1.0 + jnp.full((8, 128), ts[0], jnp.int32).astype(F32) / 250.0)
    pano = tweight * ex_l1.total() / (ROWS * COLS * NLON * C)
    lane = lax.broadcasted_iota(jnp.int32, (8, 128), 1)
    row8 = lax.broadcasted_iota(jnp.int32, (8, 128), 0)
    member = jnp.where(lane == jnp.full((8, 128), bk[0], jnp.int32), 1.0, 0.0).astype(F32)
    l2[dp] = jnp.where(
        row8 == 0, member * pano, jnp.where(row8 == 1, member, jnp.where(row8 == 2, tweight, 0.0))
    )
    ex_l2 = Exchange(l2, dp, NDP, to_dp)
    ex_l2.send()
    weight_part(1)
    parts[1].step(0)
    ex_l2.wait()
    sums2 = ex_l2.total()
    denom = jnp.maximum(sums2[1:2], 1.0)
    bucket_mean = sums2[0:1] / denom
    lane1 = lane[0:1]
    limit = jnp.zeros((1, 128), jnp.int32)
    for b in range(4):
        limit = jnp.where(lane1 == b, jnp.full((1, 128), clip[b], jnp.int32), limit)
    limit = limit.astype(F32) / 1000.0
    losses = jnp.minimum(bucket_mean, limit)
    passing = jnp.where((bucket_mean < limit) & (lane1 < 4), 1.0, 0.0)

    def coef_of(tile):
        picked = jnp.sum(tile[1:2] * passing / denom, axis=1, keepdims=True)
        return tile[2:3, 0:1] * picked

    coef, sib_coef = coef_of(l2[dp]), coef_of(l2[dp + 1 - 2 * c])

    parts[0].join(coef, sib_coef)
    weight_part(2)
    parts[2].step(0)
    parts[1].join(coef, sib_coef)
    parts[0].step(2)

    sent(es, esem)
    got(er, esem + 1)

    @pl.loop(0, ROWS)
    def _(r):
        put_sides(e3, r + 2, e3[at_row(r + 2), C : 2 * C].astype(F32), er, r)

    parts[1].step(2)
    parts[2].join(coef, sib_coef)
    parts[0].step(3)
    back(0)
    parts[2].step(2)
    parts[1].step(3)
    parts[0].step(4)
    back(1)
    parts[2].step(3)
    parts[1].step(4)
    parts[0].step(5)
    back(2)
    parts[2].step(4)
    parts[1].step(5)
    parts[0].step(6)
    back(3)
    parts[2].step(5)
    parts[1].step(6)
    parts[0].step(7)

    def through(r, carry):
        a, b = carry
        normed = (lat[r].astype(F32) - mean) * rstd
        dpre = dacc[at_row(r + 2), :] * coef * dsilu[r]
        dacc[at_row(r + 2), :] = dpre
        return (
            a + jnp.sum(dpre, axis=0, keepdims=True),
            b + jnp.sum(dpre * normed, axis=0, keepdims=True),
        )

    s1, s2 = lax.fori_loop(0, ROWS, through, (zero, zero))
    g1[lon] = jnp.where(
        sub == 0, s1, jnp.where(sub == 1, s2, jnp.where(sub == 2, err_sum * coef, 0.0))
    )
    ex_g1 = Exchange(g1, lon, NLON, to_lon)
    ex_g1.send()
    parts[2].step(6)
    parts[1].step(7)
    parts[0].step(8)
    ex_g1.wait()
    pan = ex_g1.total()
    g2[dp] = pan
    ex_g2 = Exchange(g2, dp, NDP, to_dp)
    ex_g2.send()
    means = group_sum(pan * gain) / COUNT
    m1, m2 = means[0:1], means[1:2]

    def input_gradient(r):
        normed = (lat[r].astype(F32) - mean) * rstd
        dn = dacc[at_row(r + 2), :] * gain
        g = e3[at_row(r + 2), C : 2 * C].astype(F32) * coef
        igrad[r] = (g + rstd * (dn - m1 - normed * m2)).astype(BF16)

    pl.loop(0, 8)(input_gradient)
    parts[2].step(7)
    parts[1].step(8)
    pl.loop(8, ROWS)(input_gradient)
    ex_g2.wait()
    totals = ex_g2.total() * SCALE
    wide = jnp.concatenate([losses] + [jnp.zeros_like(losses)] * 4, axis=1)
    sg_out[...] = jnp.where(sub == 3, wide, totals)
    parts[2].step(8)
    reduce_sends_done()
    assert alloc.used <= NUM_SEMS, alloc.used


def reduce_shapes(lanes):
    tile = (16, lanes)
    return [
        (3, 2, 4, 4, 4, *tile),
        (3, 4, 4, 4, *tile),
        (3, 2, 4, *tile),
        (3, 2, 4, *tile),
        (3, 4, 4, *tile),
        (3, 4, 4, *tile),
        (3, 4, 4, *tile),
        (3, 3, 4, *tile),
        (3, 7, *tile),
    ]


def shards(
    latents, target, norm_gain, norm_shift, conv_weight, conv_bias, timesteps, buckets, clip_milli
):
    win = jnp.transpose(conv_weight, (1, 2, 0, 3)).reshape(9, 40, C)
    vmem = pl.BlockSpec(memory_space=pltpu.VMEM)
    smem = pl.BlockSpec(memory_space=pltpu.SMEM)
    outs = pl.pallas_call(
        kernel,
        out_shape=(
            pltpu.VMEM((ROWS, COLS, C), BF16),
            pltpu.VMEM((9, 40, C), F32),
            pltpu.VMEM((8, C), F32),
        ),
        in_specs=[smem] * 3 + [pl.BlockSpec(memory_space=pl.ANY)] * 3 + [vmem] * 3,
        out_specs=(vmem,) * 3,
        scratch_shapes=[
            pltpu.VMEM((ROWS, COLS, C), BF16),
            pltpu.VMEM((ROWS, COLS, C), BF16),
            pltpu.VMEM((9, 40, C), BF16),
            pltpu.VMEM((ROWS, COLS, C), F32),
            pltpu.VMEM((5, 40, C), BF16),
            pltpu.VMEM((9, C, C), BF16),
            pltpu.VMEM((PADPIX, 3 * C), BF16),
            pltpu.VMEM((3 * C, PADPIX), BF16),
            pltpu.VMEM((PIX, C), F32),
            pltpu.VMEM((PIX + 4 * COLS, C), F32),
            pltpu.VMEM((PADPIX + 2 * COLS, 3 * C), BF16),
            pltpu.VMEM((3, 2, NLON, 16, C), BF16),
            pltpu.VMEM((C, C), BF16),
            pltpu.VMEM((NLON, 8, C), F32),
            pltpu.VMEM((2, ROWS, C), F32),
            pltpu.VMEM((2, ROWS, C), F32),
            pltpu.VMEM((2, ROWS, C), F32),
            pltpu.VMEM((2, ROWS, C), F32),
            pltpu.VMEM((NLON, 8, 128), F32),
            pltpu.VMEM((NDP, 8, 128), F32),
            pltpu.VMEM((NLON, 8, C), F32),
            pltpu.VMEM((NDP, 8, C), F32),
            pltpu.SemaphoreType.DMA((NUM_SEMS,)),
        ]
        + [pltpu.VMEM(shape, BF16) for first, end in LANES for shape in reduce_shapes(end - first)],
        compiler_params=pltpu.CompilerParams(
            collective_id=0, has_side_effects=True, vmem_limit_bytes=60 * 1024 * 1024
        ),
        cost_estimate=pl.CostEstimate(
            flops=3 * 2 * PIX * 9 * C * C, bytes_accessed=8 * 1024 * 1024, transcendentals=2 * PIX * C
        ),
    )(
        timesteps, buckets, clip_milli, latents[0], target[0], win,
        norm_gain, norm_shift, conv_bias,
    )
    igrad, wout, sg = outs
    weight_grad = jnp.transpose(wout.reshape(3, 3, 40, C), (2, 0, 1, 3))
    return sg[3, :4], igrad[None], weight_grad, sg[1], sg[0], sg[2]


def solution(mesh):
    placed = (
        P("dp", None, "lon", None),
        P("dp", None, "lon", None),
        P(),
        P(),
        P("dp", None, None, None),
        P(),
        P("dp"),
        P("dp"),
        P(),
    )
    return jax.shard_map(
        shards,
        mesh=mesh,
        in_specs=placed,
        out_specs=(P(), P("dp", None, "lon", None), P("dp", None, None, None), P(), P(), P()),
        check_vma=False,
    )
```

```python
import functools

import jax
import jax.numpy as jnp
from jax import lax
from jax.experimental import pallas as pl
from jax.experimental.pallas import tpu as pltpu
from jax.sharding import PartitionSpec as P

F32 = jnp.float32
BF16 = jnp.bfloat16
ROWS, COLS, C = 16, 64, 640
PIX = ROWS * COLS
PADPIX = PIX + 2 * COLS
NLON, NDP = 8, 16
COUNT = ROWS * COLS * NLON * (C // 32)
SCALE = 1.0 / (ROWS * COLS)
ORDERS = ("xyz", "yzx", "zxy")
LANES = ((0, 256), (256, 512), (512, 640))
NT = (((1,), (1,)), ((), ()))


class Sems:
    def __init__(self):
        self.used = 0

    def take(self, n=1):
        first = self.used
        self.used += n
        return first


NUM_SEMS = 200


def kernel(
    ts, bk, clip, lat_in, tgt_in, win_in, gain_r, shift_r, bias_r,
    igrad, wout, sg_out,
    lat, tgt, win, dsilu, sibw, wg_all, x3, x3t, acc, dacc, e3, agb,
    mask, stat, hs, hr, es, er, l1, l2, g1, g2, sem, *red,
):
    lon, dp = lax.axis_index("lon"), lax.axis_index("dp")
    x, yhi = lon // 2, lon % 2
    z, ylo, c = dp // 4, (dp // 2) % 2, dp % 2
    y = yhi * 2 + ylo
    here = {"x": x, "y": y, "z": z}
    alloc = Sems()

    def dev(xx, yy, zz, cc):
        return {"lon": xx * 2 + yy // 2, "dp": (zz * 2 + yy % 2) * 2 + cc}

    def along(axis, step):
        at = dict(here)
        at[axis] = (at[axis] + step) % 4
        return dev(at["x"], at["y"], at["z"], c)

    sibling = dev(x, y, z, 1 - c)

    def rcopy(src, dst, send, recv, to):
        return pltpu.make_async_remote_copy(
            src_ref=src, dst_ref=dst, send_sem=sem.at[send], recv_sem=sem.at[recv],
            device_id=to, device_id_type=pl.DeviceIdType.MESH,
        )

    def got(ref, number):
        rcopy(ref, ref, number, number, sibling).wait_recv()

    def sent(ref, number):
        rcopy(ref, ref, number, number, sibling).wait_send()

    def to_lon(i):
        return {"lon": i, "dp": dp}

    def to_dp(i):
        return {"lon": lon, "dp": i}

    loads = [
        pltpu.make_async_copy(src, dst, sem.at[alloc.take()])
        for src, dst in ((win_in, win), (lat_in, lat), (tgt_in, tgt))
    ]
    for one in loads:
        one.start()

    bar = pltpu.get_barrier_semaphore()

    def greet(to):
        pl.semaphore_signal(bar, inc=1, device_id=to, device_id_type=pl.DeviceIdType.MESH)

    @pl.loop(1, NLON)
    def _(k):
        greet(to_lon((lon + k) % NLON))

    @pl.loop(1, NDP)
    def _(k):
        greet(to_dp((dp + k) % NDP))

    far = (y + 3 + 2 * ylo) % 4
    greet(dev(x, far, z, c))

    class Exchange:
        def __init__(self, rx, me, size, to):
            self.rx, self.me, self.size, self.to = rx, me, size, to
            self.base = alloc.take(2)

        def send(self):
            @pl.loop(1, self.size)
            def _(k):
                slot = self.rx.at[self.me]
                rcopy(slot, slot, self.base, self.base + 1, self.to((self.me + k) % self.size)).start()

        def wait(self):
            others = self.rx.at[0 : self.size - 1]
            sent(others, self.base)
            got(others, self.base + 1)

        def total(self):
            return functools.reduce(lambda a, b: a + b, [self.rx[i] for i in range(self.size)])

    def at_row(r):
        return pl.ds(pl.multiple_of(r * COLS, COLS), COLS)

    def sums(r, tot):
        v = lat[r].astype(F32)
        hs[0, pl.ds(r, 1), :] = v[COLS - 1 : COLS]
        hs[1, pl.ds(r, 1), :] = v[0:1]
        return tot + jnp.sum(v, axis=0, keepdims=True)

    loads[1].wait()
    chan = lax.fori_loop(0, ROWS, sums, jnp.zeros((1, C), F32))
    gi = jnp.floor((lax.broadcasted_iota(jnp.int32, (C, C), 0).astype(F32) + 0.5) * 0.05)
    gj = jnp.floor((lax.broadcasted_iota(jnp.int32, (C, C), 1).astype(F32) + 0.5) * 0.05)
    mask[...] = jnp.where(gi == gj, 1.0, 0.0).astype(BF16)

    def group_sum(v):
        top = v.astype(BF16)
        rest = v - top.astype(F32)
        mid = rest.astype(BF16)
        low = (rest - mid.astype(F32)).astype(BF16)
        zeros = jnp.zeros((8, C), F32)
        terms = jnp.concatenate(
            [top.astype(F32), mid.astype(F32), low.astype(F32), zeros], axis=0
        ).astype(BF16)
        out = jnp.dot(terms, mask[...], preferred_element_type=F32)
        return out[0:8] + out[8:16] + out[16:24]

    sub = lax.broadcasted_iota(jnp.int32, (8, C), 0)
    pl.semaphore_wait(bar, NLON - 1 + NDP - 1 + 1)
    loads[0].wait()

    swaps = alloc.take(6)

    def swap_tap(j):
        return rcopy(win.at[2 * j + 1 - c], sibw.at[j], swaps, swaps + 1 + j, sibling)

    for j in range(4):
        swap_tap(j).start()
    pl.when(c == 1)(lambda: swap_tap(4).start())

    right, left = to_lon((lon + 1) % NLON), to_lon((lon + NLON - 1) % NLON)
    hsem = alloc.take(2)
    rcopy(hs.at[0], hr.at[0], hsem, hsem + 1, right).start()
    rcopy(hs.at[1], hr.at[1], hsem, hsem + 1, left).start()

    local_mean = group_sum(jnp.where(sub == 0, chan, 0.0))[0:1] / (PIX * 20)

    odd = x % 2
    own_d = z * 2 + ylo

    def jyz(slot, core):
        return (odd, 2 + (1 - core) * odd, 4 - core)[slot]

    def jx(slot):
        return (1 - odd, 3 - odd)[slot]

    def assemble(j):
        got(sibw.at[j], swaps + 1 + j)
        a = win[2 * j + c].astype(F32)
        b = sibw[j].astype(F32)
        first = jnp.where(c == 0, a, b)
        second = jnp.where(c == 0, b, a)
        rows = pl.ds(pl.multiple_of(own_d * 80, 16), 80)
        wg_all[2 * j + c, rows, :] = jnp.concatenate([first, second], axis=0).astype(BF16)

    LO, HI = (0, 48), (48, 32)

    def blk(j, zz, parity, part=(0, 80)):
        row = pl.multiple_of((zz * 2 + parity) * 80 + part[0], 16)
        return wg_all.at[2 * j + c, pl.ds(row, part[1]), :]

    zl, zr, zo = (z + 3) % 4, (z + 1) % 4, (z + 2) % 4
    gz = [alloc.take(3) for _ in range(3)]
    gy = [alloc.take(5) for _ in range(3)]
    gx = [alloc.take(8) for _ in range(2)]
    gd = [alloc.take(2) for _ in range(5)]

    def rows_of(n):
        return wg_all.at[0, 0:n]

    def two_ways(axis, j, zz, parity, send, recv, slot):
        plus, minus = (LO, HI) if slot % 2 == 0 else (HI, LO)
        one, two = blk(j, zz, parity, plus), blk(j, zz, parity, minus)
        return (
            rcopy(one, one, send, recv, along(axis, 1)),
            rcopy(two, two, send, recv, along(axis, 3)),
        )

    def y_copies(s, k, zz):
        return two_ways("y", jyz(s, c), zz, ylo, gy[s], gy[s] + 1 + k, s)

    def x_copies(s, k, zz, parity):
        return two_ways("x", jyz(s, c), zz, parity, gx[s], gx[s] + k, s)

    def z1(s):
        block = blk(jyz(s, c), z, ylo)
        return [rcopy(block, block, gz[s], gz[s] + 1, along("z", k)) for k in (1, 3)]

    def z2(s):
        j = jyz(s, c)
        plus, minus = (LO, HI) if s % 2 == 0 else (HI, LO)
        one, two = blk(j, zl, ylo, plus), blk(j, zr, ylo, minus)
        return (
            rcopy(one, one, gz[s], gz[s] + 2, along("z", 1)),
            rcopy(two, two, gz[s], gz[s] + 2, along("z", 3)),
        )

    def start(copies):
        for one in copies:
            one.start()

    AROUND = (z, zl, zr, zo)

    def over_x(s, body):
        if s == 0:
            body()
        elif s == 1:
            pl.when(c == 0)(body)

    BLOCKS = ((z, ylo), (zl, ylo), (zr, ylo), (zo, ylo), *((q, 1 - ylo) for q in AROUND))

    def across(n, j, core, k):
        zz, parity = BLOCKS[k]
        row = pl.multiple_of((zz * 2 + parity) * 80, 16)
        block = wg_all.at[2 * j + core, pl.ds(row, 80), :]
        return rcopy(block, block, gd[n], gd[n] + 1, sibling)

    def give(n, j, ks):
        start([across(n, j, c, k) for k in ks])

    def wave1(s):
        assemble(jyz(s, c))
        start(z1(s))
        start(y_copies(s, 0, z))
        give(s, jyz(s, c), (0,))

    def x_send(s, ks):
        def body():
            for k in ks:
                start(x_copies(s, k, *BLOCKS[k]))

        over_x(s, body)

    def wave2(s):
        got(rows_of(160), gz[s] + 1)
        start(z2(s))
        start(y_copies(s, 1, zl))
        start(y_copies(s, 2, zr))
        x_send(s, (1, 2))
        give(s, jyz(s, c), (1, 2))

    def wave3(s):
        got(rows_of(80), gz[s] + 2)
        start(y_copies(s, 3, zo))
        x_send(s, (3,))
        give(s, jyz(s, c), (3,))

    def wave4(s):
        for k in range(4):
            got(rows_of(80), gy[s] + 1 + k)
            x_send(s, (4 + k,))
            give(s, jyz(s, c), (4 + k,))

    def own_x(s):
        def body():
            assemble(jx(s))
            give(3 + s, jx(s), (0,))

        over_x(s, body)

    def wave_x(s, ks):
        def body():
            for k in ks:
                got(rows_of(80), gx[s] + k)
                give(3 + s, jx(s), (k,))

        over_x(s, body)

    def from_sibling(s):
        got(rows_of(C), gd[s] + 1)

    def from_sibling_x(s):
        def body():
            got(rows_of(C), gd[3 + s] + 1)

        if s == 0:
            body()
        else:
            pl.when(c == 1)(body)

    def sends_done():
        pl.when(c == 0)(lambda: sent(sibw.at[0:4], swaps))
        pl.when(c == 1)(lambda: sent(sibw, swaps))
        for s in range(3):
            sent(rows_of(240), gz[s])
            sent(rows_of(320), gy[s])
            sent(rows_of(C), gd[s])
        for s in range(2):

            def body(s=s):
                sent(rows_of(560), gx[s])
                sent(rows_of(C), gd[3 + s])

            over_x(s, body)

    wave1(0)
    wave1(1)
    dacc[...] = jnp.zeros((PIX + 4 * COLS, C), F32)
    own_x(0)
    own_x(1)

    def squares(r, tot):
        d = lat[r].astype(F32) - local_mean
        return tot + jnp.sum(d * d, axis=0, keepdims=True)

    chan2 = lax.fori_loop(0, ROWS, squares, jnp.zeros((1, C), F32))
    m2loc = group_sum(jnp.where(sub == 0, chan2, 0.0))[0:1]
    stat[lon] = jnp.where(sub == 0, local_mean, jnp.where(sub == 1, m2loc, 0.0))
    ex_stat = Exchange(stat, lon, NLON, to_lon)
    ex_stat.send()

    wave2(0)
    wave1(2)
    ex_stat.wait()
    sent(hs, hsem)
    got(hr, hsem + 1)
    stats = [stat[i] for i in range(NLON)]
    mean = functools.reduce(lambda a, b: a + b, [s[0:1] for s in stats]) / NLON
    spread = functools.reduce(lambda a, b: a + b, [(s[0:1] - mean) * (s[0:1] - mean) for s in stats])
    within = functools.reduce(lambda a, b: a + b, [s[1:2] for s in stats])
    var = (within + (PIX * 20) * spread) / COUNT
    rstd = lax.rsqrt(var + 1e-05)
    gain, shift = gain_r[...].reshape(1, C), shift_r[...].reshape(1, C)

    def pre_of(v):
        normed = (v - mean) * rstd
        return normed, normed * gain + shift

    def silu(v):
        _, pre = pre_of(v)
        return pre * jax.nn.sigmoid(pre)

    hr[0] = silu(hr[0])
    hr[1] = silu(hr[1])
    edge = lax.broadcasted_iota(jnp.int32, (COLS, C), 0)

    def put_sides(dst, to, a, halo, r):
        before = jnp.where(edge == 0, halo[0, pl.ds(r, 1), :], pltpu.roll(a, 1, 0))
        after = jnp.where(edge == COLS - 1, halo[1, pl.ds(r, 1), :], pltpu.roll(a, COLS - 1, 0))
        dst[at_row(to), 0:C] = before.astype(BF16)
        dst[at_row(to), 2 * C : 3 * C] = after.astype(BF16)

    zero_row = jnp.zeros((COLS, 3 * C), BF16)
    for buf, ends in ((x3, (0, PADPIX - COLS)), (e3, (0, COLS, PADPIX, PADPIX + COLS))):
        for low in ends:
            buf[low : low + COLS, :] = zero_row

    def activate(first, end):
        @pl.loop(first, end)
        def _(r):
            _normed, pre = pre_of(lat[r].astype(F32))
            sig = jax.nn.sigmoid(pre)
            a = pre * sig
            dsilu[r] = sig * (1.0 + pre * (1.0 - sig))
            x3[at_row(r + 1), C : 2 * C] = a.astype(BF16)
            put_sides(x3, r + 1, a, hr, r)

    unit = jnp.where(
        lax.broadcasted_iota(jnp.int32, (256, 256), 0) == lax.broadcasted_iota(jnp.int32, (256, 256), 1),
        1.0, 0.0,
    ).astype(BF16)

    def turn(first, end):
        for j in range(first, end):
            low, high = j * 256, min(j * 256 + 256, 3 * C)
            n = high - low
            x3t[low:high, :] = lax.dot_general(
                unit[:n, :n], x3[:, low:high], NT, preferred_element_type=F32
            ).astype(BF16)

    def forward(tap, count, fresh=False):
        fields = []
        for n in range(count):
            kh, kw = (tap + n) // 3, (tap + n) % 3
            rows = pl.ds(pl.multiple_of(kh * COLS, COLS), PIX)
            fields.append(x3[rows, pl.ds(pl.multiple_of(kw * C, 128), C)])
        w = wg_all[pl.ds(tap, count)].reshape(count * C, C)
        part = jnp.dot(jnp.concatenate(fields, axis=1), w, preferred_element_type=F32)
        acc[...] = part if fresh else acc[...] + part

    activate(0, 8)
    wave2(1)
    wave3(0)
    activate(8, ROWS)
    wave3(1)
    wave4(0)
    wave_x(0, (1, 2))
    turn(0, 3)
    wave2(2)
    wave_x(0, (3,))
    from_sibling(0)
    forward(2 * odd, 2, True)
    wave4(1)
    wave_x(1, (1, 2, 3))
    wave3(2)
    wave_x(0, (4, 5, 6, 7))
    turn(3, 8)
    from_sibling_x(0)
    forward(2 - 2 * odd, 2)
    wave_x(1, (4, 5, 6, 7))
    wave4(2)
    from_sibling(1)
    from_sibling_x(1)
    forward(4, 3)
    from_sibling(2)
    forward(7, 2)
    sends_done()

    loads[2].wait()
    bias = bias_r[...].reshape(1, C)

    def error(r, carry):
        sq, tot = carry
        v = acc[at_row(r), :] + bias + lat[r].astype(F32) - tgt[r].astype(F32)
        e3[at_row(r + 2), C : 2 * C] = v.astype(BF16)
        es[0, pl.ds(r, 1), :] = v[COLS - 1 : COLS]
        es[1, pl.ds(r, 1), :] = v[0:1]
        return sq + jnp.sum(v * v, axis=0, keepdims=True), tot + jnp.sum(v, axis=0, keepdims=True)

    zero = jnp.zeros((1, C), F32)
    sq, err_sum = lax.fori_loop(0, ROWS, error, (zero, zero))
    l1[lon] = jnp.broadcast_to(jnp.sum(sq, axis=1, keepdims=True), (8, 128))
    ex_l1 = Exchange(l1, lon, NLON, to_lon)
    ex_l1.send()
    esem = alloc.take(2)
    rcopy(es.at[0], er.at[0], esem, esem + 1, right).start()
    rcopy(es.at[1], er.at[1], esem, esem + 1, left).start()

    def back(m):
        rows = PADPIX // 2
        low = m * rows
        w = jnp.concatenate(
            [
                jnp.concatenate([wg_all[3 * kh + kw] for kw in (2, 1, 0)], axis=1)
                for kh in range(3)
            ],
            axis=0,
        )
        part = lax.dot_general(
            e3[COLS + low : COLS + low + rows, :], w, NT, preferred_element_type=F32
        )
        for kh in range(3):
            out = slice(low + kh * COLS, low + kh * COLS + rows)
            dacc[out, :] = dacc[out, :] + part[:, kh * C : (kh + 1) * C]

    NRED = 9
    groups = [red[NRED * g : NRED * g + NRED] for g in range(3)]

    def order(kw, g):
        return ORDERS[(kw + g) % 3]

    def place(kw, g, core, lon_to, d):
        at = {"x": lon_to // 2, "y": (lon_to % 2) * 2 + d % 2, "z": d // 2}
        a1, a2, a3 = order(kw, g)
        return kw, core, at[a1], at[a2], at[a3]

    def weight_part(kw):
        for g in range(3):
            first, end = LANES[g]
            for d in range(8):
                groups[g][0][place(kw, g, 1, 7, d)] = jnp.zeros((16, end - first), BF16)
        err = jnp.concatenate(
            [e3[(2 - kh) * COLS : (2 - kh) * COLS + PADPIX, C : 2 * C] for kh in range(3)], axis=1
        )
        res = jnp.dot(x3t[kw * C : (kw + 1) * C, :], err, preferred_element_type=F32)
        res = res.astype(BF16)
        for d in range(8):
            for t in range(5):
                low = d * 80 + t * 16
                for kh in range(3):
                    s = kh * 5 + t
                    for g in range(3):
                        first, end = LANES[g]
                        groups[g][0][place(kw, g, s % 2, s // 2, d)] = res[
                            low : low + 16, kh * C + first : kh * C + end
                        ]

    def add(out, terms):
        val = functools.reduce(lambda a, b: a + b, [t[...].astype(F32) for t in terms])
        out[...] = val.astype(out.dtype)

    send_sems = [alloc.take(4) for _ in range(3)]

    def reduce_sends_done():
        for g in range(3):
            rxs, r2rx, r3 = groups[g][1], groups[g][7], groups[g][8]
            sent(rxs, send_sems[g])
            sent(rxs.at[:, 0:3], send_sems[g] + 1)
            sent(r2rx, send_sems[g] + 2)
            sent(r3.at[:, 4:7], send_sems[g] + 3)

    class Lanes:
        def __init__(self, kw, g):
            wg, rxs, ra, rb, rc, rd, r2, r2rx, r3 = groups[g]
            self.r3rx = r3.at[kw, 4:7]
            self.kw, self.g, self.axes = kw, g, order(kw, g)
            self.rxs, self.r2, self.r2rx, self.r3 = rxs.at[kw], r2.at[kw], r2rx.at[kw], r3.at[kw]
            self.ra, self.rb, self.rc, self.rd = ra.at[kw], rb.at[kw], rc.at[kw], rd.at[kw]
            self.buf = wg.at[kw, c]
            send, self.recv = send_sems[g], alloc.take(5)
            self.two = wg.at[kw, 0, 0:2]
            self.swap = rcopy(wg.at[kw, 1 - c], self.rxs, send, self.recv, sibling)
            axis = self.axes[0]
            self.me = [here[a] for a in self.axes]
            far_, up, down = ((self.me[0] + k) % 4 for k in (2, 1, 3))
            self.up, self.down = up, down
            self.first = [
                rcopy(src, dst, send + 1, self.recv + n, along(axis, to))
                for src, dst, n, to in (
                    (self.buf.at[far_, 0:2], self.ra, 1, 1),
                    (self.buf.at[far_, 2:4], self.rb, 1, 3),
                    (self.buf.at[up], self.rc, 2, 1),
                    (self.buf.at[down], self.rd, 2, 3),
                )
            ]
            self.second = self.direct(1, self.r2, self.r2rx, send + 2, self.recv + 3)
            self.third = self.direct(2, self.r3, self.r3rx, send + 3, self.recv + 4)

        def direct(self, stage, buf, rx, send, recv):
            return [
                rcopy(
                    buf.at[(self.me[stage] + k) % 4], rx.at[k - 1],
                    send, recv, along(self.axes[stage], k),
                )
                for k in (1, 3, 2)
            ]

        def join(self, mine_by, theirs_by):
            got(self.rxs, self.recv)

            @pl.loop(0, 4)
            def _(i):
                own = self.buf[i].astype(F32) * mine_by
                self.buf[i] = (own + self.rxs[i].astype(F32) * theirs_by).astype(BF16)

            start(self.first[:2])

        def middle(self):
            got(self.rc, self.recv + 1)
            add(self.buf.at[self.up, 0:2], [self.buf.at[self.up, 0:2], self.ra])
            add(self.buf.at[self.down, 2:4], [self.buf.at[self.down, 2:4], self.rb])
            start(self.first[2:])

        def end_first(self):
            got(self.two, self.recv + 2)
            add(self.r2, [self.buf.at[self.me[0]], self.rc, self.rd])
            start(self.second)

        def end_second(self):
            got(self.r2rx, self.recv + 3)
            add(self.r3.at[0:4], [self.r2.at[self.me[1]]] + [self.r2rx.at[k] for k in range(3)])
            start(self.third)

        def end_third(self):
            got(self.r3rx, self.recv + 4)
            val = self.r3[self.me[2]].astype(F32)
            for k in range(3):
                val = val + self.r3[4 + k].astype(F32)
            first, end = LANES[self.g]
            agb[self.kw, c, lon, :, first:end] = val.astype(BF16)

    class Reduce:
        def __init__(self, kw):
            self.kw = kw
            self.lanes = [Lanes(kw, g) for g in range(3)]
            slot = agb.at[kw, c, lon]
            self.sems = alloc.take(5)
            send, recv = self.sems, self.sems + 1
            self.over_y = rcopy(slot, slot, send, recv, dev(x, (y + 2) % 4, z, c))
            pair = agb.at[kw, c, pl.ds(2 * x, 2)]
            self.over_x = [rcopy(pair, pair, send, recv + 1, along("x", k)) for k in (1, 3, 2)]
            self.give = rcopy(agb.at[kw, c], agb.at[kw, c], send + 3, recv + 3, sibling)

        def join(self, mine_by, theirs_by):
            for one in self.lanes:
                one.join(mine_by, theirs_by)

        def step(self, n):
            kw = self.kw
            if n == 0:
                for one in self.lanes:
                    one.swap.start()
            elif n == 2:
                for one in self.lanes:
                    one.middle()
            elif n == 3:
                for one in self.lanes:
                    one.end_first()
            elif n == 4:
                for one in self.lanes:
                    one.end_second()
            elif n == 5:
                for one in self.lanes:
                    one.end_third()
                self.over_y.start()
            elif n == 6:
                got(agb.at[kw, c, 0], self.sems + 1)
                start(self.over_x)
            elif n == 7:
                got(agb.at[kw, c, 0:6], self.sems + 2)
                self.give.start()
            elif n == 8:
                got(agb.at[kw, 1 - c], self.sems + 4)
                sent(agb.at[kw, c, 0:7], self.sems)
                sent(agb.at[kw, c], self.sems + 3)
                for row in range(3):
                    tiles = []
                    for t in range(5):
                        s = row * 5 + t
                        tiles.append(agb[kw, s % 2, s // 2].astype(F32))
                    rows = jnp.concatenate(tiles, axis=0)
                    wout[3 * row + kw] = jnp.where(c == 0, rows[0:40], rows[40:80]) * SCALE

    parts = [Reduce(kw) for kw in range(3)]
    weight_part(0)
    parts[0].step(0)

    ex_l1.wait()
    tweight = 1.0 / (1.0 + jnp.full((8, 128), ts[0], jnp.int32).astype(F32) / 250.0)
    pano = tweight * ex_l1.total() / (ROWS * COLS * NLON * C)
    lane = lax.broadcasted_iota(jnp.int32, (8, 128), 1)
    row8 = lax.broadcasted_iota(jnp.int32, (8, 128), 0)
    member = jnp.where(lane == jnp.full((8, 128), bk[0], jnp.int32), 1.0, 0.0).astype(F32)
    l2[dp] = jnp.where(
        row8 == 0, member * pano, jnp.where(row8 == 1, member, jnp.where(row8 == 2, tweight, 0.0))
    )
    ex_l2 = Exchange(l2, dp, NDP, to_dp)
    ex_l2.send()
    weight_part(1)
    parts[1].step(0)
    ex_l2.wait()
    sums2 = ex_l2.total()
    denom = jnp.maximum(sums2[1:2], 1.0)
    bucket_mean = sums2[0:1] / denom
    lane1 = lane[0:1]
    limit = jnp.zeros((1, 128), jnp.int32)
    for b in range(4):
        limit = jnp.where(lane1 == b, jnp.full((1, 128), clip[b], jnp.int32), limit)
    limit = limit.astype(F32) / 1000.0
    losses = jnp.minimum(bucket_mean, limit)
    passing = jnp.where((bucket_mean < limit) & (lane1 < 4), 1.0, 0.0)

    def coef_of(tile):
        picked = jnp.sum(tile[1:2] * passing / denom, axis=1, keepdims=True)
        return tile[2:3, 0:1] * picked

    coef, sib_coef = coef_of(l2[dp]), coef_of(l2[dp + 1 - 2 * c])

    parts[0].join(coef, sib_coef)
    weight_part(2)
    parts[2].step(0)
    parts[1].join(coef, sib_coef)
    parts[0].step(2)

    sent(es, esem)
    got(er, esem + 1)
    parts[2].join(coef, sib_coef)

    @pl.loop(0, ROWS)
    def _(r):
        put_sides(e3, r + 2, e3[at_row(r + 2), C : 2 * C].astype(F32), er, r)

    parts[1].step(2)
    parts[0].step(3)
    parts[2].step(2)
    back(0)
    parts[1].step(3)
    parts[0].step(4)
    parts[2].step(3)
    back(1)
    parts[1].step(4)
    parts[0].step(5)
    parts[2].step(4)

    def through(r, carry):
        a, b = carry
        normed = (lat[r].astype(F32) - mean) * rstd
        dpre = dacc[at_row(r + 2), :] * coef * dsilu[r]
        dacc[at_row(r + 2), :] = dpre
        return (
            a + jnp.sum(dpre, axis=0, keepdims=True),
            b + jnp.sum(dpre * normed, axis=0, keepdims=True),
        )

    s1, s2 = lax.fori_loop(0, ROWS, through, (zero, zero))
    g1[lon] = jnp.where(
        sub == 0, s1, jnp.where(sub == 1, s2, jnp.where(sub == 2, err_sum * coef, 0.0))
    )
    ex_g1 = Exchange(g1, lon, NLON, to_lon)
    ex_g1.send()
    parts[1].step(5)
    parts[0].step(6)
    parts[2].step(5)
    ex_g1.wait()
    pan = ex_g1.total()
    g2[dp] = pan
    ex_g2 = Exchange(g2, dp, NDP, to_dp)
    ex_g2.send()
    means = group_sum(pan * gain) / COUNT
    m1, m2 = means[0:1], means[1:2]

    def input_gradient(r):
        normed = (lat[r].astype(F32) - mean) * rstd
        dn = dacc[at_row(r + 2), :] * gain
        g = e3[at_row(r + 2), C : 2 * C].astype(F32) * coef
        igrad[r] = (g + rstd * (dn - m1 - normed * m2)).astype(BF16)

    pl.loop(0, 8)(input_gradient)
    parts[2].step(6)
    parts[1].step(6)
    parts[0].step(7)
    pl.loop(8, ROWS)(input_gradient)
    parts[2].step(7)
    parts[1].step(7)
    parts[0].step(8)
    ex_g2.wait()
    totals = ex_g2.total() * SCALE
    wide = jnp.concatenate([losses] + [jnp.zeros_like(losses)] * 4, axis=1)
    sg_out[...] = jnp.where(sub == 3, wide, totals)
    parts[1].step(8)
    parts[2].step(8)
    reduce_sends_done()
    assert alloc.used <= NUM_SEMS, alloc.used


def reduce_shapes(lanes):
    tile = (16, lanes)
    return [
        (3, 2, 4, 4, 4, *tile),
        (3, 4, 4, 4, *tile),
        (3, 2, 4, *tile),
        (3, 2, 4, *tile),
        (3, 4, 4, *tile),
        (3, 4, 4, *tile),
        (3, 4, 4, *tile),
        (3, 3, 4, *tile),
        (3, 7, *tile),
    ]


def shards(
    latents, target, norm_gain, norm_shift, conv_weight, conv_bias, timesteps, buckets, clip_milli
):
    win = jnp.transpose(conv_weight, (1, 2, 0, 3)).reshape(9, 40, C)
    vmem = pl.BlockSpec(memory_space=pltpu.VMEM)
    smem = pl.BlockSpec(memory_space=pltpu.SMEM)
    outs = pl.pallas_call(
        kernel,
        out_shape=(
            pltpu.VMEM((ROWS, COLS, C), BF16),
            pltpu.VMEM((9, 40, C), F32),
            pltpu.VMEM((8, C), F32),
        ),
        in_specs=[smem] * 3 + [pl.BlockSpec(memory_space=pl.ANY)] * 3 + [vmem] * 3,
        out_specs=(vmem,) * 3,
        scratch_shapes=[
            pltpu.VMEM((ROWS, COLS, C), BF16),
            pltpu.VMEM((ROWS, COLS, C), BF16),
            pltpu.VMEM((9, 40, C), BF16),
            pltpu.VMEM((ROWS, COLS, C), F32),
            pltpu.VMEM((5, 40, C), BF16),
            pltpu.VMEM((9, C, C), BF16),
            pltpu.VMEM((PADPIX, 3 * C), BF16),
            pltpu.VMEM((3 * C, PADPIX), BF16),
            pltpu.VMEM((PIX, C), F32),
            pltpu.VMEM((PIX + 4 * COLS, C), F32),
            pltpu.VMEM((PADPIX + 2 * COLS, 3 * C), BF16),
            pltpu.VMEM((3, 2, NLON, 16, C), BF16),
            pltpu.VMEM((C, C), BF16),
            pltpu.VMEM((NLON, 8, C), F32),
            pltpu.VMEM((2, ROWS, C), F32),
            pltpu.VMEM((2, ROWS, C), F32),
            pltpu.VMEM((2, ROWS, C), F32),
            pltpu.VMEM((2, ROWS, C), F32),
            pltpu.VMEM((NLON, 8, 128), F32),
            pltpu.VMEM((NDP, 8, 128), F32),
            pltpu.VMEM((NLON, 8, C), F32),
            pltpu.VMEM((NDP, 8, C), F32),
            pltpu.SemaphoreType.DMA((NUM_SEMS,)),
        ]
        + [pltpu.VMEM(shape, BF16) for first, end in LANES for shape in reduce_shapes(end - first)],
        compiler_params=pltpu.CompilerParams(
            collective_id=0, has_side_effects=True, vmem_limit_bytes=60 * 1024 * 1024
        ),
        cost_estimate=pl.CostEstimate(
            flops=3 * 2 * PIX * 9 * C * C, bytes_accessed=8 * 1024 * 1024, transcendentals=2 * PIX * C
        ),
    )(
        timesteps, buckets, clip_milli, latents[0], target[0], win,
        norm_gain, norm_shift, conv_bias,
    )
    igrad, wout, sg = outs
    weight_grad = jnp.transpose(wout.reshape(3, 3, 40, C), (2, 0, 1, 3))
    return sg[3, :4], igrad[None], weight_grad, sg[1], sg[0], sg[2]


def solution(mesh):
    placed = (
        P("dp", None, "lon", None),
        P("dp", None, "lon", None),
        P(),
        P(),
        P("dp", None, None, None),
        P(),
        P("dp"),
        P("dp"),
        P(),
    )
    return jax.shard_map(
        shards,
        mesh=mesh,
        in_specs=placed,
        out_specs=(P(), P("dp", None, "lon", None), P("dp", None, None, None), P(), P(), P()),
        check_vma=False,
    )
```

```python
import functools

import jax
import jax.numpy as jnp
from jax import lax
from jax.experimental import pallas as pl
from jax.experimental.pallas import tpu as pltpu
from jax.sharding import PartitionSpec as P

F32 = jnp.float32
BF16 = jnp.bfloat16
ROWS, COLS, C = 16, 64, 640
PIX = ROWS * COLS
PADPIX = PIX + 2 * COLS
NLON, NDP = 8, 16
COUNT = ROWS * COLS * NLON * (C // 32)
SCALE = 1.0 / (ROWS * COLS)
ORDERS = ("xyz", "yzx", "zxy")
LANES = ((0, 256), (256, 512), (512, 640))
NT = (((1,), (1,)), ((), ()))


class Sems:
    def __init__(self):
        self.used = 0

    def take(self, n=1):
        first = self.used
        self.used += n
        return first


NUM_SEMS = 200


def kernel(
    ts, bk, clip, lat_in, tgt_in, win_in, gain_r, shift_r, bias_r,
    igrad, wout, sg_out,
    lat, tgt, win, dsilu, sibw, wg_all, x3, x3t, acc, dacc, e3, agb,
    mask, stat, hs, hr, es, er, l1, l2, g1, g2, sem, *red,
):
    lon, dp = lax.axis_index("lon"), lax.axis_index("dp")
    x, yhi = lon // 2, lon % 2
    z, ylo, c = dp // 4, (dp // 2) % 2, dp % 2
    y = yhi * 2 + ylo
    here = {"x": x, "y": y, "z": z}
    alloc = Sems()

    def dev(xx, yy, zz, cc):
        return {"lon": xx * 2 + yy // 2, "dp": (zz * 2 + yy % 2) * 2 + cc}

    def along(axis, step):
        at = dict(here)
        at[axis] = (at[axis] + step) % 4
        return dev(at["x"], at["y"], at["z"], c)

    sibling = dev(x, y, z, 1 - c)

    def rcopy(src, dst, send, recv, to):
        return pltpu.make_async_remote_copy(
            src_ref=src, dst_ref=dst, send_sem=sem.at[send], recv_sem=sem.at[recv],
            device_id=to, device_id_type=pl.DeviceIdType.MESH,
        )

    def got(ref, number):
        rcopy(ref, ref, number, number, sibling).wait_recv()

    def sent(ref, number):
        rcopy(ref, ref, number, number, sibling).wait_send()

    def to_lon(i):
        return {"lon": i, "dp": dp}

    def to_dp(i):
        return {"lon": lon, "dp": i}

    loads = [
        pltpu.make_async_copy(src, dst, sem.at[alloc.take()])
        for src, dst in ((win_in, win), (lat_in, lat), (tgt_in, tgt))
    ]
    for one in loads:
        one.start()

    bar = pltpu.get_barrier_semaphore()

    def greet(to):
        pl.semaphore_signal(bar, inc=1, device_id=to, device_id_type=pl.DeviceIdType.MESH)

    @pl.loop(1, NLON)
    def _(k):
        greet(to_lon((lon + k) % NLON))

    @pl.loop(1, NDP)
    def _(k):
        greet(to_dp((dp + k) % NDP))

    far = (y + 3 + 2 * ylo) % 4
    greet(dev(x, far, z, c))

    class Exchange:
        def __init__(self, rx, me, size, to):
            self.rx, self.me, self.size, self.to = rx, me, size, to
            self.base = alloc.take(2)

        def send(self):
            @pl.loop(1, self.size)
            def _(k):
                slot = self.rx.at[self.me]
                rcopy(slot, slot, self.base, self.base + 1, self.to((self.me + k) % self.size)).start()

        def wait(self):
            others = self.rx.at[0 : self.size - 1]
            sent(others, self.base)
            got(others, self.base + 1)

        def total(self):
            return functools.reduce(lambda a, b: a + b, [self.rx[i] for i in range(self.size)])

    def at_row(r):
        return pl.ds(pl.multiple_of(r * COLS, COLS), COLS)

    def sums(r, tot):
        v = lat[r].astype(F32)
        hs[0, pl.ds(r, 1), :] = v[COLS - 1 : COLS]
        hs[1, pl.ds(r, 1), :] = v[0:1]
        return tot + jnp.sum(v, axis=0, keepdims=True)

    loads[1].wait()
    chan = lax.fori_loop(0, ROWS, sums, jnp.zeros((1, C), F32))
    gi = jnp.floor((lax.broadcasted_iota(jnp.int32, (C, C), 0).astype(F32) + 0.5) * 0.05)
    gj = jnp.floor((lax.broadcasted_iota(jnp.int32, (C, C), 1).astype(F32) + 0.5) * 0.05)
    mask[...] = jnp.where(gi == gj, 1.0, 0.0).astype(BF16)

    def group_sum(v):
        top = v.astype(BF16)
        rest = v - top.astype(F32)
        mid = rest.astype(BF16)
        low = (rest - mid.astype(F32)).astype(BF16)
        zeros = jnp.zeros((8, C), F32)
        terms = jnp.concatenate(
            [top.astype(F32), mid.astype(F32), low.astype(F32), zeros], axis=0
        ).astype(BF16)
        out = jnp.dot(terms, mask[...], preferred_element_type=F32)
        return out[0:8] + out[8:16] + out[16:24]

    sub = lax.broadcasted_iota(jnp.int32, (8, C), 0)
    pl.semaphore_wait(bar, NLON - 1 + NDP - 1 + 1)
    loads[0].wait()

    swaps = alloc.take(6)

    def swap_tap(j):
        return rcopy(win.at[2 * j + 1 - c], sibw.at[j], swaps, swaps + 1 + j, sibling)

    for j in range(4):
        swap_tap(j).start()
    pl.when(c == 1)(lambda: swap_tap(4).start())

    right, left = to_lon((lon + 1) % NLON), to_lon((lon + NLON - 1) % NLON)
    hsem = alloc.take(2)
    rcopy(hs.at[0], hr.at[0], hsem, hsem + 1, right).start()
    rcopy(hs.at[1], hr.at[1], hsem, hsem + 1, left).start()

    local_mean = group_sum(jnp.where(sub == 0, chan, 0.0))[0:1] / (PIX * 20)

    odd = x % 2
    own_d = z * 2 + ylo

    def jyz(slot, core):
        return (odd, 2 + (1 - core) * odd, 4 - core)[slot]

    def jx(slot):
        return (1 - odd, 3 - odd)[slot]

    def assemble(j):
        got(sibw.at[j], swaps + 1 + j)
        a = win[2 * j + c].astype(F32)
        b = sibw[j].astype(F32)
        first = jnp.where(c == 0, a, b)
        second = jnp.where(c == 0, b, a)
        rows = pl.ds(pl.multiple_of(own_d * 80, 16), 80)
        wg_all[2 * j + c, rows, :] = jnp.concatenate([first, second], axis=0).astype(BF16)

    LO, HI = (0, 48), (48, 32)

    def blk(j, zz, parity, part=(0, 80)):
        row = pl.multiple_of((zz * 2 + parity) * 80 + part[0], 16)
        return wg_all.at[2 * j + c, pl.ds(row, part[1]), :]

    zl, zr, zo = (z + 3) % 4, (z + 1) % 4, (z + 2) % 4
    gz = [alloc.take(3) for _ in range(3)]
    gy = [alloc.take(5) for _ in range(3)]
    gx = [alloc.take(8) for _ in range(2)]
    gd = [alloc.take(2) for _ in range(5)]

    def rows_of(n):
        return wg_all.at[0, 0:n]

    def two_ways(axis, j, zz, parity, send, recv, slot):
        plus, minus = (LO, HI) if slot % 2 == 0 else (HI, LO)
        one, two = blk(j, zz, parity, plus), blk(j, zz, parity, minus)
        return (
            rcopy(one, one, send, recv, along(axis, 1)),
            rcopy(two, two, send, recv, along(axis, 3)),
        )

    def y_copies(s, k, zz):
        return two_ways("y", jyz(s, c), zz, ylo, gy[s], gy[s] + 1 + k, s)

    def x_copies(s, k, zz, parity):
        return two_ways("x", jyz(s, c), zz, parity, gx[s], gx[s] + k, s)

    def z1(s):
        block = blk(jyz(s, c), z, ylo)
        return [rcopy(block, block, gz[s], gz[s] + 1, along("z", k)) for k in (1, 3)]

    def z2(s):
        j = jyz(s, c)
        plus, minus = (LO, HI) if s % 2 == 0 else (HI, LO)
        one, two = blk(j, zl, ylo, plus), blk(j, zr, ylo, minus)
        return (
            rcopy(one, one, gz[s], gz[s] + 2, along("z", 1)),
            rcopy(two, two, gz[s], gz[s] + 2, along("z", 3)),
        )

    def start(copies):
        for one in copies:
            one.start()

    AROUND = (z, zl, zr, zo)

    def over_x(s, body):
        if s == 0:
            body()
        elif s == 1:
            pl.when(c == 0)(body)

    BLOCKS = ((z, ylo), (zl, ylo), (zr, ylo), (zo, ylo), *((q, 1 - ylo) for q in AROUND))

    def across(n, j, core, k):
        zz, parity = BLOCKS[k]
        row = pl.multiple_of((zz * 2 + parity) * 80, 16)
        block = wg_all.at[2 * j + core, pl.ds(row, 80), :]
        return rcopy(block, block, gd[n], gd[n] + 1, sibling)

    def give(n, j, ks):
        start([across(n, j, c, k) for k in ks])

    def wave1(s):
        assemble(jyz(s, c))
        start(z1(s))
        start(y_copies(s, 0, z))
        give(s, jyz(s, c), (0,))

    def x_send(s, ks):
        def body():
            for k in ks:
                start(x_copies(s, k, *BLOCKS[k]))

        over_x(s, body)

    def wave2(s):
        got(rows_of(160), gz[s] + 1)
        start(z2(s))
        start(y_copies(s, 1, zl))
        start(y_copies(s, 2, zr))
        x_send(s, (1, 2))
        give(s, jyz(s, c), (1, 2))

    def wave3(s):
        got(rows_of(80), gz[s] + 2)
        start(y_copies(s, 3, zo))
        x_send(s, (3,))
        give(s, jyz(s, c), (3,))

    def wave4(s):
        for k in range(4):
            got(rows_of(80), gy[s] + 1 + k)
            x_send(s, (4 + k,))
            give(s, jyz(s, c), (4 + k,))

    def own_x(s):
        def body():
            assemble(jx(s))
            give(3 + s, jx(s), (0,))

        over_x(s, body)

    def wave_x(s, ks):
        def body():
            for k in ks:
                got(rows_of(80), gx[s] + k)
                give(3 + s, jx(s), (k,))

        over_x(s, body)

    def from_sibling(s):
        got(rows_of(C), gd[s] + 1)

    def from_sibling_x(s):
        def body():
            got(rows_of(C), gd[3 + s] + 1)

        if s == 0:
            body()
        else:
            pl.when(c == 1)(body)

    def sends_done():
        pl.when(c == 0)(lambda: sent(sibw.at[0:4], swaps))
        pl.when(c == 1)(lambda: sent(sibw, swaps))
        for s in range(3):
            sent(rows_of(240), gz[s])
            sent(rows_of(320), gy[s])
            sent(rows_of(C), gd[s])
        for s in range(2):

            def body(s=s):
                sent(rows_of(560), gx[s])
                sent(rows_of(C), gd[3 + s])

            over_x(s, body)

    wave1(0)
    wave1(1)
    dacc[...] = jnp.zeros((PIX + 4 * COLS, C), F32)
    own_x(0)
    own_x(1)

    def squares(r, tot):
        d = lat[r].astype(F32) - local_mean
        return tot + jnp.sum(d * d, axis=0, keepdims=True)

    chan2 = lax.fori_loop(0, ROWS, squares, jnp.zeros((1, C), F32))
    m2loc = group_sum(jnp.where(sub == 0, chan2, 0.0))[0:1]
    stat[lon] = jnp.where(sub == 0, local_mean, jnp.where(sub == 1, m2loc, 0.0))
    ex_stat = Exchange(stat, lon, NLON, to_lon)
    ex_stat.send()

    wave2(0)
    wave1(2)
    ex_stat.wait()
    sent(hs, hsem)
    got(hr, hsem + 1)
    stats = [stat[i] for i in range(NLON)]
    mean = functools.reduce(lambda a, b: a + b, [s[0:1] for s in stats]) / NLON
    spread = functools.reduce(lambda a, b: a + b, [(s[0:1] - mean) * (s[0:1] - mean) for s in stats])
    within = functools.reduce(lambda a, b: a + b, [s[1:2] for s in stats])
    var = (within + (PIX * 20) * spread) / COUNT
    rstd = lax.rsqrt(var + 1e-05)
    gain, shift = gain_r[...].reshape(1, C), shift_r[...].reshape(1, C)

    def pre_of(v):
        normed = (v - mean) * rstd
        return normed, normed * gain + shift

    def silu(v):
        _, pre = pre_of(v)
        return pre * jax.nn.sigmoid(pre)

    hr[0] = silu(hr[0])
    hr[1] = silu(hr[1])
    edge = lax.broadcasted_iota(jnp.int32, (COLS, C), 0)

    def put_sides(dst, to, a, halo, r):
        before = jnp.where(edge == 0, halo[0, pl.ds(r, 1), :], pltpu.roll(a, 1, 0))
        after = jnp.where(edge == COLS - 1, halo[1, pl.ds(r, 1), :], pltpu.roll(a, COLS - 1, 0))
        dst[at_row(to), 0:C] = before.astype(BF16)
        dst[at_row(to), 2 * C : 3 * C] = after.astype(BF16)

    zero_row = jnp.zeros((COLS, 3 * C), BF16)
    for buf, ends in ((x3, (0, PADPIX - COLS)), (e3, (0, COLS, PADPIX, PADPIX + COLS))):
        for low in ends:
            buf[low : low + COLS, :] = zero_row

    def activate(first, end):
        @pl.loop(first, end)
        def _(r):
            _normed, pre = pre_of(lat[r].astype(F32))
            sig = jax.nn.sigmoid(pre)
            a = pre * sig
            dsilu[r] = sig * (1.0 + pre * (1.0 - sig))
            x3[at_row(r + 1), C : 2 * C] = a.astype(BF16)
            put_sides(x3, r + 1, a, hr, r)

    unit = jnp.where(
        lax.broadcasted_iota(jnp.int32, (256, 256), 0) == lax.broadcasted_iota(jnp.int32, (256, 256), 1),
        1.0, 0.0,
    ).astype(BF16)

    def turn(first, end):
        for j in range(first, end):
            low, high = j * 256, min(j * 256 + 256, 3 * C)
            n = high - low
            x3t[low:high, :] = lax.dot_general(
                unit[:n, :n], x3[:, low:high], NT, preferred_element_type=F32
            ).astype(BF16)

    def forward(tap, count, fresh=False):
        @pl.loop(0, 2)
        def _(m):
            fields = []
            for n in range(count):
                kh, kw = (tap + n) // 3, (tap + n) % 3
                rows = pl.ds(pl.multiple_of(kh * COLS + m * 512, COLS), 512)
                fields.append(x3[rows, pl.ds(pl.multiple_of(kw * C, 128), C)])
            w = wg_all[pl.ds(tap, count)].reshape(count * C, C)
            part = jnp.dot(jnp.concatenate(fields, axis=1), w, preferred_element_type=F32)
            out = pl.ds(pl.multiple_of(m * 512, 512), 512)
            acc[out, :] = part if fresh else acc[out, :] + part

    activate(0, 8)
    wave2(1)
    wave3(0)
    activate(8, ROWS)
    wave3(1)
    wave4(0)
    wave_x(0, (1, 2))
    turn(0, 3)
    wave2(2)
    wave_x(0, (3,))
    from_sibling(0)
    forward(2 * odd, 2, True)
    wave4(1)
    wave_x(1, (1, 2, 3))
    wave3(2)
    wave_x(0, (4, 5, 6, 7))
    turn(3, 8)
    from_sibling_x(0)
    forward(2 - 2 * odd, 2)
    wave_x(1, (4, 5, 6, 7))
    wave4(2)
    from_sibling(1)
    from_sibling_x(1)
    forward(4, 3)
    from_sibling(2)
    forward(7, 2)
    sends_done()

    loads[2].wait()
    bias = bias_r[...].reshape(1, C)

    def error(r, carry):
        sq, tot = carry
        v = acc[at_row(r), :] + bias + lat[r].astype(F32) - tgt[r].astype(F32)
        e3[at_row(r + 2), C : 2 * C] = v.astype(BF16)
        es[0, pl.ds(r, 1), :] = v[COLS - 1 : COLS]
        es[1, pl.ds(r, 1), :] = v[0:1]
        return sq + jnp.sum(v * v, axis=0, keepdims=True), tot + jnp.sum(v, axis=0, keepdims=True)

    zero = jnp.zeros((1, C), F32)
    sq, err_sum = lax.fori_loop(0, ROWS, error, (zero, zero))
    l1[lon] = jnp.broadcast_to(jnp.sum(sq, axis=1, keepdims=True), (8, 128))
    ex_l1 = Exchange(l1, lon, NLON, to_lon)
    ex_l1.send()
    esem = alloc.take(2)
    rcopy(es.at[0], er.at[0], esem, esem + 1, right).start()
    rcopy(es.at[1], er.at[1], esem, esem + 1, left).start()

    def back(m):
        rows = PADPIX // 2
        low = m * rows
        w = jnp.concatenate(
            [
                jnp.concatenate([wg_all[3 * kh + kw] for kw in (2, 1, 0)], axis=1)
                for kh in range(3)
            ],
            axis=0,
        )
        part = lax.dot_general(
            e3[COLS + low : COLS + low + rows, :], w, NT, preferred_element_type=F32
        )
        for kh in range(3):
            out = slice(low + kh * COLS, low + kh * COLS + rows)
            dacc[out, :] = dacc[out, :] + part[:, kh * C : (kh + 1) * C]

    NRED = 9
    groups = [red[NRED * g : NRED * g + NRED] for g in range(3)]

    def order(kw, g):
        return ORDERS[(kw + g) % 3]

    def place(kw, g, core, lon_to, d):
        at = {"x": lon_to // 2, "y": (lon_to % 2) * 2 + d % 2, "z": d // 2}
        a1, a2, a3 = order(kw, g)
        return kw, core, at[a1], at[a2], at[a3]

    def weight_part(kw):
        for g in range(3):
            first, end = LANES[g]
            for d in range(8):
                groups[g][0][place(kw, g, 1, 7, d)] = jnp.zeros((16, end - first), BF16)
        err = jnp.concatenate(
            [e3[(2 - kh) * COLS : (2 - kh) * COLS + PADPIX, C : 2 * C] for kh in range(3)], axis=1
        )
        res = jnp.dot(x3t[kw * C : (kw + 1) * C, :], err, preferred_element_type=F32)
        res = res.astype(BF16)
        for d in range(8):
            for t in range(5):
                low = d * 80 + t * 16
                for kh in range(3):
                    s = kh * 5 + t
                    for g in range(3):
                        first, end = LANES[g]
                        groups[g][0][place(kw, g, s % 2, s // 2, d)] = res[
                            low : low + 16, kh * C + first : kh * C + end
                        ]

    def add(out, terms):
        val = functools.reduce(lambda a, b: a + b, [t[...].astype(F32) for t in terms])
        out[...] = val.astype(out.dtype)

    send_sems = [alloc.take(4) for _ in range(3)]

    def reduce_sends_done():
        for g in range(3):
            rxs, r2rx, r3 = groups[g][1], groups[g][7], groups[g][8]
            sent(rxs, send_sems[g])
            sent(rxs.at[:, 0:3], send_sems[g] + 1)
            sent(r2rx, send_sems[g] + 2)
            sent(r3.at[:, 4:7], send_sems[g] + 3)

    class Lanes:
        def __init__(self, kw, g):
            wg, rxs, ra, rb, rc, rd, r2, r2rx, r3 = groups[g]
            self.r3rx = r3.at[kw, 4:7]
            self.kw, self.g, self.axes = kw, g, order(kw, g)
            self.rxs, self.r2, self.r2rx, self.r3 = rxs.at[kw], r2.at[kw], r2rx.at[kw], r3.at[kw]
            self.ra, self.rb, self.rc, self.rd = ra.at[kw], rb.at[kw], rc.at[kw], rd.at[kw]
            self.buf = wg.at[kw, c]
            send, self.recv = send_sems[g], alloc.take(5)
            self.two = wg.at[kw, 0, 0:2]
            self.swap = rcopy(wg.at[kw, 1 - c], self.rxs, send, self.recv, sibling)
            axis = self.axes[0]
            self.me = [here[a] for a in self.axes]
            far_, up, down = ((self.me[0] + k) % 4 for k in (2, 1, 3))
            self.up, self.down = up, down
            self.first = [
                rcopy(src, dst, send + 1, self.recv + n, along(axis, to))
                for src, dst, n, to in (
                    (self.buf.at[far_, 0:2], self.ra, 1, 1),
                    (self.buf.at[far_, 2:4], self.rb, 1, 3),
                    (self.buf.at[up], self.rc, 2, 1),
                    (self.buf.at[down], self.rd, 2, 3),
                )
            ]
            self.second = self.direct(1, self.r2, self.r2rx, send + 2, self.recv + 3)
            self.third = self.direct(2, self.r3, self.r3rx, send + 3, self.recv + 4)

        def direct(self, stage, buf, rx, send, recv):
            return [
                rcopy(
                    buf.at[(self.me[stage] + k) % 4], rx.at[k - 1],
                    send, recv, along(self.axes[stage], k),
                )
                for k in (1, 3, 2)
            ]

        def join(self, mine_by, theirs_by):
            got(self.rxs, self.recv)

            @pl.loop(0, 4)
            def _(i):
                own = self.buf[i].astype(F32) * mine_by
                self.buf[i] = (own + self.rxs[i].astype(F32) * theirs_by).astype(BF16)

            start(self.first[:2])

        def middle(self):
            got(self.rc, self.recv + 1)
            add(self.buf.at[self.up, 0:2], [self.buf.at[self.up, 0:2], self.ra])
            add(self.buf.at[self.down, 2:4], [self.buf.at[self.down, 2:4], self.rb])
            start(self.first[2:])

        def end_first(self):
            got(self.two, self.recv + 2)
            add(self.r2, [self.buf.at[self.me[0]], self.rc, self.rd])
            start(self.second)

        def end_second(self):
            got(self.r2rx, self.recv + 3)
            add(self.r3.at[0:4], [self.r2.at[self.me[1]]] + [self.r2rx.at[k] for k in range(3)])
            start(self.third)

        def end_third(self):
            got(self.r3rx, self.recv + 4)
            val = self.r3[self.me[2]].astype(F32)
            for k in range(3):
                val = val + self.r3[4 + k].astype(F32)
            first, end = LANES[self.g]
            agb[self.kw, c, lon, :, first:end] = val.astype(BF16)

    class Reduce:
        def __init__(self, kw):
            self.kw = kw
            self.lanes = [Lanes(kw, g) for g in range(3)]
            slot = agb.at[kw, c, lon]
            self.sems = alloc.take(5)
            send, recv = self.sems, self.sems + 1
            self.over_y = rcopy(slot, slot, send, recv, dev(x, (y + 2) % 4, z, c))
            pair = agb.at[kw, c, pl.ds(2 * x, 2)]
            self.over_x = [rcopy(pair, pair, send, recv + 1, along("x", k)) for k in (1, 3, 2)]
            self.give = rcopy(agb.at[kw, c], agb.at[kw, c], send + 3, recv + 3, sibling)

        def join(self, mine_by, theirs_by):
            for one in self.lanes:
                one.join(mine_by, theirs_by)

        def step(self, n):
            kw = self.kw
            if n == 0:
                for one in self.lanes:
                    one.swap.start()
            elif n == 2:
                for one in self.lanes:
                    one.middle()
            elif n == 3:
                for one in self.lanes:
                    one.end_first()
            elif n == 4:
                for one in self.lanes:
                    one.end_second()
            elif n == 5:
                for one in self.lanes:
                    one.end_third()
                self.over_y.start()
            elif n == 6:
                got(agb.at[kw, c, 0], self.sems + 1)
                start(self.over_x)
            elif n == 7:
                got(agb.at[kw, c, 0:6], self.sems + 2)
                self.give.start()
            elif n == 8:
                got(agb.at[kw, 1 - c], self.sems + 4)
                sent(agb.at[kw, c, 0:7], self.sems)
                sent(agb.at[kw, c], self.sems + 3)
                for row in range(3):
                    tiles = []
                    for t in range(5):
                        s = row * 5 + t
                        tiles.append(agb[kw, s % 2, s // 2].astype(F32))
                    rows = jnp.concatenate(tiles, axis=0)
                    wout[3 * row + kw] = jnp.where(c == 0, rows[0:40], rows[40:80]) * SCALE

    parts = [Reduce(kw) for kw in range(3)]
    weight_part(0)
    parts[0].step(0)

    ex_l1.wait()
    tweight = 1.0 / (1.0 + jnp.full((8, 128), ts[0], jnp.int32).astype(F32) / 250.0)
    pano = tweight * ex_l1.total() / (ROWS * COLS * NLON * C)
    lane = lax.broadcasted_iota(jnp.int32, (8, 128), 1)
    row8 = lax.broadcasted_iota(jnp.int32, (8, 128), 0)
    member = jnp.where(lane == jnp.full((8, 128), bk[0], jnp.int32), 1.0, 0.0).astype(F32)
    l2[dp] = jnp.where(
        row8 == 0, member * pano, jnp.where(row8 == 1, member, jnp.where(row8 == 2, tweight, 0.0))
    )
    ex_l2 = Exchange(l2, dp, NDP, to_dp)
    ex_l2.send()
    weight_part(1)
    parts[1].step(0)
    ex_l2.wait()
    sums2 = ex_l2.total()
    denom = jnp.maximum(sums2[1:2], 1.0)
    bucket_mean = sums2[0:1] / denom
    lane1 = lane[0:1]
    limit = jnp.zeros((1, 128), jnp.int32)
    for b in range(4):
        limit = jnp.where(lane1 == b, jnp.full((1, 128), clip[b], jnp.int32), limit)
    limit = limit.astype(F32) / 1000.0
    losses = jnp.minimum(bucket_mean, limit)
    passing = jnp.where((bucket_mean < limit) & (lane1 < 4), 1.0, 0.0)

    def coef_of(tile):
        picked = jnp.sum(tile[1:2] * passing / denom, axis=1, keepdims=True)
        return tile[2:3, 0:1] * picked

    coef, sib_coef = coef_of(l2[dp]), coef_of(l2[dp + 1 - 2 * c])

    parts[0].join(coef, sib_coef)
    weight_part(2)
    parts[2].step(0)
    parts[1].join(coef, sib_coef)
    parts[0].step(2)

    sent(es, esem)
    got(er, esem + 1)
    parts[2].join(coef, sib_coef)

    @pl.loop(0, ROWS)
    def _(r):
        put_sides(e3, r + 2, e3[at_row(r + 2), C : 2 * C].astype(F32), er, r)

    parts[1].step(2)
    parts[0].step(3)
    parts[2].step(2)
    back(0)
    parts[2].step(3)
    parts[1].step(3)
    parts[0].step(4)
    back(1)
    parts[2].step(4)
    parts[1].step(4)
    parts[0].step(5)

    def through(r, carry):
        a, b = carry
        normed = (lat[r].astype(F32) - mean) * rstd
        dpre = dacc[at_row(r + 2), :] * coef * dsilu[r]
        dacc[at_row(r + 2), :] = dpre
        return (
            a + jnp.sum(dpre, axis=0, keepdims=True),
            b + jnp.sum(dpre * normed, axis=0, keepdims=True),
        )

    s1, s2 = lax.fori_loop(0, ROWS, through, (zero, zero))
    g1[lon] = jnp.where(
        sub == 0, s1, jnp.where(sub == 1, s2, jnp.where(sub == 2, err_sum * coef, 0.0))
    )
    ex_g1 = Exchange(g1, lon, NLON, to_lon)
    ex_g1.send()
    parts[2].step(5)
    parts[1].step(5)
    parts[0].step(6)
    ex_g1.wait()
    pan = ex_g1.total()
    g2[dp] = pan
    ex_g2 = Exchange(g2, dp, NDP, to_dp)
    ex_g2.send()
    means = group_sum(pan * gain) / COUNT
    m1, m2 = means[0:1], means[1:2]

    def input_gradient(r):
        normed = (lat[r].astype(F32) - mean) * rstd
        dn = dacc[at_row(r + 2), :] * gain
        g = e3[at_row(r + 2), C : 2 * C].astype(F32) * coef
        igrad[r] = (g + rstd * (dn - m1 - normed * m2)).astype(BF16)

    pl.loop(0, 8)(input_gradient)
    parts[2].step(6)
    parts[1].step(6)
    parts[0].step(7)
    pl.loop(8, ROWS)(input_gradient)
    parts[2].step(7)
    parts[1].step(7)
    parts[0].step(8)
    ex_g2.wait()
    totals = ex_g2.total() * SCALE
    wide = jnp.concatenate([losses] + [jnp.zeros_like(losses)] * 4, axis=1)
    sg_out[...] = jnp.where(sub == 3, wide, totals)
    parts[1].step(8)
    parts[2].step(8)
    reduce_sends_done()
    assert alloc.used <= NUM_SEMS, alloc.used


def reduce_shapes(lanes):
    tile = (16, lanes)
    return [
        (3, 2, 4, 4, 4, *tile),
        (3, 4, 4, 4, *tile),
        (3, 2, 4, *tile),
        (3, 2, 4, *tile),
        (3, 4, 4, *tile),
        (3, 4, 4, *tile),
        (3, 4, 4, *tile),
        (3, 3, 4, *tile),
        (3, 7, *tile),
    ]


def shards(
    latents, target, norm_gain, norm_shift, conv_weight, conv_bias, timesteps, buckets, clip_milli
):
    win = jnp.transpose(conv_weight, (1, 2, 0, 3)).reshape(9, 40, C)
    vmem = pl.BlockSpec(memory_space=pltpu.VMEM)
    smem = pl.BlockSpec(memory_space=pltpu.SMEM)
    outs = pl.pallas_call(
        kernel,
        out_shape=(
            pltpu.VMEM((ROWS, COLS, C), BF16),
            pltpu.VMEM((9, 40, C), F32),
            pltpu.VMEM((8, C), F32),
        ),
        in_specs=[smem] * 3 + [pl.BlockSpec(memory_space=pl.ANY)] * 3 + [vmem] * 3,
        out_specs=(vmem,) * 3,
        scratch_shapes=[
            pltpu.VMEM((ROWS, COLS, C), BF16),
            pltpu.VMEM((ROWS, COLS, C), BF16),
            pltpu.VMEM((9, 40, C), BF16),
            pltpu.VMEM((ROWS, COLS, C), F32),
            pltpu.VMEM((5, 40, C), BF16),
            pltpu.VMEM((9, C, C), BF16),
            pltpu.VMEM((PADPIX, 3 * C), BF16),
            pltpu.VMEM((3 * C, PADPIX), BF16),
            pltpu.VMEM((PIX, C), F32),
            pltpu.VMEM((PIX + 4 * COLS, C), F32),
            pltpu.VMEM((PADPIX + 2 * COLS, 3 * C), BF16),
            pltpu.VMEM((3, 2, NLON, 16, C), BF16),
            pltpu.VMEM((C, C), BF16),
            pltpu.VMEM((NLON, 8, C), F32),
            pltpu.VMEM((2, ROWS, C), F32),
            pltpu.VMEM((2, ROWS, C), F32),
            pltpu.VMEM((2, ROWS, C), F32),
            pltpu.VMEM((2, ROWS, C), F32),
            pltpu.VMEM((NLON, 8, 128), F32),
            pltpu.VMEM((NDP, 8, 128), F32),
            pltpu.VMEM((NLON, 8, C), F32),
            pltpu.VMEM((NDP, 8, C), F32),
            pltpu.SemaphoreType.DMA((NUM_SEMS,)),
        ]
        + [pltpu.VMEM(shape, BF16) for first, end in LANES for shape in reduce_shapes(end - first)],
        compiler_params=pltpu.CompilerParams(
            collective_id=0, has_side_effects=True, vmem_limit_bytes=60 * 1024 * 1024
        ),
        cost_estimate=pl.CostEstimate(
            flops=3 * 2 * PIX * 9 * C * C, bytes_accessed=8 * 1024 * 1024, transcendentals=2 * PIX * C
        ),
    )(
        timesteps, buckets, clip_milli, latents[0], target[0], win,
        norm_gain, norm_shift, conv_bias,
    )
    igrad, wout, sg = outs
    weight_grad = jnp.transpose(wout.reshape(3, 3, 40, C), (2, 0, 1, 3))
    return sg[3, :4], igrad[None], weight_grad, sg[1], sg[0], sg[2]


def solution(mesh):
    placed = (
        P("dp", None, "lon", None),
        P("dp", None, "lon", None),
        P(),
        P(),
        P("dp", None, None, None),
        P(),
        P("dp"),
        P("dp"),
        P(),
    )
    return jax.shard_map(
        shards,
        mesh=mesh,
        in_specs=placed,
        out_specs=(P(), P("dp", None, "lon", None), P("dp", None, None, None), P(), P(), P()),
        check_vma=False,
    )
```
